128 devices in a mesh: dp: 32 (over z, y, core), tensor: 4 (over x).
Axes of the slice: x: 4, y: 4, z: 4, core: 2. Of those that a mesh axis runs over, the one named last changes fastest.
Arguments:
- tokens: bfloat16 [16384, 4096], P('dp', 'tensor'), may hold values from -6 to 6
- norm_gain: bfloat16 [4096], replicated, may hold values from 0.099609375 to 1.8984375
- w_query: bfloat16 [4096, 4096], P(None, 'tensor')
- key_weight: bfloat16 [4096, 1024], P(None, 'tensor')
- value_weight: bfloat16 [4096, 1024], P(None, 'tensor'), may hold values from -0.09375 to 0.09375
- w_output: bfloat16 [4096, 4096], P('tensor'), may hold values from -0.09375 to 0.09375
- doc_lengths: int32 [8], replicated, may hold values from 1 to 8192, 16384 in all
Outputs:
- attended: bfloat16 [16384, 4096], P('dp', 'tensor')
The draws below stay inside these ranges and needn't reach their ends.
Inputs may be any that keep to these rules, and one draw needn't show every extreme that they name: `doc_lengths`: they sum to 16384 and the longest is exactly 8192.
All inputs are finite; a program needn't handle non-finite values.
Results may differ from the reference program's by a relative error of at most 0.012.
The reference program's roundings to bfloat16 on the way count: a program that leaves them out, or rounds other values in their place, can miss the bound.
Values may be sent and summed in bfloat16 or wider, within the bound.
No kernel may reach another device: no remote copies, remote signals or barrier semaphores. Data moves between devices by JAX's collectives and lax.ppermute only.
A program may use at most 128 MiB of HBM per device.

```python
import math
import jax
import jax.numpy as jnp
import numpy as np
from jax import lax

MODEL_WIDTH = 4096
QUERY_HEAD_COUNT = 32
KEY_VALUE_HEADS = 8
HEAD_DIMENSION = 128
NDOC = 8
PACKED_TOKENS = 16384
MOSTLEN = 8192


def draw_w_query(key, part):
    key = jax.random.fold_in(key, 11)
    sampled_weights = jax.random.normal(key, (MODEL_WIDTH, QUERY_HEAD_COUNT * HEAD_DIMENSION), jnp.float32) * MODEL_WIDTH ** (-0.5)
    sampled_weights = sampled_weights * 2.5
    return sampled_weights.astype(jnp.bfloat16)


def draw_key_weight(key, part):
    key = jax.random.fold_in(key, 23)
    sampled_weights = jax.random.normal(key, (MODEL_WIDTH, KEY_VALUE_HEADS * HEAD_DIMENSION), jnp.float32) * MODEL_WIDTH ** (-0.5)
    return sampled_weights.astype(jnp.bfloat16)


def steps_of(own_key, extent, shards, least, largest):
    level, own = 1.0, jax.random.fold_in(own_key, 6)
    for dim, shards_of in shards:
        heights = jnp.exp(jax.random.uniform(jax.random.fold_in(own, dim), (shards_of,), jnp.float32, least / len(shards), largest / len(shards)))
        level = level * jnp.repeat(heights, extent[dim] // shards_of).reshape([-1 if axis == dim else 1 for axis in range(len(extent))])
    return level


def length_profile(count, total, reach, slope):
    loads = [(1 << 20) // math.isqrt(rank ** slope) + 1 for rank in range(2, count + 1)]
    surplus, counts = total - reach - (count - 1), [1] * (count - 1)
    while surplus > 0:
        free = [i for i in range(count - 1) if counts[i] < reach]
        mass, budget = sum([loads[i] for i in free]), surplus
        for i in free:
            addition = min(reach - counts[i], max(1, budget * loads[i] // mass), surplus)
            counts[i] = counts[i] + addition
            surplus = surplus - addition
    return np.array([reach] + counts)


def uneven_parts(rng, amount, total, reach, slope):
    if amount == 2:
        one = jax.random.randint(rng, (), max(1, total - reach), min(reach, total - 1) + 1)
        return jnp.stack([one, total - one])
    sizes = jnp.asarray(length_profile(amount, total, reach, slope), jnp.int32)
    pairs = (amount - 1) // 2
    source_of, receiver = sizes[1:1 + 2 * pairs:2], sizes[2:2 + 2 * pairs:2]
    margin = jnp.minimum(source_of - 1, reach - receiver)
    shifted = jax.random.randint(jax.random.fold_in(rng, 1), (pairs,), 0, 1 << 20) % (margin + 1)
    sizes = sizes.at[1:1 + 2 * pairs:2].set(source_of - shifted).at[2:2 + 2 * pairs:2].set(receiver + shifted)
    return sizes[jax.random.permutation(jax.random.fold_in(rng, 2), amount)]


def scatter_about(key, dims, scale, bound, split=(), held_as=jnp.bfloat16):
    drawn = scale * jax.random.normal(key, dims, jnp.float32)
    if split:
        drawn = drawn * steps_of(key, dims, split, -0.22, 0.18)
    return jnp.clip(drawn, -bound, bound).astype(held_as)


def setup_inputs(seed: int = 0) -> dict:
    key_of = jax.random.split(jax.random.key(seed), 8)
    return {
        "tokens": scatter_about(key_of[0], (PACKED_TOKENS, MODEL_WIDTH), 1.0, 6.0, ((0, 32), (1, 4))),
        "norm_gain": jnp.clip(1.0 + 0.18 * jax.random.normal(key_of[1], (MODEL_WIDTH,), jnp.float32), 0.099609375, 1.8984375).astype(jnp.bfloat16),
        "w_query": draw_w_query(jax.random.fold_in(key_of[7], 71), 0),
        "key_weight": draw_key_weight(jax.random.fold_in(key_of[7], 71), 0),
        "value_weight": scatter_about(key_of[4], (MODEL_WIDTH, KEY_VALUE_HEADS * HEAD_DIMENSION), MODEL_WIDTH ** -0.5, 0.09375, ((1, 4),)),
        "w_output": scatter_about(key_of[5], (QUERY_HEAD_COUNT * HEAD_DIMENSION, MODEL_WIDTH), (QUERY_HEAD_COUNT * HEAD_DIMENSION) ** -0.5, 0.09375, ((0, 4),)),
        "doc_lengths": uneven_parts(key_of[6], NDOC, PACKED_TOKENS, MOSTLEN, 2).astype(jnp.int32),
    }


EPSILON = 1e-05
THETA = 500000.0
NEGATIVE = -1e+30

def document_info(positions, doc_lengths):
    doc_ends = jnp.cumsum(doc_lengths).astype(jnp.int32)
    doc_starts = (doc_ends - doc_lengths).astype(jnp.int32)
    doc_index = lax.optimization_barrier(jnp.sum((positions[:, None] >= doc_ends[None, :]).astype(jnp.int32), axis=1))
    doc_first = lax.optimization_barrier(jnp.max(jnp.where(doc_starts[None, :] <= positions[:, None], doc_starts[None, :], 0), axis=1))
    return (doc_index.astype(jnp.int32), doc_first.astype(jnp.int32))

def rope_tables(offsets, head_size):
    half_size = head_size // 2
    exponents = jnp.arange(half_size, dtype=jnp.float32) * (2.0 / head_size)
    frequency = jnp.exp(-exponents * jnp.log(jnp.float32(THETA)))
    angles = offsets.astype(jnp.float32)[:, None] * frequency[None, :]
    return (jnp.cos(angles), jnp.sin(angles))

def rotate_pairs(value_rows, cosine, sine):
    half_size = value_rows.shape[-1] // 2
    first_half = value_rows[..., :half_size]
    second_half = value_rows[..., half_size:]
    cosine = cosine[:, None, :]
    sine = sine[:, None, :]
    return jnp.concatenate([first_half * cosine - second_half * sine, second_half * cosine + first_half * sine], axis=-1)

def reference(tokens, norm_gain, w_query, key_weight, value_weight, w_output, doc_lengths):
    floats = tokens.astype(jnp.float32)
    mean_square = lax.optimization_barrier(jnp.mean(floats * floats, axis=1, keepdims=True))
    normalized_input = (floats * lax.rsqrt(mean_square + EPSILON) * norm_gain.astype(jnp.float32)[None, :]).astype(jnp.bfloat16)
    positions = jnp.arange(PACKED_TOKENS, dtype=jnp.int32)
    doc_index, doc_first = document_info(positions, doc_lengths)
    cosine, sine = rope_tables(positions - doc_first, HEAD_DIMENSION)
    queries = jnp.dot(normalized_input, w_query, preferred_element_type=jnp.float32).reshape(PACKED_TOKENS, QUERY_HEAD_COUNT, HEAD_DIMENSION)
    queries = rotate_pairs(queries, cosine, sine).astype(jnp.bfloat16)
    key_rows = jnp.dot(normalized_input, key_weight, preferred_element_type=jnp.float32).reshape(PACKED_TOKENS, KEY_VALUE_HEADS, HEAD_DIMENSION)
    key_rows = rotate_pairs(key_rows, cosine, sine).astype(jnp.bfloat16)
    value_rows = jnp.dot(normalized_input, value_weight, preferred_element_type=jnp.float32).astype(jnp.bfloat16).reshape(PACKED_TOKENS, KEY_VALUE_HEADS, HEAD_DIMENSION)
    query_heads = jnp.transpose(queries, (1, 0, 2))
    key_heads = jnp.transpose(key_rows, (1, 0, 2))
    value_heads = jnp.transpose(value_rows, (1, 0, 2))
    query_group_size = QUERY_HEAD_COUNT // KEY_VALUE_HEADS
    block_len = min(512, PACKED_TOKENS)
    block_num = PACKED_TOKENS // block_len
    scale = HEAD_DIMENSION ** (-0.5)

    def one_block(index):
        head = index // block_num
        begin = index % block_num * block_len
        query_block = lax.dynamic_slice_in_dim(query_heads[head], begin, block_len, 0)
        key_all = key_heads[head // query_group_size]
        value_all = value_heads[head // query_group_size]
        query_pos = begin + jnp.arange(block_len, dtype=jnp.int32)
        query_doc = lax.dynamic_slice_in_dim(doc_index, begin, block_len, 0)
        allowed = (positions[None, :] <= query_pos[:, None]) & (doc_index[None, :] == query_doc[:, None])
        scores = jnp.dot(query_block, key_all.T, preferred_element_type=jnp.float32) * scale
        scores = jnp.where(allowed, scores, NEGATIVE)
        top = lax.optimization_barrier(jnp.max(scores, axis=1, keepdims=True))
        expo_vals = jnp.where(allowed, jnp.exp(scores - top), 0.0)
        total = lax.optimization_barrier(jnp.sum(expo_vals, axis=1, keepdims=True))
        summed = jnp.dot(expo_vals.astype(jnp.bfloat16), value_all, preferred_element_type=jnp.float32)
        return summed / total
    blocks = lax.map(one_block, jnp.arange(QUERY_HEAD_COUNT * block_num, dtype=jnp.int32))
    mixed = jnp.transpose(blocks.reshape(QUERY_HEAD_COUNT, PACKED_TOKENS, HEAD_DIMENSION), (1, 0, 2)).reshape(PACKED_TOKENS, QUERY_HEAD_COUNT * HEAD_DIMENSION).astype(jnp.bfloat16)
    return jnp.dot(mixed, w_output, preferred_element_type=jnp.float32).astype(jnp.bfloat16)
```

```python
import functools

import jax
import jax.numpy as jnp
from jax import lax
from jax.experimental import pallas as pl
from jax.experimental.pallas import tpu as pltpu
from jax.sharding import PartitionSpec as P

HD = 128
EPSILON = 1e-05
THETA = 500000.0
NEGATIVE = -1e30
DIMS = (4, 4, 2)
BF = jnp.bfloat16
F32 = jnp.float32
MIB = 1 << 20
LOG2E = 1.4426950408889634


def dp_perm(dz, dy, dc):
    nz, ny, nc = DIMS
    pairs = []
    for z in range(nz):
        for y in range(ny):
            for c in range(nc):
                src = (z * ny + y) * nc + c
                dst = (((z + dz) % nz) * ny + (y + dy) % ny) * nc + (c + dc) % nc
                pairs.append((src, dst))
    return pairs


def dp_send(value, dz=0, dy=0, dc=0):
    return lax.ppermute(value, "dp", dp_perm(dz, dy, dc))


def x_send(value, shift):
    return lax.ppermute(value, "tensor", [(i, (i + shift) % 4) for i in range(4)])


def cost(flops, bytes_accessed, transcendentals=0):
    return pl.CostEstimate(
        flops=int(flops), bytes_accessed=int(bytes_accessed), transcendentals=int(transcendentals)
    )


def rope_tables(positions, doc_lengths):
    doc_starts = jnp.cumsum(doc_lengths) - doc_lengths
    doc_first = jnp.max(
        jnp.where(doc_starts[None, :] <= positions[:, None], doc_starts[None, :], 0), axis=1
    )
    half_size = HD // 2
    exponents = jnp.arange(half_size, dtype=F32) * (2.0 / HD)
    frequency = jnp.exp(-exponents * jnp.log(F32(THETA)))
    angles = (positions - doc_first).astype(F32)[:, None] * frequency[None, :]
    cosine, sine = jnp.cos(angles), jnp.sin(angles)
    return (
        jnp.concatenate([cosine, cosine], axis=1),
        jnp.concatenate([-sine, sine], axis=1),
    )


def rotate(value, cosine, sine):
    return value * cosine + pltpu.roll(value, HD // 2, 1) * sine


def kv_kernel(
    idx_ref, t_ref, a_ref, b_ref, c_ref, d_ref, gain_ref, wk_ref, wv_ref, cos_ref, sin_ref,
    xn_ref, mine_ref, send_ref,
):
    rows, width = t_ref.shape
    half = rows // 2
    x = idx_ref[3]
    core = idx_ref[2]
    step = 64

    def cols(shift):
        return pl.ds(pl.multiple_of(lax.rem(x + shift, 4) * width, width), width)

    def norm_rows(far_ref, far_begin, begin):
        part = pl.ds(begin, step)
        pieces = [
            (t_ref[part, :], 0),
            (a_ref[part, :], 3),
            (b_ref[part, :], 1),
            (far_ref[pl.ds(far_begin, step), :], 2),
        ]
        floats = [(p.astype(F32), s) for p, s in pieces]
        square = sum(jnp.sum(f * f, axis=1, keepdims=True) for f, _ in floats)
        inv = lax.rsqrt(square * (1.0 / (4 * width)) + EPSILON)
        for f, s in floats:
            gain = gain_ref[:, cols(s)].astype(F32)
            xn_ref[part, cols(s)] = (f * inv * gain).astype(BF)

    def top(i, carry):
        norm_rows(c_ref, pl.multiple_of(i * step, step), pl.multiple_of(i * step, step))
        return carry

    def bottom(i, carry):
        norm_rows(d_ref, pl.multiple_of(i * step, step), pl.multiple_of(half + i * step, step))
        return carry

    lax.fori_loop(0, half // step, top, 0)
    lax.fori_loop(0, half // step, bottom, 0)

    keys = jnp.dot(xn_ref[...], wk_ref[...], preferred_element_type=F32)
    cosine, sine = cos_ref[...], sin_ref[...]
    key0 = rotate(keys[:, :HD], cosine, sine).astype(BF)
    key1 = rotate(keys[:, HD:], cosine, sine).astype(BF)

    def put(first, second, columns):
        @pl.when(core == 0)
        def _():
            mine_ref[:, columns] = first
            send_ref[:, columns] = second

        @pl.when(core != 0)
        def _():
            mine_ref[:, columns] = second
            send_ref[:, columns] = first

    put(key0, key1, slice(0, HD))
    vals = jnp.dot(xn_ref[...], wv_ref[...], preferred_element_type=F32).astype(BF)
    put(vals[:, :HD], vals[:, HD:], slice(HD, 2 * HD))


def kv_project(idx, t, a, b, c, d, gain, wk, wv, cosine, sine):
    rows = t.shape[0]
    width = wk.shape[0]
    vm = pl.BlockSpec(memory_space=pltpu.VMEM)
    return pl.pallas_call(
        kv_kernel,
        out_shape=(
            jax.ShapeDtypeStruct((rows, width), BF),
            jax.ShapeDtypeStruct((rows, 2 * HD), BF),
            jax.ShapeDtypeStruct((rows, 2 * HD), BF),
        ),
        in_specs=[pl.BlockSpec(memory_space=pltpu.SMEM)] + [vm] * 10,
        out_specs=(vm, vm, vm),
        compiler_params=pltpu.CompilerParams(vmem_limit_bytes=40 * MIB),
        cost_estimate=cost(2 * rows * width * 4 * HD, 12 * MIB),
        name="norm_keys_values",
    )(idx, t, a, b, c, d, gain, wk, wv, cosine, sine)


def q_kernel(idx_ref, xn_ref, wq_ref, cos_ref, sin_ref, *refs):
    send_refs, mine_refs, scr = refs[0:4], refs[4:8], refs[8]
    j = pl.program_id(0)
    z = idx_ref[0]
    part = mine_refs[0].shape[1]
    res = jnp.dot(xn_ref[...], wq_ref[...], preferred_element_type=F32)
    cosine, sine = cos_ref[...], sin_ref[...]
    for e in range(2):
        scr[e] = rotate(res[:, e * HD : (e + 1) * HD], cosine, sine).astype(BF)

    def put(out_refs):
        for d in range(4):
            begin = pl.multiple_of(lax.rem(z + d, 4) * part, part)
            for e in range(2):
                out_refs[d][lax.rem(j, 2) * 2 + e] = scr[e, pl.ds(begin, part), :]

    @pl.when(j < 2)
    def _():
        put(send_refs)

    @pl.when(j >= 2)
    def _():
        put(mine_refs)


def q_project(idx, xn, wq, cosine, sine):
    rows, width = xn.shape
    part = rows // 4

    def w_map(j, idx_ref):
        core = idx_ref[2]
        group = jnp.where(j < 2, 1 - core, core)
        return (0, group * 2 + lax.rem(j, 2))

    full = lambda shape: pl.BlockSpec(shape, lambda j, idx_ref: (0,) * len(shape))
    outs = pl.pallas_call(
        q_kernel,
        out_shape=tuple(jax.ShapeDtypeStruct((4, part, HD), BF) for _ in range(8)),
        grid_spec=pltpu.PrefetchScalarGridSpec(
            num_scalar_prefetch=1,
            grid=(4,),
            in_specs=[
                full((rows, width)),
                pl.BlockSpec((width, 2 * HD), w_map),
                full((rows, HD)),
                full((rows, HD)),
            ],
            out_specs=tuple(full((4, part, HD)) for _ in range(8)),
            scratch_shapes=[pltpu.VMEM((2, rows, HD), BF)],
        ),
        compiler_params=pltpu.CompilerParams(
            vmem_limit_bytes=40 * MIB, dimension_semantics=("arbitrary",)
        ),
        cost_estimate=cost(2 * rows * width * 8 * HD, 14 * MIB),
        name="queries",
    )(idx, xn, wq, cosine, sine)
    return outs[:4], outs[4:]


KEYS = 1024
SCALE2 = HD ** (-0.5) * LOG2E


def attention_kernel(pieces, tiles, total_tokens, n_kv, idx_ref, len_ref, *refs):
    kv_refs = refs[:n_kv]
    q_refs = refs[n_kv : n_kv + len(tiles)]
    o_refs = refs[n_kv + len(tiles) : n_kv + 2 * len(tiles)]
    kv, acc, top, sem = refs[n_kv + 2 * len(tiles) :]
    z, y, core = idx_ref[0], idx_ref[1], idx_ref[2]

    def position(dz, dy, dc):
        zz, yy, cc = lax.rem(z + dz, 4), lax.rem(y + dy, 4), lax.rem(core + dc, 2)
        return zz * (total_tokens // 4) + yy * (total_tokens // 16) + cc * (total_tokens // 32)

    copies = []
    for n, (array, row, count, dz, dy, dc, extra) in enumerate(pieces):
        begin = pl.multiple_of(position(dz, dy, dc) + extra, 128)
        copy = pltpu.make_async_copy(
            kv_refs[array].at[pl.ds(row, count), :], kv.at[pl.ds(begin, count), :], sem.at[n]
        )
        copy.start()
        copies.append(copy)
    for copy in copies:
        copy.wait()

    ones = jnp.ones((KEYS, HD), BF)
    for n, (dz, dc, per_z) in enumerate(tiles):
        tokens = q_refs[n].shape[1]
        rows = 4 * tokens
        start = position(dz, 0, dc) + z * per_z
        last = start + tokens - 1
        first_low = jnp.int32(0)
        first_high = jnp.int32(0)
        pos = start + lax.rem(lax.broadcasted_iota(jnp.int32, (rows, 1), 0), tokens)
        first = jnp.zeros((rows, 1), jnp.int32)
        begin = jnp.int32(0)
        for i in range(8):
            first_low = jnp.where(begin <= start, begin, first_low)
            first_high = jnp.where(begin <= last, begin, first_high)
            first = jnp.where(pos >= begin, begin, first)
            begin = begin + len_ref[i]
        lo = first_low // KEYS
        hi = last // KEYS + 1
        full_lo = jnp.clip((first_high + KEYS - 1) // KEYS, lo, hi)
        full_hi = jnp.clip((start + 1) // KEYS, full_lo, hi)
        top[...] = jnp.full_like(top, NEGATIVE)
        acc[...] = jnp.zeros_like(acc)

        def block(masked, k):
            base = pl.multiple_of(k * KEYS, KEYS)
            key = kv[pl.ds(base, KEYS), :HD]
            val = jnp.concatenate([kv[pl.ds(base, KEYS), HD:], ones], axis=1)
            for h in range(4):
                part = slice(h * tokens, (h + 1) * tokens)
                s = lax.dot_general(
                    q_refs[n][h], key, (((1,), (1,)), ((), ())), preferred_element_type=F32
                )
                if masked:
                    kpos = base + lax.broadcasted_iota(jnp.int32, s.shape, 1)
                    allowed = (kpos <= pos[part]) & (kpos >= first[part])
                    s = jnp.where(allowed, s, NEGATIVE)
                old = top[part, :]
                new = jnp.maximum(old, jnp.max(s, axis=1, keepdims=True))
                top[part, :] = new
                alpha = jnp.exp2((old - new) * SCALE2)
                p = jnp.exp2((s - new[:, :1]) * SCALE2)
                if masked:
                    p = jnp.where(allowed, p, 0.0)
                pv = jnp.dot(p.astype(BF), val, preferred_element_type=F32)
                acc[part, :HD] = acc[part, :HD] * alpha + pv[:, :HD]
                acc[part, HD:] = acc[part, HD:] * alpha + pv[:, HD:]

        def run(masked, low, high):
            def step(k, carry):
                block(masked, k)
                return carry

            lax.fori_loop(low, high, step, 0)

        run(True, lo, full_lo)
        run(False, full_lo, full_hi)
        run(True, full_hi, hi)
        for h in range(4):
            part = slice(h * tokens, (h + 1) * tokens)
            o_refs[n][h] = (acc[part, :HD] / acc[part, HD:]).astype(BF)


def attention(idx, doc_lengths, kv_arrays, pieces, queries, tiles, total_tokens):
    tokens = queries[0].shape[1]
    smem = pl.BlockSpec(memory_space=pltpu.SMEM)
    hbm = pl.BlockSpec(memory_space=pl.ANY)
    vm = pl.BlockSpec(memory_space=pltpu.VMEM)
    return pl.pallas_call(
        functools.partial(attention_kernel, pieces, tiles, total_tokens, len(kv_arrays)),
        out_shape=tuple(jax.ShapeDtypeStruct(q.shape, BF) for q in queries),
        in_specs=[smem, smem] + [hbm] * len(kv_arrays) + [vm] * len(queries),
        out_specs=tuple(vm for _ in queries),
        scratch_shapes=[
            pltpu.VMEM((total_tokens, 2 * HD), BF),
            pltpu.VMEM((4 * tokens, 2 * HD), F32),
            pltpu.VMEM((4 * tokens, HD), F32),
            pltpu.SemaphoreType.DMA((len(pieces),)),
        ],
        compiler_params=pltpu.CompilerParams(vmem_limit_bytes=48 * MIB),
        cost_estimate=cost(10e6 * 512, 12 * MIB, 10e6),
        name="attention",
    )(idx, doc_lengths, *kv_arrays, *queries)


def out_kernel(dests, idx_ref, w_ref, *refs):
    o_refs, out_ref, scr = refs[:8], refs[8], refs[9]
    z, core = idx_ref[0], idx_ref[2]
    part = o_refs[0].shape[1]

    @pl.when(pl.program_id(0) == 0)
    def _():
        for g in range(2):
            for d in range(4):
                begin = pl.multiple_of(lax.rem(z + d, 4) * part, part)
                group = lax.rem(core + g, 2) * (4 * HD)
                for h in range(4):
                    scr[pl.ds(begin, part), pl.ds(pl.multiple_of(group + h * HD, HD), HD)] = (
                        o_refs[g * 4 + d][h]
                    )

    out_ref[...] = jnp.dot(scr[...], w_ref[...], preferred_element_type=F32).astype(out_ref.dtype)


def out_project(idx, w, pieces, dests, dtype):
    part = pieces[0].shape[1]
    rows = part * 4
    feat, model = w.shape
    width = model // 4
    block = 512
    per = width // block

    def w_map(j, idx_ref):
        shift = jnp.int32(dests[0])
        for n, s in enumerate(dests):
            shift = jnp.where(j >= n * per, s, shift)
        return (0, lax.rem(idx_ref[3] + shift, 4) * per + lax.rem(j, per))

    return pl.pallas_call(
        functools.partial(out_kernel, dests),
        out_shape=jax.ShapeDtypeStruct((rows, width * len(dests)), dtype),
        grid_spec=pltpu.PrefetchScalarGridSpec(
            num_scalar_prefetch=1,
            grid=(per * len(dests),),
            in_specs=[pl.BlockSpec((feat, block), w_map)]
            + [pl.BlockSpec((4, part, HD), lambda j, idx_ref: (0, 0, 0))] * 8,
            out_specs=pl.BlockSpec((rows, block), lambda j, idx_ref: (0, j)),
            scratch_shapes=[pltpu.VMEM((rows, feat), BF)],
        ),
        compiler_params=pltpu.CompilerParams(
            vmem_limit_bytes=32 * MIB, dimension_semantics=("arbitrary",)
        ),
        cost_estimate=cost(
            2 * rows * feat * width * len(dests), (2 * feat + 4 * rows) * width * len(dests)
        ),
        name="output_projection",
    )(idx, w, *pieces)


def gather_kv(mine, other):
    rows = mine.shape[0]
    half = rows // 2
    arrays, pieces = [], []

    def keep(array, parts):
        n = len(arrays)
        arrays.append(array)
        row = 0
        for count, dz, dy, dc, extra in parts:
            pieces.append((n, row, count, dz % 4, dy % 4, dc, extra))
            row += count

    keep(mine, [(rows, 0, 0, 0, 0)])
    keep(other, [(rows, 0, 0, 1, 0)])
    for part, dc, axis in ((mine, 0, "y"), (other, 1, "z")):
        near = functools.partial(dp_send, **{"dc": 0})
        move = (lambda v, s: dp_send(v, dy=s)) if axis == "y" else (lambda v, s: dp_send(v, dz=s))
        cross = (lambda v, s: dp_send(v, dz=s)) if axis == "y" else (lambda v, s: dp_send(v, dy=s))

        def at(along, across):
            return (across, along) if axis == "y" else (along, across)

        up, down = move(part, 1), move(part, -1)
        own_up, own_down = cross(part, 1), cross(part, -1)
        far_top = move(up[:half], 1)
        far_bottom = move(down[half:], -1)
        line = jnp.concatenate([up, down, far_top, far_bottom], axis=0)

        def line_parts(across):
            return [
                (rows, *at(-1, across), dc, 0),
                (rows, *at(1, across), dc, 0),
                (half, *at(2, across), dc, 0),
                (half, *at(2, across), dc, half),
            ]

        line_up, line_down = cross(line, 1), cross(line, -1)
        keep(line, line_parts(0))
        keep(own_up, [(rows, *at(0, -1), dc, 0)])
        keep(own_down, [(rows, *at(0, 1), dc, 0)])
        keep(line_up, line_parts(-1))
        keep(line_down, line_parts(1))
        far_own = cross(own_up, 1)
        far_line0 = cross(line_up[:rows], 1)
        far_line1 = cross(line_down[rows:], -1)
        keep(far_own, [(rows, *at(0, 2), dc, 0)])
        keep(far_line0, line_parts(2)[:1])
        keep(far_line1, line_parts(2)[1:])
    return arrays, pieces


def body(tokens, norm_gain, w_query, key_weight, value_weight, w_output, doc_lengths):
    rows = tokens.shape[0]
    half = rows // 2
    part = rows // 4
    dp = lax.axis_index("dp").astype(jnp.int32)
    x = lax.axis_index("tensor").astype(jnp.int32)
    idx = jnp.stack([dp // 8, (dp // 2) % 4, dp % 2, x])
    positions = dp * rows + jnp.arange(rows, dtype=jnp.int32)
    cosine, sine = rope_tables(positions, doc_lengths)

    a, b = x_send(tokens, 1), x_send(tokens, -1)
    c, d = x_send(a[:half], 1), x_send(b[half:], -1)
    xn, kv_mine, kv_send = kv_project(
        idx, tokens, a, b, c, d, norm_gain[None, :], key_weight, value_weight, cosine, sine
    )
    kv_other = dp_send(kv_send, dc=1)
    arrays, pieces = gather_kv(kv_mine, kv_other)

    q_send, q_mine = q_project(idx, xn, w_query, cosine, sine)
    queries, tiles = [], []
    for dd in range(4):
        queries.append(q_mine[0] if dd == 0 else dp_send(q_mine[dd], dz=dd))
        tiles.append(((-dd) % 4, 0, part))
    for dd in range(4):
        queries.append(dp_send(q_send[dd], dz=dd, dc=1))
        tiles.append(((-dd) % 4, 1, part))
    outs = attention(idx, doc_lengths, arrays, pieces, queries, tiles, rows * 32)

    back = []
    for dd in range(4):
        back.append(outs[dd] if dd == 0 else dp_send(outs[dd], dz=-dd))
    for dd in range(4):
        back.append(dp_send(outs[4 + dd], dz=-dd, dc=1))

    far = out_project(idx, w_output, back, (2,), BF)
    far_up, far_down = x_send(far[:half], 1), x_send(far[half:], -1)
    width = tokens.shape[1]
    near = out_project(idx, w_output, back, (1, 3, 0), F32)
    up = jnp.concatenate([near[:half, :width] + far_up, near[half:, :width]], axis=0)
    down = jnp.concatenate(
        [near[:half, width : 2 * width], near[half:, width : 2 * width] + far_down], axis=0
    )
    got_up, got_down = x_send(up.astype(BF), 1), x_send(down.astype(BF), -1)
    return (near[:, 2 * width :] + got_up.astype(F32) + got_down.astype(F32)).astype(BF)


def solution(mesh):
    return jax.shard_map(
        body,
        mesh=mesh,
        in_specs=(
            P("dp", "tensor"),
            P(),
            P(None, "tensor"),
            P(None, "tensor"),
            P(None, "tensor"),
            P("tensor", None),
            P(),
        ),
        out_specs=P("dp", "tensor"),
        check_vma=False,
    )
```

```python
import functools

import jax
import jax.numpy as jnp
from jax import lax
from jax.experimental import pallas as pl
from jax.experimental.pallas import tpu as pltpu
from jax.sharding import PartitionSpec as P

HD = 128
EPSILON = 1e-05
THETA = 500000.0
NEGATIVE = -1e30
DIMS = (4, 4, 2)
BF = jnp.bfloat16
F32 = jnp.float32
MIB = 1 << 20
LOG2E = 1.4426950408889634


def dp_perm(dz, dy, dc):
    nz, ny, nc = DIMS
    pairs = []
    for z in range(nz):
        for y in range(ny):
            for c in range(nc):
                src = (z * ny + y) * nc + c
                dst = (((z + dz) % nz) * ny + (y + dy) % ny) * nc + (c + dc) % nc
                pairs.append((src, dst))
    return pairs


def dp_send(value, dz=0, dy=0, dc=0):
    return lax.ppermute(value, "dp", dp_perm(dz, dy, dc))


def x_send(value, shift):
    return lax.ppermute(value, "tensor", [(i, (i + shift) % 4) for i in range(4)])


def cost(flops, bytes_accessed, transcendentals=0):
    return pl.CostEstimate(
        flops=int(flops), bytes_accessed=int(bytes_accessed), transcendentals=int(transcendentals)
    )


def rope_tables(positions, doc_lengths):
    doc_starts = jnp.cumsum(doc_lengths) - doc_lengths
    doc_first = jnp.max(
        jnp.where(doc_starts[None, :] <= positions[:, None], doc_starts[None, :], 0), axis=1
    )
    half_size = HD // 2
    exponents = jnp.arange(half_size, dtype=F32) * (2.0 / HD)
    frequency = jnp.exp(-exponents * jnp.log(F32(THETA)))
    angles = (positions - doc_first).astype(F32)[:, None] * frequency[None, :]
    cosine, sine = jnp.cos(angles), jnp.sin(angles)
    return (
        jnp.concatenate([cosine, cosine], axis=1),
        jnp.concatenate([-sine, sine], axis=1),
    )


def rotate(value, cosine, sine):
    return value * cosine + pltpu.roll(value, HD // 2, 1) * sine


def kv_kernel(
    idx_ref, t_ref, a_ref, b_ref, c_ref, d_ref, gain_ref, wk_ref, wv_ref, cos_ref, sin_ref,
    xn_ref, mine_ref, send_ref,
):
    rows, width = t_ref.shape
    half = rows // 2
    x = idx_ref[3]
    core = idx_ref[2]
    step = 64

    def cols(shift):
        return pl.ds(pl.multiple_of(lax.rem(x + shift, 4) * width, width), width)

    def norm_rows(far_ref, far_begin, begin):
        part = pl.ds(begin, step)
        pieces = [
            (t_ref[part, :], 0),
            (a_ref[part, :], 3),
            (b_ref[part, :], 1),
            (far_ref[pl.ds(far_begin, step), :], 2),
        ]
        floats = [(p.astype(F32), s) for p, s in pieces]
        square = sum(jnp.sum(f * f, axis=1, keepdims=True) for f, _ in floats)
        inv = lax.rsqrt(square * (1.0 / (4 * width)) + EPSILON)
        for f, s in floats:
            gain = gain_ref[:, cols(s)].astype(F32)
            xn_ref[part, cols(s)] = (f * inv * gain).astype(BF)

    def top(i, carry):
        norm_rows(c_ref, pl.multiple_of(i * step, step), pl.multiple_of(i * step, step))
        return carry

    def bottom(i, carry):
        norm_rows(d_ref, pl.multiple_of(i * step, step), pl.multiple_of(half + i * step, step))
        return carry

    lax.fori_loop(0, half // step, top, 0)
    lax.fori_loop(0, half // step, bottom, 0)

    keys = jnp.dot(xn_ref[...], wk_ref[...], preferred_element_type=F32)
    cosine, sine = cos_ref[...], sin_ref[...]
    key0 = rotate(keys[:, :HD], cosine, sine).astype(BF)
    key1 = rotate(keys[:, HD:], cosine, sine).astype(BF)

    def put(first, second, begin):
        @pl.when(core == 0)
        def _():
            mine_ref[pl.ds(begin, rows), :] = first
            send_ref[pl.ds(begin, rows), :] = second

        @pl.when(core != 0)
        def _():
            mine_ref[pl.ds(begin, rows), :] = second
            send_ref[pl.ds(begin, rows), :] = first

    put(key0, key1, 0)
    vals = jnp.dot(xn_ref[...], wv_ref[...], preferred_element_type=F32).astype(BF)
    put(vals[:, :HD], vals[:, HD:], rows)


def kv_project(idx, t, a, b, c, d, gain, wk, wv, cosine, sine):
    rows = t.shape[0]
    width = wk.shape[0]
    vm = pl.BlockSpec(memory_space=pltpu.VMEM)
    return pl.pallas_call(
        kv_kernel,
        out_shape=(
            jax.ShapeDtypeStruct((rows, width), BF),
            jax.ShapeDtypeStruct((2 * rows, HD), BF),
            jax.ShapeDtypeStruct((2 * rows, HD), BF),
        ),
        in_specs=[pl.BlockSpec(memory_space=pltpu.SMEM)] + [vm] * 10,
        out_specs=(vm, vm, vm),
        compiler_params=pltpu.CompilerParams(vmem_limit_bytes=40 * MIB),
        cost_estimate=cost(2 * rows * width * 4 * HD, 12 * MIB),
        name="norm_keys_values",
    )(idx, t, a, b, c, d, gain, wk, wv, cosine, sine)


def q_kernel(idx_ref, xn_ref, wq_ref, cos_ref, sin_ref, send_ref, mine_ref, scr):
    j = pl.program_id(0)
    z = idx_ref[0]
    part = mine_ref.shape[2]
    res = jnp.dot(xn_ref[...], wq_ref[...], preferred_element_type=F32)
    cosine, sine = cos_ref[...], sin_ref[...]
    for e in range(2):
        scr[e] = rotate(res[:, e * HD : (e + 1) * HD], cosine, sine).astype(BF)

    def put(out_ref):
        for d in range(4):
            begin = pl.multiple_of(lax.rem(z + d, 4) * part, part)
            for e in range(2):
                out_ref[d, lax.rem(j, 2) * 2 + e] = scr[e, pl.ds(begin, part), :]

    @pl.when(j < 2)
    def _():
        put(send_ref)

    @pl.when(j >= 2)
    def _():
        put(mine_ref)


def q_project(idx, xn, wq, cosine, sine):
    rows, width = xn.shape
    part = rows // 4

    def w_map(j, idx_ref):
        core = idx_ref[2]
        group = jnp.where(j < 2, 1 - core, core)
        return (0, group * 2 + lax.rem(j, 2))

    full = lambda shape: pl.BlockSpec(shape, lambda j, idx_ref: (0,) * len(shape))
    return pl.pallas_call(
        q_kernel,
        out_shape=tuple(jax.ShapeDtypeStruct((4, 4, part, HD), BF) for _ in range(2)),
        grid_spec=pltpu.PrefetchScalarGridSpec(
            num_scalar_prefetch=1,
            grid=(4,),
            in_specs=[
                full((rows, width)),
                pl.BlockSpec((width, 2 * HD), w_map),
                full((rows, HD)),
                full((rows, HD)),
            ],
            out_specs=tuple(full((4, 4, part, HD)) for _ in range(2)),
            scratch_shapes=[pltpu.VMEM((2, rows, HD), BF)],
        ),
        compiler_params=pltpu.CompilerParams(
            vmem_limit_bytes=40 * MIB, dimension_semantics=("arbitrary",)
        ),
        cost_estimate=cost(2 * rows * width * 8 * HD, 14 * MIB),
        name="queries",
    )(idx, xn, wq, cosine, sine)


KEYS = 1024
SCALE2 = HD ** (-0.5) * LOG2E


def attention_kernel(plan, total_tokens, part, idx_ref, len_ref, *refs):
    kv_pieces, q_pieces, n_arrays = plan
    arrays = refs[:n_arrays]
    o_ref, key_ref, val_ref, q_ref, acc, top, sem = refs[n_arrays:]
    z, y, core = idx_ref[0], idx_ref[1], idx_ref[2]
    group_rows = 4 * part
    rows = 2 * group_rows

    def position(dz, dy, dc):
        zz, yy, cc = lax.rem(z + dz, 4), lax.rem(y + dy, 4), lax.rem(core + dc, 2)
        return zz * (total_tokens // 4) + yy * (total_tokens // 16) + cc * (total_tokens // 32)

    copies = []

    def fetch(array, row, count, target):
        copy = pltpu.make_async_copy(arrays[array].at[pl.ds(row, count), :], target, sem.at[len(copies)])
        copy.start()
        copies.append(copy)

    for array, row, count, dz, dy, dc, kind in kv_pieces:
        begin = pl.multiple_of(position(dz, dy, dc), 128)
        fetch(array, row, count, (key_ref, val_ref)[kind].at[pl.ds(begin, count), :])
    for array, row, d, g in q_pieces:
        fetch(array, row, group_rows, q_ref.at[pl.ds(d * rows + g * group_rows, group_rows), :])
    for copy in copies:
        copy.wait()

    ones = jnp.ones((KEYS, HD), BF)

    def tile(d, carry):
        plane = lax.rem(z + 4 - d, 4) * (total_tokens // 4) + y * (total_tokens // 16) + z * part
        starts = [plane + lax.rem(core + g, 2) * (total_tokens // 32) for g in range(2)]
        low = jnp.minimum(starts[0], starts[1])
        last = jnp.maximum(starts[0], starts[1]) + part - 1
        pos = [s + lax.broadcasted_iota(jnp.int32, (part, 1), 0) for s in starts]
        first = [jnp.zeros((part, 1), jnp.int32) for _ in starts]
        first_low = jnp.int32(0)
        first_high = jnp.int32(0)
        begin = jnp.int32(0)
        for i in range(8):
            first_low = jnp.where(begin <= low, begin, first_low)
            first_high = jnp.where(begin <= last, begin, first_high)
            first = [jnp.where(p >= begin, begin, f) for p, f in zip(pos, first)]
            begin = begin + len_ref[i]
        lo = first_low // KEYS
        hi = last // KEYS + 1
        full_lo = jnp.clip((first_high + KEYS - 1) // KEYS, lo, hi)
        full_hi = jnp.clip((low + 1) // KEYS, full_lo, hi)
        top[...] = jnp.full_like(top, NEGATIVE)
        acc[...] = jnp.zeros_like(acc)

        def block(masked, k):
            base = pl.multiple_of(k * KEYS, KEYS)
            key = key_ref[pl.ds(base, KEYS), :]
            val = jnp.concatenate([val_ref[pl.ds(base, KEYS), :], ones], axis=1)

            def scores(n):
                begin = pl.multiple_of(d * rows + n * part, part)
                return lax.dot_general(
                    q_ref[pl.ds(begin, part), :], key, (((1,), (1,)), ((), ())),
                    preferred_element_type=F32,
                )

            following = scores(0)
            for n in range(8):
                s = following
                if n < 7:
                    following = scores(n + 1)
                chunk = slice(n * part, (n + 1) * part)
                if masked:
                    kpos = base + lax.broadcasted_iota(jnp.int32, s.shape, 1)
                    allowed = (kpos <= pos[n // 4]) & (kpos >= first[n // 4])
                    s = jnp.where(allowed, s, NEGATIVE)
                old = top[chunk, :]
                new = jnp.maximum(old, jnp.max(s, axis=1, keepdims=True))
                top[chunk, :] = new
                alpha = jnp.exp2((old - new) * SCALE2)
                p = jnp.exp2((s - new[:, :1]) * SCALE2).astype(BF)
                pv = jnp.dot(p, val, preferred_element_type=F32)
                acc[chunk, :HD] = acc[chunk, :HD] * alpha + pv[:, :HD]
                acc[chunk, HD:] = acc[chunk, HD:] * alpha + pv[:, HD:]

        def run(masked, begin, end):
            def step(k, inner):
                block(masked, k)
                return inner

            lax.fori_loop(begin, end, step, 0)

        run(True, lo, full_lo)
        run(False, full_lo, full_hi)
        run(True, full_hi, hi)
        o_ref[d] = (acc[:, :HD] / acc[:, HD:]).astype(BF)
        return carry

    lax.fori_loop(0, 4, tile, 0)


def attention(idx, doc_lengths, arrays, kv_pieces, q_pieces, part, total_tokens):
    rows = 8 * part
    smem = pl.BlockSpec(memory_space=pltpu.SMEM)
    hbm = pl.BlockSpec(memory_space=pl.ANY)
    vm = pl.BlockSpec(memory_space=pltpu.VMEM)
    plan = (kv_pieces, q_pieces, len(arrays))
    return pl.pallas_call(
        functools.partial(attention_kernel, plan, total_tokens, part),
        out_shape=jax.ShapeDtypeStruct((4, rows, HD), BF),
        in_specs=[smem, smem] + [hbm] * len(arrays),
        out_specs=vm,
        scratch_shapes=[
            pltpu.VMEM((total_tokens, HD), BF),
            pltpu.VMEM((total_tokens, HD), BF),
            pltpu.VMEM((4 * rows, HD), BF),
            pltpu.VMEM((rows, 2 * HD), F32),
            pltpu.VMEM((rows, HD), F32),
            pltpu.SemaphoreType.DMA((len(kv_pieces) + len(q_pieces),)),
        ],
        compiler_params=pltpu.CompilerParams(vmem_limit_bytes=48 * MIB),
        cost_estimate=cost(10e6 * 512, 12 * MIB, 10e6),
        name="attention",
    )(idx, doc_lengths, *arrays)


def out_kernel(dests, idx_ref, w_ref, *refs):
    o_refs, other_ref, out_ref, scr = refs[:4], refs[4], refs[5], refs[6]
    z, core = idx_ref[0], idx_ref[2]
    part = o_refs[0].shape[0] // 4

    @pl.when(pl.program_id(0) == 0)
    def _():
        for g in range(2):
            for d in range(4):
                begin = pl.multiple_of(lax.rem(z + d, 4) * part, part)
                group = lax.rem(core + g, 2) * (4 * HD)
                for h in range(4):
                    scr[pl.ds(begin, part), pl.ds(pl.multiple_of(group + h * HD, HD), HD)] = (
                        o_refs[d][h * part : (h + 1) * part, :]
                        if g == 0
                        else other_ref[(4 * d + h) * part : (4 * d + h + 1) * part, :]
                    )

    out_ref[...] = jnp.dot(scr[...], w_ref[...], preferred_element_type=F32).astype(out_ref.dtype)


def out_project(idx, w, pieces, other, dests, dtype):
    part = pieces[0].shape[0] // 8
    rows = part * 4
    feat, model = w.shape
    width = model // 4
    block = 512
    per = width // block

    def w_map(j, idx_ref):
        shift = jnp.int32(dests[0])
        for n, s in enumerate(dests):
            shift = jnp.where(j >= n * per, s, shift)
        return (0, lax.rem(idx_ref[3] + shift, 4) * per + lax.rem(j, per))

    return pl.pallas_call(
        functools.partial(out_kernel, dests),
        out_shape=jax.ShapeDtypeStruct((rows, width * len(dests)), dtype),
        grid_spec=pltpu.PrefetchScalarGridSpec(
            num_scalar_prefetch=1,
            grid=(per * len(dests),),
            in_specs=[pl.BlockSpec((feat, block), w_map)]
            + [pl.BlockSpec((4 * part, HD), lambda j, idx_ref: (0, 0))] * 4
            + [pl.BlockSpec((16 * part, HD), lambda j, idx_ref: (0, 0))],
            out_specs=pl.BlockSpec((rows, block), lambda j, idx_ref: (0, j)),
            scratch_shapes=[pltpu.VMEM((rows, feat), BF)],
        ),
        compiler_params=pltpu.CompilerParams(
            vmem_limit_bytes=32 * MIB, dimension_semantics=("arbitrary",)
        ),
        cost_estimate=cost(
            2 * rows * feat * width * len(dests), (2 * feat + 4 * rows) * width * len(dests)
        ),
        name="output_projection",
    )(idx, w, *pieces, other)


def exchange(mine, other, q_mine, q_other):
    size = mine.shape[0]
    rows = size // 2
    share = q_mine.shape[1]
    arrays, kv_pieces, q_pieces = [], [], []

    def keep(array, row, parts):
        for entry in parts:
            if len(entry) == 4:
                dz, dy, dc, kinds = entry
                for kind in kinds:
                    kv_pieces.append((len(arrays), row, rows, dz % 4, dy % 4, dc, kind))
                    row += rows
            else:
                q_pieces.append((len(arrays), row, *entry))
                row += share
        arrays.append(array)

    def line_parts(dc, vary, fixed):
        at = (lambda n: (fixed, n)) if vary == "y" else (lambda n: (n, fixed))
        return [(*at(n), dc, (0, 1)) for n in (0, -1, 1, 2)]

    def move_y(value, shift):
        return dp_send(value, dy=shift)

    def move_z(value, shift):
        return dp_send(value, dz=shift)

    a_up, a_down = move_y(mine, 1), move_y(mine, -1)
    b_up, b_down = move_z(other, 1), move_z(other, -1)
    a_far = [move_y(a_up[:rows], 1), move_y(a_down[rows:], -1)]
    b_far = [move_z(b_up[:rows], 1), move_z(b_down[rows:], -1)]
    a_line = [mine, a_up, a_down, *a_far]
    b_line = jnp.concatenate([other, b_up, b_down, *b_far], axis=0)

    a_line_up = jnp.concatenate([q_mine[1], q_other[1], q_mine[2], *a_line], axis=0)
    a_line_down = jnp.concatenate([*a_line, q_other[2], q_mine[3], q_other[3]], axis=0)
    from_below, from_above = move_z(a_line_up, 1), move_z(a_line_down, -1)
    from_left, from_right = move_y(b_line, 1), move_y(b_line, -1)
    far_below = move_z(from_below[2 * share : 3 * share + 2 * size], 1)
    far_above = move_z(from_above[2 * size : 4 * size + share], -1)
    far_left = move_y(from_left[: 2 * size], 1)
    far_right = move_y(from_right[2 * size :], -1)

    keep(a_line_down, 0, line_parts(0, "y", 0))
    keep(b_line, 0, line_parts(1, "z", 0))
    keep(q_mine.reshape(4 * share, HD), 0, [(0, 0)])
    keep(q_other.reshape(4 * share, HD), 0, [(0, 1)])
    keep(from_below, 0, [(1, 0), (1, 1)])
    keep(from_below, 3 * share, line_parts(0, "y", -1))
    keep(from_above, 0, line_parts(0, "y", 1))
    keep(from_above, 4 * size + share, [(3, 0), (3, 1)])
    keep(from_left, 0, line_parts(1, "z", -1))
    keep(from_right, 0, line_parts(1, "z", 1))
    keep(far_below, 0, [(2, 0), *line_parts(0, "y", 2)[:2]])
    keep(far_above, 0, [*line_parts(0, "y", 2)[2:], (2, 1)])
    keep(far_left, 0, line_parts(1, "z", 2)[:2])
    keep(far_right, 0, line_parts(1, "z", 2)[2:])
    return arrays, kv_pieces, q_pieces


def body(tokens, norm_gain, w_query, key_weight, value_weight, w_output, doc_lengths):
    rows, width = tokens.shape
    half = rows // 2
    part = rows // 4
    dp = lax.axis_index("dp").astype(jnp.int32)
    x = lax.axis_index("tensor").astype(jnp.int32)
    idx = jnp.stack([dp // 8, (dp // 2) % 4, dp % 2, x])
    positions = dp * rows + jnp.arange(rows, dtype=jnp.int32)
    cosine, sine = rope_tables(positions, doc_lengths)

    a, b = x_send(tokens, 1), x_send(tokens, -1)
    c, d = x_send(a[:half], 1), x_send(b[half:], -1)
    xn, kv_mine, kv_send = kv_project(
        idx, tokens, a, b, c, d, norm_gain[None, :], key_weight, value_weight, cosine, sine
    )
    kv_other = dp_send(kv_send, dc=1)
    q_send, q_mine = q_project(idx, xn, w_query, cosine, sine)
    q_send = q_send.reshape(4, 4 * part, HD)
    q_mine = q_mine.reshape(4, 4 * part, HD)
    q_other = dp_send(q_send, dc=1)
    arrays, kv_pieces, q_pieces = exchange(kv_mine, kv_other, q_mine, q_other)
    outs = attention(idx, doc_lengths, arrays, kv_pieces, q_pieces, part, rows * 32)

    back = [outs[0]] + [dp_send(outs[n], dz=-n) for n in (1, 2, 3)]
    other = dp_send(jnp.concatenate([o[4 * part :] for o in back], axis=0), dc=1)

    far = out_project(idx, w_output, back, other, (2,), BF)
    far_up, far_down = x_send(far[:half], 1), x_send(far[half:], -1)
    near = out_project(idx, w_output, back, other, (1, 3, 0), F32)
    up_ready = x_send(near[half:, :width].astype(BF), 1)
    down_ready = x_send(near[:half, width : 2 * width].astype(BF), -1)
    up_sum = x_send((near[:half, :width] + far_up).astype(BF), 1)
    down_sum = x_send((near[half:, width : 2 * width] + far_down).astype(BF), -1)
    got_up = jnp.concatenate([up_sum, up_ready], axis=0)
    got_down = jnp.concatenate([down_ready, down_sum], axis=0)
    return (near[:, 2 * width :] + got_up.astype(F32) + got_down.astype(F32)).astype(BF)


def solution(mesh):
    return jax.shard_map(
        body,
        mesh=mesh,
        in_specs=(
            P("dp", "tensor"),
            P(),
            P(None, "tensor"),
            P(None, "tensor"),
            P(None, "tensor"),
            P("tensor", None),
            P(),
        ),
        out_specs=P("dp", "tensor"),
        check_vma=False,
    )
```

```python
import functools

import jax
import jax.numpy as jnp
from jax import lax
from jax.experimental import pallas as pl
from jax.experimental.pallas import tpu as pltpu
from jax.sharding import PartitionSpec as P

HD = 128
EPSILON = 1e-05
THETA = 500000.0
NEGATIVE = -1e30
DIMS = (4, 4, 2)
BF = jnp.bfloat16
F32 = jnp.float32
MIB = 1 << 20
LOG2E = 1.4426950408889634


def dp_perm(dz, dy, dc):
    nz, ny, nc = DIMS
    pairs = []
    for z in range(nz):
        for y in range(ny):
            for c in range(nc):
                src = (z * ny + y) * nc + c
                dst = (((z + dz) % nz) * ny + (y + dy) % ny) * nc + (c + dc) % nc
                pairs.append((src, dst))
    return pairs


def dp_send(value, dz=0, dy=0, dc=0):
    return lax.ppermute(value, "dp", dp_perm(dz, dy, dc))


def x_send(value, shift):
    return lax.ppermute(value, "tensor", [(i, (i + shift) % 4) for i in range(4)])


def cost(flops, bytes_accessed, transcendentals=0):
    return pl.CostEstimate(
        flops=int(flops), bytes_accessed=int(bytes_accessed), transcendentals=int(transcendentals)
    )


def rope_tables(positions, doc_lengths):
    doc_starts = jnp.cumsum(doc_lengths) - doc_lengths
    doc_first = jnp.max(
        jnp.where(doc_starts[None, :] <= positions[:, None], doc_starts[None, :], 0), axis=1
    )
    half_size = HD // 2
    exponents = jnp.arange(half_size, dtype=F32) * (2.0 / HD)
    frequency = jnp.exp(-exponents * jnp.log(F32(THETA)))
    angles = (positions - doc_first).astype(F32)[:, None] * frequency[None, :]
    cosine, sine = jnp.cos(angles), jnp.sin(angles)
    return (
        jnp.concatenate([cosine, cosine], axis=1),
        jnp.concatenate([-sine, sine], axis=1),
    )


def rotate(value, cosine, sine):
    return value * cosine + pltpu.roll(value, HD // 2, 1) * sine


def kv_kernel(
    idx_ref, t_ref, a_ref, b_ref, c_ref, d_ref, gain_ref, wk_ref, wv_ref, cos_ref, sin_ref,
    xn_ref, mine_ref, send_ref,
):
    rows, width = t_ref.shape
    half = rows // 2
    x = idx_ref[3]
    core = idx_ref[2]
    step = 32

    def cols(shift):
        return pl.ds(pl.multiple_of(lax.rem(x + shift, 4) * width, width), width)

    def norm_rows(far_ref, far_begin, begin):
        part = pl.ds(begin, step)
        pieces = [
            (t_ref[part, :], 0),
            (a_ref[part, :], 3),
            (b_ref[part, :], 1),
            (far_ref[pl.ds(far_begin, step), :], 2),
        ]
        floats = [(p.astype(F32), s) for p, s in pieces]
        square = sum(jnp.sum(f * f, axis=1, keepdims=True) for f, _ in floats)
        inv = lax.rsqrt(square * (1.0 / (4 * width)) + EPSILON)
        for f, s in floats:
            gain = gain_ref[:, cols(s)].astype(F32)
            xn_ref[part, cols(s)] = (f * inv * gain).astype(BF)

    def top(i, carry):
        norm_rows(c_ref, pl.multiple_of(i * step, step), pl.multiple_of(i * step, step))
        return carry

    def bottom(i, carry):
        norm_rows(d_ref, pl.multiple_of(i * step, step), pl.multiple_of(half + i * step, step))
        return carry

    lax.fori_loop(0, half // step, top, 0)
    lax.fori_loop(0, half // step, bottom, 0)

    keys = jnp.dot(xn_ref[...], wk_ref[...], preferred_element_type=F32)
    cosine, sine = cos_ref[...], sin_ref[...]
    key0 = rotate(keys[:, :HD], cosine, sine).astype(BF)
    key1 = rotate(keys[:, HD:], cosine, sine).astype(BF)

    def put(first, second, begin):
        @pl.when(core == 0)
        def _():
            mine_ref[pl.ds(begin, rows), :] = first
            send_ref[pl.ds(begin, rows), :] = second

        @pl.when(core != 0)
        def _():
            mine_ref[pl.ds(begin, rows), :] = second
            send_ref[pl.ds(begin, rows), :] = first

    put(key0, key1, 0)
    vals = jnp.dot(xn_ref[...], wv_ref[...], preferred_element_type=F32).astype(BF)
    put(vals[:, :HD], vals[:, HD:], rows)


def kv_project(idx, t, a, b, c, d, gain, wk, wv, cosine, sine):
    rows = t.shape[0]
    width = wk.shape[0]
    vm = pl.BlockSpec(memory_space=pltpu.VMEM)
    return pl.pallas_call(
        kv_kernel,
        out_shape=(
            jax.ShapeDtypeStruct((rows, width), BF),
            jax.ShapeDtypeStruct((2 * rows, HD), BF),
            jax.ShapeDtypeStruct((2 * rows, HD), BF),
        ),
        in_specs=[pl.BlockSpec(memory_space=pltpu.SMEM)] + [vm] * 10,
        out_specs=(vm, vm, vm),
        compiler_params=pltpu.CompilerParams(vmem_limit_bytes=40 * MIB),
        cost_estimate=cost(2 * rows * width * 4 * HD, 12 * MIB),
        name="norm_keys_values",
    )(idx, t, a, b, c, d, gain, wk, wv, cosine, sine)


def q_kernel(idx_ref, xn0_ref, xn1_ref, wq_ref, cos_ref, sin_ref, send_ref, mine_ref, scr):
    j = pl.program_id(0)
    z = idx_ref[0]
    rows = xn0_ref.shape[0]
    part = rows // 4
    for c, xn_ref in enumerate((xn0_ref, xn1_ref)):
        res = jnp.dot(xn_ref[...], wq_ref[...], preferred_element_type=F32)
        span = slice(c * rows, (c + 1) * rows)
        cosine, sine = cos_ref[span, :], sin_ref[span, :]
        for e in range(2):
            scr[e, span] = rotate(res[:, e * HD : (e + 1) * HD], cosine, sine).astype(BF)

    def put(out_ref):
        for d in range(4):
            for c in range(2):
                begin = pl.multiple_of(c * rows + lax.rem(z + d, 4) * part, part)
                for e in range(2):
                    target = pl.multiple_of((c * 4 + lax.rem(j, 2) * 2 + e) * part, part)
                    out_ref[d, pl.ds(target, part), :] = scr[e, pl.ds(begin, part), :]

    @pl.when(j < 2)
    def _():
        put(send_ref)

    @pl.when(j >= 2)
    def _():
        put(mine_ref)


def q_project(idx, xn0, xn1, wq, cosine, sine):
    rows, width = xn0.shape

    def w_map(j, idx_ref):
        core = idx_ref[2]
        group = jnp.where(j < 2, 1 - core, core)
        return (0, group * 2 + lax.rem(j, 2))

    full = lambda shape: pl.BlockSpec(shape, lambda j, idx_ref: (0,) * len(shape))
    return pl.pallas_call(
        q_kernel,
        out_shape=tuple(jax.ShapeDtypeStruct((4, 2 * rows, HD), BF) for _ in range(2)),
        grid_spec=pltpu.PrefetchScalarGridSpec(
            num_scalar_prefetch=1,
            grid=(4,),
            in_specs=[
                full((rows, width)),
                full((rows, width)),
                pl.BlockSpec((width, 2 * HD), w_map),
                full((2 * rows, HD)),
                full((2 * rows, HD)),
            ],
            out_specs=tuple(full((4, 2 * rows, HD)) for _ in range(2)),
            scratch_shapes=[pltpu.VMEM((2, 2 * rows, HD), BF)],
        ),
        compiler_params=pltpu.CompilerParams(
            vmem_limit_bytes=40 * MIB, dimension_semantics=("arbitrary",)
        ),
        cost_estimate=cost(4 * rows * width * 8 * HD, 14 * MIB),
        name="queries",
    )(idx, xn0, xn1, wq, cosine, sine)


KEYS = 1024
SCALE2 = HD ** (-0.5) * LOG2E


def attention_kernel(plan, total_tokens, chunk_index, idx_ref, len_ref, *refs):
    kv_pieces, q_pieces, n_arrays = plan
    arrays, refs = refs[:n_arrays], refs[n_arrays:]
    if chunk_index == 0:
        acc_out, top_out, key_ref, val_ref, q_ref, sem = refs
    else:
        acc_in, top_in, o_ref, key_ref, val_ref, q_ref, acc_scr, top_scr, sem = refs
    z, y, core = idx_ref[0], idx_ref[1], idx_ref[2]
    chip = total_tokens // 16
    per_chip = chip // 2
    rows_d = q_ref.shape[0] // 4
    part = rows_d // 16
    span = rows_d // 8
    copies = []

    def fetch(array, row, count, target):
        copy = pltpu.make_async_copy(arrays[array].at[pl.ds(row, count), :], target, sem.at[len(copies)])
        copy.start()
        copies.append(copy)

    for array, row, dz, dy, kind in kv_pieces:
        begin = (lax.rem(z + dz, 4) * 4 + lax.rem(y + dy, 4)) * per_chip
        begin = pl.multiple_of(begin, per_chip)
        fetch(array, row, per_chip, (key_ref, val_ref)[kind].at[pl.ds(begin, per_chip), :])
    for array, row, count, target in q_pieces:
        fetch(array, row, count, q_ref.at[pl.ds(target, count), :])
    for ref in (key_ref, val_ref):
        ref[16 * per_chip :, :] = jnp.zeros_like(ref[16 * per_chip :, :])
    for copy in copies:
        copy.wait()

    ones = jnp.ones((KEYS, HD), BF)
    lane = lax.broadcasted_iota(jnp.int32, (1, KEYS), 1)
    quarter = per_chip // 2
    from_core = lax.rem(core + lax.rem(lane // quarter, 2), 2)
    key_offset = (
        (lane // per_chip) * chip
        + from_core * (chip // 2)
        + chunk_index * quarter
        + lax.rem(lane, quarter)
    )

    def tile(d, carry):
        if chunk_index == 0:
            acc, top = acc_out.at[d], top_out.at[d]
            top[...] = jnp.full_like(top, NEGATIVE)
            acc[...] = jnp.zeros_like(acc)
        else:
            acc, top = acc_scr, top_scr
            top[...] = top_in[d]
            acc[...] = acc_in[d]
        base = (lax.rem(z + 4 - d, 4) * 4 + y) * chip + z * part
        starts = [base + lax.rem(core + g, 2) * (chip // 2) + c * quarter for g in range(2) for c in range(2)]
        low = base
        last = base + chip // 2 + quarter + part - 1
        token = lax.rem(lax.broadcasted_iota(jnp.int32, (span, 1), 0), part)
        pos = [s + token for s in starts]
        first = [jnp.zeros((span, 1), jnp.int32) for _ in starts]
        first_low = jnp.int32(0)
        first_high = jnp.int32(0)
        begin = jnp.int32(0)
        for i in range(8):
            first_low = jnp.where(begin <= low, begin, first_low)
            first_high = jnp.where(begin <= last, begin, first_high)
            first = [jnp.where(p >= begin, begin, f) for p, f in zip(pos, first)]
            begin = begin + len_ref[i]
        lo = first_low // chip
        count = (last // chip + 1 - lo + 1) // 2
        full_lo = jnp.clip(((first_high + chip - 1) // chip - lo + 1) // 2, 0, count)
        full_hi = jnp.clip(((low + 1) // chip - lo) // 2, full_lo, count)

        def block(masked, k):
            first_chip = lo + 2 * k
            at = pl.multiple_of(first_chip * per_chip, per_chip)
            key = key_ref[pl.ds(at, KEYS), :]
            val = jnp.concatenate([val_ref[pl.ds(at, KEYS), :], ones], axis=1)
            kpos = key_offset + first_chip * chip

            def scores(n):
                begin = pl.multiple_of(d * rows_d + n * span, span)
                return lax.dot_general(
                    q_ref[pl.ds(begin, span), :], key, (((1,), (1,)), ((), ())),
                    preferred_element_type=F32,
                )

            following = scores(0)
            for n in range(8):
                s = following
                if n < 7:
                    following = scores(n + 1)
                rows = slice(n * span, (n + 1) * span)
                if masked:
                    allowed = (kpos <= pos[n // 2]) & (kpos >= first[n // 2])
                    s = jnp.where(allowed, s, NEGATIVE)
                old = top[rows, :]
                new = jnp.maximum(old, jnp.max(s, axis=1, keepdims=True))
                top[rows, :] = new
                alpha = jnp.exp2((old - new) * SCALE2)
                p = jnp.exp2((s - new[:, :1]) * SCALE2).astype(BF)
                pv = jnp.dot(p, val, preferred_element_type=F32)
                acc[rows, :HD] = acc[rows, :HD] * alpha + pv[:, :HD]
                acc[rows, HD:] = acc[rows, HD:] * alpha + pv[:, HD:]

        def run(masked, begin, end):
            def step(k, inner):
                block(masked, k)
                return inner

            lax.fori_loop(begin, end, step, 0)

        run(True, 0, full_lo)
        run(False, full_lo, full_hi)
        run(True, full_hi, count)
        if chunk_index == 1:
            o_ref[d] = (acc[:, :HD] / acc[:, HD:]).astype(BF)
        return carry

    lax.fori_loop(0, 4, tile, 0)


def attention(idx, doc_lengths, kv_arrays, kv_pieces, q_arrays, q_pieces, state, chunk_index, total_tokens):
    rows = total_tokens // 16
    smem = pl.BlockSpec(memory_space=pltpu.SMEM)
    hbm = pl.BlockSpec(memory_space=pl.ANY)
    vm = pl.BlockSpec(memory_space=pltpu.VMEM)
    n_kv = len(kv_arrays)
    q_pieces = [(n_kv + entry[0], *entry[1:]) for entry in q_pieces]
    arrays = [*kv_arrays, *q_arrays]
    plan = (kv_pieces, q_pieces, len(arrays))
    keys = total_tokens // 2 + KEYS // 2
    state_shapes = (
        jax.ShapeDtypeStruct((4, rows, 2 * HD), F32),
        jax.ShapeDtypeStruct((4, rows, HD), F32),
    )
    extra = [] if chunk_index == 0 else [pltpu.VMEM((rows, 2 * HD), F32), pltpu.VMEM((rows, HD), F32)]
    out_shape = state_shapes if chunk_index == 0 else jax.ShapeDtypeStruct((4, rows, HD), BF)
    return pl.pallas_call(
        functools.partial(attention_kernel, plan, total_tokens, chunk_index),
        out_shape=out_shape,
        in_specs=[smem, smem] + [hbm] * len(arrays) + [vm] * len(state),
        out_specs=(vm, vm) if chunk_index == 0 else vm,
        scratch_shapes=[
            pltpu.VMEM((keys, HD), BF),
            pltpu.VMEM((keys, HD), BF),
            pltpu.VMEM((4 * rows, HD), BF),
            *extra,
            pltpu.SemaphoreType.DMA((len(kv_pieces) + len(q_pieces),)),
        ],
        compiler_params=pltpu.CompilerParams(vmem_limit_bytes=48 * MIB),
        cost_estimate=cost(5e6 * 512, 10 * MIB, 5e6),
        name="attention",
    )(idx, doc_lengths, *arrays, *state)


def out_kernel(dests, idx_ref, w_ref, *refs):
    o_refs, other_ref, out_ref, scr = refs[:4], refs[4], refs[5], refs[6]
    z, core = idx_ref[0], idx_ref[2]
    part = o_refs[0].shape[0] // 8

    @pl.when(pl.program_id(0) == 0)
    def _():
        for g in range(2):
            group = lax.rem(core + g, 2) * (4 * HD)
            for d in range(4):
                for c in range(2):
                    begin = pl.multiple_of(c * 4 * part + lax.rem(z + d, 4) * part, part)
                    for h in range(4):
                        at = (c * 4 + h) * part
                        scr[pl.ds(begin, part), pl.ds(pl.multiple_of(group + h * HD, HD), HD)] = (
                            o_refs[d][at : at + part, :]
                            if g == 0
                            else other_ref[8 * d * part + at : 8 * d * part + at + part, :]
                        )

    out_ref[...] = jnp.dot(scr[...], w_ref[...], preferred_element_type=F32).astype(out_ref.dtype)


def out_project(idx, w, pieces, other, dests, dtype):
    rows = pieces[0].shape[0] // 2
    feat, model = w.shape
    width = model // 4
    block = 512
    per = width // block

    def w_map(j, idx_ref):
        shift = jnp.int32(dests[0])
        for n, s in enumerate(dests):
            shift = jnp.where(j >= n * per, s, shift)
        return (0, lax.rem(idx_ref[3] + shift, 4) * per + lax.rem(j, per))

    return pl.pallas_call(
        functools.partial(out_kernel, dests),
        out_shape=jax.ShapeDtypeStruct((rows, width * len(dests)), dtype),
        grid_spec=pltpu.PrefetchScalarGridSpec(
            num_scalar_prefetch=1,
            grid=(per * len(dests),),
            in_specs=[pl.BlockSpec((feat, block), w_map)]
            + [pl.BlockSpec((rows, HD), lambda j, idx_ref: (0, 0))] * 4
            + [pl.BlockSpec((4 * rows, HD), lambda j, idx_ref: (0, 0))],
            out_specs=pl.BlockSpec((rows, block), lambda j, idx_ref: (0, j)),
            scratch_shapes=[pltpu.VMEM((rows, feat), BF)],
        ),
        compiler_params=pltpu.CompilerParams(
            vmem_limit_bytes=32 * MIB, dimension_semantics=("arbitrary",)
        ),
        cost_estimate=cost(
            2 * rows * feat * width * len(dests), (2 * feat + 4 * rows) * width * len(dests)
        ),
        name="output_projection",
    )(idx, w, *pieces, other)


def exchange(mine, other, along_y):
    rows = mine.shape[0] // 2
    half = 2 * rows
    arrays, pieces = [], []

    def keep(array, fixed, blocks):
        for n, block in enumerate(blocks):
            dz, dy = (fixed % 4, block % 4) if along_y else (block % 4, fixed % 4)
            for kind in range(2):
                pieces.append((len(arrays), (2 * n + kind) * half, dz, dy, kind))
        arrays.append(array)

    def near(value, shift):
        return dp_send(value, dy=shift) if along_y else dp_send(value, dz=shift)

    def cross(value, shift):
        return dp_send(value, dz=shift) if along_y else dp_send(value, dy=shift)

    own = jnp.concatenate([mine[:rows], other[:rows], mine[rows:], other[rows:]], axis=0)
    up, down = near(own, 1), near(own, -1)
    far_keys, far_values = near(up[:half], 1), near(down[half:], -1)
    line = jnp.concatenate([own, up, down, far_keys, far_values], axis=0)
    line_up, line_down = cross(line, 1), cross(line, -1)
    far_up = cross(line_up[: 4 * half], 1)
    far_down = cross(line_down[4 * half :], -1)
    keep(line, 0, (0, -1, 1, 2))
    keep(line_up, -1, (0, -1, 1, 2))
    keep(line_down, 1, (0, -1, 1, 2))
    keep(far_up, 2, (0, -1))
    keep(far_down, 2, (1, 2))
    return arrays, pieces


def gather_x(tokens):
    half = tokens.shape[0] // 2
    a, b = x_send(tokens, 1), x_send(tokens, -1)
    return a, b, x_send(a[:half], 1), x_send(b[half:], -1)


def body(tokens, norm_gain, w_query, key_weight, value_weight, w_output, doc_lengths):
    rows, width = tokens.shape
    half = rows // 2
    dp = lax.axis_index("dp").astype(jnp.int32)
    x = lax.axis_index("tensor").astype(jnp.int32)
    idx = jnp.stack([dp // 8, (dp // 2) % 4, dp % 2, x])
    positions = dp * rows + jnp.arange(rows, dtype=jnp.int32)
    cosine, sine = rope_tables(positions, doc_lengths)

    def project(part, gathered, span):
        return kv_project(
            idx, part, *gathered, norm_gain[None, :], key_weight, value_weight,
            cosine[span], sine[span],
        )

    part0, part1 = tokens[:half], tokens[half:]
    gathered0 = gather_x(part0)
    part1, gathered0 = lax.optimization_barrier((part1, gathered0))
    gathered1 = gather_x(part1)
    xn0, mine0, send0 = project(part0, gathered0, slice(0, half))
    other0 = dp_send(send0, dc=1)
    kv0, pieces0 = exchange(mine0, other0, True)
    xn1, mine1, send1 = project(part1, gathered1, slice(half, rows))
    other1 = dp_send(send1, dc=1)
    kv1, pieces1 = exchange(mine1, other1, False)

    q_send, q_mine = q_project(idx, xn0, xn1, w_query, cosine, sine)
    q_other = dp_send(q_send, dc=1)
    q_arrays = [q_mine.reshape(4 * rows, HD), q_other.reshape(4 * rows, HD)]
    q_pieces = [(0, 0, rows, 0), (1, 0, rows, rows)]
    for n in (1, 2, 3):
        both = jnp.concatenate([q_mine[n], q_other[n]], axis=0)
        q_pieces.append((len(q_arrays), 0, 2 * rows, 2 * rows * n))
        q_arrays.append(dp_send(both, dz=n))

    total = rows * 32
    state = attention(idx, doc_lengths, kv0, pieces0, q_arrays, q_pieces, (), 0, total)
    outs = attention(idx, doc_lengths, kv1, pieces1, q_arrays, q_pieces, state, 1, total)

    back = [outs[0]] + [dp_send(outs[n], dz=-n) for n in (1, 2, 3)]
    other = dp_send(jnp.concatenate([o[rows:] for o in back], axis=0), dc=1)

    far = out_project(idx, w_output, back, other, (2,), BF)
    far_up, far_down = x_send(far[:half], 1), x_send(far[half:], -1)
    near = out_project(idx, w_output, back, other, (1, 3, 0), F32)
    up_ready = x_send(near[half:, :width].astype(BF), 1)
    down_ready = x_send(near[:half, width : 2 * width].astype(BF), -1)
    up_sum = x_send((near[:half, :width] + far_up).astype(BF), 1)
    down_sum = x_send((near[half:, width : 2 * width] + far_down).astype(BF), -1)
    got_up = jnp.concatenate([up_sum, up_ready], axis=0)
    got_down = jnp.concatenate([down_ready, down_sum], axis=0)
    return (near[:, 2 * width :] + got_up.astype(F32) + got_down.astype(F32)).astype(BF)


def solution(mesh):
    return jax.shard_map(
        body,
        mesh=mesh,
        in_specs=(
            P("dp", "tensor"),
            P(),
            P(None, "tensor"),
            P(None, "tensor"),
            P(None, "tensor"),
            P("tensor", None),
            P(),
        ),
        out_specs=P("dp", "tensor"),
        check_vma=False,
    )
```

```python
import functools

import jax
import jax.numpy as jnp
from jax import lax
from jax.experimental import pallas as pl
from jax.experimental.pallas import tpu as pltpu
from jax.sharding import PartitionSpec as P

HD = 128
EPSILON = 1e-05
THETA = 500000.0
NEGATIVE = -1e30
DIMS = (4, 4, 2)
BF = jnp.bfloat16
F32 = jnp.float32
MIB = 1 << 20
LOG2E = 1.4426950408889634


def dp_perm(dz, dy, dc):
    nz, ny, nc = DIMS
    pairs = []
    for z in range(nz):
        for y in range(ny):
            for c in range(nc):
                src = (z * ny + y) * nc + c
                dst = (((z + dz) % nz) * ny + (y + dy) % ny) * nc + (c + dc) % nc
                pairs.append((src, dst))
    return pairs


def dp_send(value, dz=0, dy=0, dc=0):
    return lax.ppermute(value, "dp", dp_perm(dz, dy, dc))


def x_send(value, shift):
    return lax.ppermute(value, "tensor", [(i, (i + shift) % 4) for i in range(4)])


def cost(flops, bytes_accessed, transcendentals=0):
    return pl.CostEstimate(
        flops=int(flops), bytes_accessed=int(bytes_accessed), transcendentals=int(transcendentals)
    )


def rope_tables(positions, doc_lengths):
    doc_starts = jnp.cumsum(doc_lengths) - doc_lengths
    doc_first = jnp.max(
        jnp.where(doc_starts[None, :] <= positions[:, None], doc_starts[None, :], 0), axis=1
    )
    half_size = HD // 2
    exponents = jnp.arange(half_size, dtype=F32) * (2.0 / HD)
    frequency = jnp.exp(-exponents * jnp.log(F32(THETA)))
    angles = (positions - doc_first).astype(F32)[:, None] * frequency[None, :]
    cosine, sine = jnp.cos(angles), jnp.sin(angles)
    return (
        jnp.concatenate([cosine, cosine], axis=1),
        jnp.concatenate([-sine, sine], axis=1),
    )


def rotate(value, cosine, sine):
    return value * cosine + pltpu.roll(value, HD // 2, 1) * sine


def kv_kernel(
    idx_ref, t_ref, a_ref, b_ref, c_ref, d_ref, gain_ref, wk_ref, wv_ref, cos_ref, sin_ref,
    xn_ref, mine_ref, send_ref,
):
    rows, width = t_ref.shape
    half = rows // 2
    x = idx_ref[3]
    core = idx_ref[2]
    step = 64

    def cols(shift):
        return pl.ds(pl.multiple_of(lax.rem(x + shift, 4) * width, width), width)

    def norm_rows(far_ref, far_begin, begin):
        part = pl.ds(begin, step)
        pieces = [
            (t_ref[part, :], 0),
            (a_ref[part, :], 3),
            (b_ref[part, :], 1),
            (far_ref[pl.ds(far_begin, step), :], 2),
        ]
        floats = [(p.astype(F32), s) for p, s in pieces]
        square = sum(jnp.sum(f * f, axis=1, keepdims=True) for f, _ in floats)
        inv = lax.rsqrt(square * (1.0 / (4 * width)) + EPSILON)
        for f, s in floats:
            gain = gain_ref[:, cols(s)].astype(F32)
            xn_ref[part, cols(s)] = (f * inv * gain).astype(BF)

    def top(i, carry):
        norm_rows(c_ref, pl.multiple_of(i * step, step), pl.multiple_of(i * step, step))
        return carry

    def bottom(i, carry):
        norm_rows(d_ref, pl.multiple_of(i * step, step), pl.multiple_of(half + i * step, step))
        return carry

    lax.fori_loop(0, half // step, top, 0)
    lax.fori_loop(0, half // step, bottom, 0)

    keys = jnp.dot(xn_ref[...], wk_ref[...], preferred_element_type=F32)
    cosine, sine = cos_ref[...], sin_ref[...]
    key0 = rotate(keys[:, :HD], cosine, sine).astype(BF)
    key1 = rotate(keys[:, HD:], cosine, sine).astype(BF)

    def put(first, second, begin):
        @pl.when(core == 0)
        def _():
            mine_ref[pl.ds(begin, rows), :] = first
            send_ref[pl.ds(begin, rows), :] = second

        @pl.when(core != 0)
        def _():
            mine_ref[pl.ds(begin, rows), :] = second
            send_ref[pl.ds(begin, rows), :] = first

    put(key0, key1, 0)
    vals = jnp.dot(xn_ref[...], wv_ref[...], preferred_element_type=F32).astype(BF)
    put(vals[:, :HD], vals[:, HD:], rows)


def kv_project(idx, t, a, b, c, d, gain, wk, wv, cosine, sine):
    rows = t.shape[0]
    width = wk.shape[0]
    vm = pl.BlockSpec(memory_space=pltpu.VMEM)
    return pl.pallas_call(
        kv_kernel,
        out_shape=(
            jax.ShapeDtypeStruct((rows, width), BF),
            jax.ShapeDtypeStruct((2 * rows, HD), BF),
            jax.ShapeDtypeStruct((2 * rows, HD), BF),
        ),
        in_specs=[pl.BlockSpec(memory_space=pltpu.SMEM)] + [vm] * 10,
        out_specs=(vm, vm, vm),
        compiler_params=pltpu.CompilerParams(vmem_limit_bytes=40 * MIB),
        cost_estimate=cost(2 * rows * width * 4 * HD, 12 * MIB),
        name="norm_keys_values",
    )(idx, t, a, b, c, d, gain, wk, wv, cosine, sine)


def q_kernel(idx_ref, xn_ref, wq_ref, cos_ref, sin_ref, send_ref, mine_ref):
    j = pl.program_id(0)
    rows = xn_ref.shape[0]
    res = jnp.dot(xn_ref[...], wq_ref[...], preferred_element_type=F32)
    cosine, sine = cos_ref[...], sin_ref[...]
    heads = [rotate(res[:, e * HD : (e + 1) * HD], cosine, sine).astype(BF) for e in range(2)]

    def put(out_ref):
        for e in range(2):
            begin = pl.multiple_of((lax.rem(j, 2) * 2 + e) * rows, rows)
            out_ref[pl.ds(begin, rows), :] = heads[e]

    @pl.when(j < 2)
    def _():
        put(send_ref)

    @pl.when(j >= 2)
    def _():
        put(mine_ref)


def q_project(idx, xn, wq, cosine, sine):
    rows, width = xn.shape

    def w_map(j, idx_ref):
        core = idx_ref[2]
        group = jnp.where(j < 2, 1 - core, core)
        return (0, group * 2 + lax.rem(j, 2))

    full = lambda shape: pl.BlockSpec(shape, lambda j, idx_ref: (0,) * len(shape))
    return pl.pallas_call(
        q_kernel,
        out_shape=tuple(jax.ShapeDtypeStruct((4 * rows, HD), BF) for _ in range(2)),
        grid_spec=pltpu.PrefetchScalarGridSpec(
            num_scalar_prefetch=1,
            grid=(4,),
            in_specs=[
                full((rows, width)),
                pl.BlockSpec((width, 2 * HD), w_map),
                full((rows, HD)),
                full((rows, HD)),
            ],
            out_specs=tuple(full((4 * rows, HD)) for _ in range(2)),
        ),
        compiler_params=pltpu.CompilerParams(
            vmem_limit_bytes=40 * MIB, dimension_semantics=("arbitrary",)
        ),
        cost_estimate=cost(2 * rows * width * 8 * HD, 14 * MIB),
        name="queries",
    )(idx, xn, wq, cosine, sine)


SCALE2 = HD ** (-0.5) * LOG2E
CHUNK = 256


def attention_kernel(pieces, n_kv, call, last_call, idx_ref, len_ref, *refs):
    kv_refs, refs = refs[:n_kv], refs[n_kv:]
    q_mine, q_other, refs = refs[0], refs[1], refs[2:]
    if call > 0:
        acc_in, top_in, refs = refs[0], refs[1], refs[2:]
    if call == last_call:
        o_ref, acc, top, refs = refs[0], refs[1], refs[2], refs[3:]
    else:
        acc, top, refs = refs[0], refs[1], refs[2:]
    key_ref, val_ref, q_ref, first_ref, todo_ref, sem = refs
    z, y, core = idx_ref[0], idx_ref[1], idx_ref[2]
    group = q_ref.shape[0] // 2
    size = group // 4
    own = [(z * 4 + y) * 2 + lax.rem(core + g, 2) for g in range(2)]
    copies = []

    def fetch(source, target):
        copy = pltpu.make_async_copy(source, target, sem.at[len(copies)])
        copy.start()
        copies.append(copy)

    for array, row, dz, dy, dc, kind in pieces:
        block = (lax.rem(z + dz, 4) * 4 + lax.rem(y + dy, 4)) * 2 + lax.rem(core + dc, 2)
        begin = pl.multiple_of(block * size, size)
        fetch(kv_refs[array].at[pl.ds(row, size), :], (key_ref, val_ref)[kind].at[pl.ds(begin, size), :])
    fetch(q_mine, q_ref.at[pl.ds(0, group), :])
    fetch(q_other, q_ref.at[pl.ds(group, group), :])
    if call > 0:
        top[...] = top_in[...]
        acc[...] = acc_in[...]
    else:
        top[...] = jnp.full_like(top, NEGATIVE)
        acc[...] = jnp.zeros_like(acc)

    low_first = [jnp.int32(0), jnp.int32(0)]
    high_first = [jnp.int32(0), jnp.int32(0)]
    begin = jnp.int32(0)
    first = [jnp.zeros((size, 1), jnp.int32) for _ in range(2)]
    token = lax.broadcasted_iota(jnp.int32, (size, 1), 0)
    for i in range(8):
        for g in range(2):
            low_first[g] = jnp.where(begin <= own[g] * size, begin, low_first[g])
            high_first[g] = jnp.where(begin <= own[g] * size + size - 1, begin, high_first[g])
            first[g] = jnp.where(token + own[g] * size >= begin, begin, first[g])
        begin = begin + len_ref[i]
    for g in range(2):
        first_ref[pl.ds(g * size, size), :] = first[g]
    lo = jnp.minimum(low_first[0], low_first[1]) // size
    lower = jnp.minimum(own[0], own[1])
    all_from = jnp.maximum(high_first[0], high_first[1])
    ones = jnp.ones((size, HD), BF)
    for copy in copies:
        copy.wait()

    def stage(j):
        zz, yy, cc = j // 8, lax.rem(j // 2, 4), lax.rem(j, 2)
        away = jnp.where(cc == core, lax.rem(zz - z + 4, 4), lax.rem(yy - y + 4, 4))
        return jnp.where(away == 0, 0, jnp.where(away == 2, 2, 1))

    def load(blocks):
        spans = [pl.ds(pl.multiple_of(j * size, size), size) for j in blocks]
        keys = [key_ref[span, :] for span in spans]
        vals = [jnp.concatenate([val_ref[span, :], ones], axis=1) for span in spans]
        if len(blocks) == 1:
            return keys[0], vals[0]
        return jnp.concatenate(keys, axis=0), jnp.concatenate(vals, axis=0)

    def scores(row, key):
        return lax.dot_general(
            q_ref[pl.ds(row, CHUNK), :], key, (((1,), (1,)), ((), ())), preferred_element_type=F32
        )

    def absorb(row, s, val):
        rows = pl.ds(row, CHUNK)
        old = top[rows, :]
        new = jnp.maximum(old, jnp.max(s, axis=1, keepdims=True))
        top[rows, :] = new
        alpha = jnp.exp2((old - new) * SCALE2)
        p = jnp.exp2((s - new[:, :1]) * SCALE2).astype(BF)
        pv = jnp.dot(p, val, preferred_element_type=F32)
        acc[rows, :HD] = acc[rows, :HD] * alpha + pv[:, :HD]
        acc[rows, HD:] = acc[rows, HD:] * alpha + pv[:, HD:]

    def whole(blocks):
        key, val = load(blocks)
        following = scores(0, key)
        for n in range(2 * group // CHUNK):
            s = following
            if (n + 1) * CHUNK < 2 * group:
                following = scores((n + 1) * CHUNK, key)
            absorb(n * CHUNK, s, val)

    def masked(g, j, diagonal):
        key, val = load([j])
        base = g * group
        qpos = (own[1] - own[0]) * g + own[0]

        def width(n):
            return (n * CHUNK) % size + CHUNK if diagonal else size

        def row(n):
            return pl.multiple_of(base + n * CHUNK, CHUNK)

        following = scores(row(0), key[: width(0)])
        for n in range(group // CHUNK):
            s = following
            if (n + 1) * CHUNK < group:
                following = scores(row(n + 1), key[: width(n + 1)])
            at = (n * CHUNK) % size
            start = first_ref[pl.ds(pl.multiple_of(g * size + at, CHUNK), CHUNK), :]
            kpos = j * size + lax.broadcasted_iota(jnp.int32, (1, width(n)), 1)
            allowed = kpos >= start
            if diagonal:
                pos = qpos * size + at + lax.broadcasted_iota(jnp.int32, (CHUNK, 1), 0)
                allowed = allowed & (kpos <= pos)
            absorb(row(n), jnp.where(allowed, s, NEGATIVE), val[: width(n)])

    def collect(j, count):
        take = (j < lower) & (j * size >= all_from) & (stage(j) == call)

        @pl.when(take)
        def _():
            todo_ref[count] = j

        return count + take.astype(jnp.int32)

    count = lax.fori_loop(lo, lower, collect, jnp.int32(0))

    def pair(k, carry):
        whole([todo_ref[2 * k], todo_ref[2 * k + 1]])
        return carry

    lax.fori_loop(0, count // 2, pair, 0)

    @pl.when(lax.rem(count, 2) == 1)
    def _():
        whole([todo_ref[count - 1]])

    def rest(j, carry):
        here = (stage(j) == call) & ~((j < lower) & (j * size >= all_from))

        @pl.when(here)
        def _():
            def one(g, inner):
                own_g = (own[1] - own[0]) * g + own[0]
                from_g = (low_first[1] - low_first[0]) * g + low_first[0]
                needed = (j * size + size - 1 >= from_g) & (j < own_g)

                @pl.when(needed)
                def _():
                    masked(g, j, False)

                if call == 0:
                    @pl.when(j == own_g)
                    def _():
                        masked(g, j, True)

                return inner

            lax.fori_loop(0, 2, one, 0)

        return carry

    lax.fori_loop(lo, lower + 2, rest, 0)
    if call == last_call:
        o_ref[...] = (acc[:, :HD] / acc[:, HD:]).astype(BF)


def attention(idx, doc_lengths, kv, queries, state, call, last_call, total_tokens):
    rows = 2 * queries[0].shape[0]
    size = rows // 8
    smem = pl.BlockSpec(memory_space=pltpu.SMEM)
    hbm = pl.BlockSpec(memory_space=pl.ANY)
    vm = pl.BlockSpec(memory_space=pltpu.VMEM)
    arrays, pieces = kv
    last = call == last_call
    wide, narrow = (rows, 2 * HD), (rows, HD)
    return pl.pallas_call(
        functools.partial(attention_kernel, pieces, len(arrays), call, last_call),
        out_shape=jax.ShapeDtypeStruct((rows, HD), BF)
        if last
        else (jax.ShapeDtypeStruct(wide, F32), jax.ShapeDtypeStruct(narrow, F32)),
        in_specs=[smem, smem] + [hbm] * (len(arrays) + 2) + [vm] * len(state),
        out_specs=vm if last else (vm, vm),
        scratch_shapes=[
            *([pltpu.VMEM(wide, F32), pltpu.VMEM(narrow, F32)] if last else []),
            pltpu.VMEM((total_tokens, HD), BF),
            pltpu.VMEM((total_tokens, HD), BF),
            pltpu.VMEM((rows, HD), BF),
            pltpu.VMEM((2 * size, 1), jnp.int32),
            pltpu.SMEM((32,), jnp.int32),
            pltpu.SemaphoreType.DMA((len(pieces) + 2,)),
        ],
        compiler_params=pltpu.CompilerParams(vmem_limit_bytes=48 * MIB),
        cost_estimate=cost(8e6 * 512, 10 * MIB, 8e6),
        name="attention",
    )(idx, doc_lengths, *arrays, *queries, *state)


def out_kernel(dests, idx_ref, w_ref, mine_ref, other_ref, out_ref, scr):
    core = idx_ref[2]
    rows = scr.shape[0]

    @pl.when(pl.program_id(0) == 0)
    def _():
        for g, ref in enumerate((mine_ref, other_ref)):
            group = lax.rem(core + g, 2) * (4 * HD)
            for h in range(4):
                column = pl.ds(pl.multiple_of(group + h * HD, HD), HD)
                scr[:, column] = ref[h * rows : (h + 1) * rows, :]

    out_ref[...] = jnp.dot(scr[...], w_ref[...], preferred_element_type=F32).astype(out_ref.dtype)


def out_project(idx, w, mine, other, dests, dtype):
    rows = mine.shape[0] // 4
    feat, model = w.shape
    width = model // 4
    block = 512
    per = width // block

    def w_map(j, idx_ref):
        shift = jnp.int32(dests[0])
        for n, s in enumerate(dests):
            shift = jnp.where(j >= n * per, s, shift)
        return (0, lax.rem(idx_ref[3] + shift, 4) * per + lax.rem(j, per))

    return pl.pallas_call(
        functools.partial(out_kernel, dests),
        out_shape=jax.ShapeDtypeStruct((rows, width * len(dests)), dtype),
        grid_spec=pltpu.PrefetchScalarGridSpec(
            num_scalar_prefetch=1,
            grid=(per * len(dests),),
            in_specs=[pl.BlockSpec((feat, block), w_map)]
            + [pl.BlockSpec((4 * rows, HD), lambda j, idx_ref: (0, 0))] * 2,
            out_specs=pl.BlockSpec((rows, block), lambda j, idx_ref: (0, j)),
            scratch_shapes=[pltpu.VMEM((rows, feat), BF)],
        ),
        compiler_params=pltpu.CompilerParams(
            vmem_limit_bytes=32 * MIB, dimension_semantics=("arbitrary",)
        ),
        cost_estimate=cost(
            2 * rows * feat * width * len(dests), (2 * feat + 4 * rows) * width * len(dests)
        ),
        name="output_projection",
    )(idx, w, mine, other)


def exchange(mine, other):
    rows = mine.shape[0] // 2
    block = 2 * rows
    stages = [([], []) for _ in range(3)]

    def keep(n, array, places, dc):
        arrays, pieces = stages[n]
        for i, (dz, dy) in enumerate(places):
            for kind in range(2):
                pieces.append((len(arrays), i * block + kind * rows, dz % 4, dy % 4, dc, kind))
        arrays.append(array)

    def move_y(value, shift):
        return dp_send(value, dy=shift)

    def move_z(value, shift):
        return dp_send(value, dz=shift)

    a_up, a_down = move_y(mine, 1), move_y(mine, -1)
    b_up, b_down_values = move_z(other, 1), move_z(other[rows:], -1)
    b_far = [move_z(b_up[:rows], 1), move_z(b_down_values, -1)]
    b_line = jnp.concatenate([other, b_up, *b_far], axis=0)
    from_left, from_right = move_y(b_line, 1), move_y(b_line, -1)
    a_far = [move_y(a_up[:rows], 1), move_y(a_down[rows:], -1)]
    a_line = jnp.concatenate([mine, a_up, a_down, *a_far], axis=0)
    a_line, b_line = lax.optimization_barrier((a_line, b_line))
    from_below, from_above = move_z(a_line, 1), move_z(a_line[block:], -1)
    left_far = move_y(from_left[: block + rows], 1)
    right_far = move_y(from_right[block + rows :], -1)
    far_below, far_above = move_z(from_below[:block], 1), move_z(from_above, -1)

    keep(0, a_line, [(0, 0), (0, -1), (0, 1), (0, 2)], 0)
    keep(0, b_line, [(0, 0), (-1, 0), (-2, 0)], 1)
    keep(1, from_below, [(-1, 0), (-1, -1), (-1, 1), (-1, 2)], 0)
    keep(1, from_left, [(0, -1), (-1, -1), (-2, -1)], 1)
    keep(1, from_right, [(0, 1), (-1, 1), (-2, 1)], 1)
    keep(2, far_below, [(2, 0)], 0)
    keep(2, far_above, [(2, -1), (2, 1), (2, 2)], 0)
    arrays, pieces = stages[2]
    for place, (array, row, kind) in (
        (0, (left_far, 0, 0)),
        (0, (left_far, rows, 1)),
        (-1, (left_far, block, 0)),
        (-1, (right_far, 0, 1)),
        (-2, (right_far, rows, 0)),
        (-2, (right_far, block, 1)),
    ):
        index = len(arrays) + (array is right_far)
        pieces.append((index, row, place % 4, 2, 1, kind))
    arrays.extend([left_far, right_far])
    return stages


def gather_x(tokens):
    half = tokens.shape[0] // 2
    a, b = x_send(tokens, 1), x_send(tokens, -1)
    return a, b, x_send(a[:half], 1), x_send(b[half:], -1)


def body(tokens, norm_gain, w_query, key_weight, value_weight, w_output, doc_lengths):
    rows, width = tokens.shape
    half = rows // 2
    dp = lax.axis_index("dp").astype(jnp.int32)
    x = lax.axis_index("tensor").astype(jnp.int32)
    idx = jnp.stack([dp // 8, (dp // 2) % 4, dp % 2, x])
    positions = dp * rows + jnp.arange(rows, dtype=jnp.int32)
    cosine, sine = rope_tables(positions, doc_lengths)

    xn, mine, send = kv_project(
        idx, tokens, *gather_x(tokens), norm_gain[None, :], key_weight, value_weight, cosine, sine
    )
    other = dp_send(send, dc=1)
    xn, other = lax.optimization_barrier((xn, other))
    q_send, q_mine = q_project(idx, xn, w_query, cosine, sine)
    q_other = dp_send(q_send, dc=1)
    queries = (q_mine, q_other)
    state = ()
    for call, kv in enumerate(exchange(mine, other)):
        state = attention(idx, doc_lengths, kv, queries, state, call, 2, rows * 32)

    mixed = state[: 4 * rows]
    mixed_other = dp_send(state[4 * rows :], dc=1)
    far = out_project(idx, w_output, mixed, mixed_other, (2,), BF)
    far_up, far_down = x_send(far[:half], 1), x_send(far[half:], -1)
    near = out_project(idx, w_output, mixed, mixed_other, (1, 3, 0), F32)
    up_ready = x_send(near[half:, :width].astype(BF), 1)
    down_ready = x_send(near[:half, width : 2 * width].astype(BF), -1)
    up_sum = x_send((near[:half, :width] + far_up).astype(BF), 1)
    down_sum = x_send((near[half:, width : 2 * width] + far_down).astype(BF), -1)
    got_up = jnp.concatenate([up_sum, up_ready], axis=0)
    got_down = jnp.concatenate([down_ready, down_sum], axis=0)
    return (near[:, 2 * width :] + got_up.astype(F32) + got_down.astype(F32)).astype(BF)


def solution(mesh):
    return jax.shard_map(
        body,
        mesh=mesh,
        in_specs=(
            P("dp", "tensor"),
            P(),
            P(None, "tensor"),
            P(None, "tensor"),
            P(None, "tensor"),
            P("tensor", None),
            P(),
        ),
        out_specs=P("dp", "tensor"),
        check_vma=False,
    )
```

```python
import functools

import jax
import jax.numpy as jnp
from jax import lax
from jax.experimental import pallas as pl
from jax.experimental.pallas import tpu as pltpu
from jax.sharding import PartitionSpec as P

HD = 128
EPSILON = 1e-05
THETA = 500000.0
NEGATIVE = -1e30
DIMS = (4, 4, 2)
BF = jnp.bfloat16
F32 = jnp.float32
MIB = 1 << 20
LOG2E = 1.4426950408889634


def dp_perm(dz, dy, dc):
    nz, ny, nc = DIMS
    pairs = []
    for z in range(nz):
        for y in range(ny):
            for c in range(nc):
                src = (z * ny + y) * nc + c
                dst = (((z + dz) % nz) * ny + (y + dy) % ny) * nc + (c + dc) % nc
                pairs.append((src, dst))
    return pairs


def dp_send(value, dz=0, dy=0, dc=0):
    return lax.ppermute(value, "dp", dp_perm(dz, dy, dc))


def x_send(value, shift):
    return lax.ppermute(value, "tensor", [(i, (i + shift) % 4) for i in range(4)])


def cost(flops, bytes_accessed, transcendentals=0):
    return pl.CostEstimate(
        flops=int(flops), bytes_accessed=int(bytes_accessed), transcendentals=int(transcendentals)
    )


def rope_tables(positions, doc_lengths):
    doc_starts = jnp.cumsum(doc_lengths) - doc_lengths
    doc_first = jnp.max(
        jnp.where(doc_starts[None, :] <= positions[:, None], doc_starts[None, :], 0), axis=1
    )
    half_size = HD // 2
    exponents = jnp.arange(half_size, dtype=F32) * (2.0 / HD)
    frequency = jnp.exp(-exponents * jnp.log(F32(THETA)))
    angles = (positions - doc_first).astype(F32)[:, None] * frequency[None, :]
    cosine, sine = jnp.cos(angles), jnp.sin(angles)
    return (
        jnp.concatenate([cosine, cosine], axis=1),
        jnp.concatenate([-sine, sine], axis=1),
    )


def rotate(value, cosine, sine):
    return value * cosine + pltpu.roll(value, HD // 2, 1) * sine


def kv_kernel(
    idx_ref, t_ref, a_ref, b_ref, c_ref, d_ref, gain_ref, wk_ref, wv_ref, cos_ref, sin_ref,
    xn_ref, mine_ref, send_ref,
):
    rows, width = t_ref.shape
    half = rows // 2
    x = idx_ref[3]
    core = idx_ref[2]
    step = 64

    def cols(shift):
        return pl.ds(pl.multiple_of(lax.rem(x + shift, 4) * width, width), width)

    def norm_rows(far_ref, far_begin, begin):
        part = pl.ds(begin, step)
        pieces = [
            (t_ref[part, :], 0),
            (a_ref[part, :], 3),
            (b_ref[part, :], 1),
            (far_ref[pl.ds(far_begin, step), :], 2),
        ]
        floats = [(p.astype(F32), s) for p, s in pieces]
        square = sum(jnp.sum(f * f, axis=1, keepdims=True) for f, _ in floats)
        inv = lax.rsqrt(square * (1.0 / (4 * width)) + EPSILON)
        for f, s in floats:
            gain = gain_ref[:, cols(s)].astype(F32)
            xn_ref[part, cols(s)] = (f * inv * gain).astype(BF)

    def top(i, carry):
        norm_rows(c_ref, pl.multiple_of(i * step, step), pl.multiple_of(i * step, step))
        return carry

    def bottom(i, carry):
        norm_rows(d_ref, pl.multiple_of(i * step, step), pl.multiple_of(half + i * step, step))
        return carry

    lax.fori_loop(0, half // step, top, 0)
    lax.fori_loop(0, half // step, bottom, 0)

    keys = jnp.dot(xn_ref[...], wk_ref[...], preferred_element_type=F32)
    cosine, sine = cos_ref[...], sin_ref[...]
    key0 = rotate(keys[:, :HD], cosine, sine).astype(BF)
    key1 = rotate(keys[:, HD:], cosine, sine).astype(BF)

    def put(first, second, begin):
        @pl.when(core == 0)
        def _():
            mine_ref[pl.ds(begin, rows), :] = first
            send_ref[pl.ds(begin, rows), :] = second

        @pl.when(core != 0)
        def _():
            mine_ref[pl.ds(begin, rows), :] = second
            send_ref[pl.ds(begin, rows), :] = first

    put(key0, key1, 0)
    vals = jnp.dot(xn_ref[...], wv_ref[...], preferred_element_type=F32).astype(BF)
    put(vals[:, :HD], vals[:, HD:], rows)


def kv_project(idx, t, a, b, c, d, gain, wk, wv, cosine, sine):
    rows = t.shape[0]
    width = wk.shape[0]
    vm = pl.BlockSpec(memory_space=pltpu.VMEM)
    return pl.pallas_call(
        kv_kernel,
        out_shape=(
            jax.ShapeDtypeStruct((rows, width), BF),
            jax.ShapeDtypeStruct((2 * rows, HD), BF),
            jax.ShapeDtypeStruct((2 * rows, HD), BF),
        ),
        in_specs=[pl.BlockSpec(memory_space=pltpu.SMEM)] + [vm] * 10,
        out_specs=(vm, vm, vm),
        compiler_params=pltpu.CompilerParams(vmem_limit_bytes=40 * MIB),
        cost_estimate=cost(2 * rows * width * 4 * HD, 12 * MIB),
        name="norm_keys_values",
    )(idx, t, a, b, c, d, gain, wk, wv, cosine, sine)


def q_kernel(idx_ref, xn_ref, wq_ref, cos_ref, sin_ref, send_ref, mine_ref):
    j = pl.program_id(0)
    half = xn_ref.shape[0] // 2
    res = jnp.dot(xn_ref[...], wq_ref[...], preferred_element_type=F32)
    cosine, sine = cos_ref[...], sin_ref[...]
    heads = [rotate(res[:, e * HD : (e + 1) * HD], cosine, sine).astype(BF) for e in range(2)]

    def put(out_ref):
        for e in range(2):
            for t in range(2):
                begin = pl.multiple_of((t * 4 + lax.rem(j, 2) * 2 + e) * half, half)
                out_ref[pl.ds(begin, half), :] = heads[e][t * half : (t + 1) * half]

    @pl.when(j < 2)
    def _():
        put(send_ref)

    @pl.when(j >= 2)
    def _():
        put(mine_ref)


def q_project(idx, xn, wq, cosine, sine):
    rows, width = xn.shape

    def w_map(j, idx_ref):
        core = idx_ref[2]
        group = jnp.where(j < 2, 1 - core, core)
        return (0, group * 2 + lax.rem(j, 2))

    full = lambda shape: pl.BlockSpec(shape, lambda j, idx_ref: (0,) * len(shape))
    return pl.pallas_call(
        q_kernel,
        out_shape=tuple(jax.ShapeDtypeStruct((4 * rows, HD), BF) for _ in range(2)),
        grid_spec=pltpu.PrefetchScalarGridSpec(
            num_scalar_prefetch=1,
            grid=(4,),
            in_specs=[
                full((rows, width)),
                pl.BlockSpec((width, 2 * HD), w_map),
                full((rows, HD)),
                full((rows, HD)),
            ],
            out_specs=tuple(full((4 * rows, HD)) for _ in range(2)),
        ),
        compiler_params=pltpu.CompilerParams(
            vmem_limit_bytes=40 * MIB, dimension_semantics=("arbitrary",)
        ),
        cost_estimate=cost(2 * rows * width * 8 * HD, 14 * MIB),
        name="queries",
    )(idx, xn, wq, cosine, sine)


SCALE2 = HD ** (-0.5) * LOG2E
CHUNK = 256


def attention_kernel(pieces, n_kv, half, idx_ref, len_ref, *refs):
    first_stage = half is None
    kv_refs, refs = refs[:n_kv], refs[n_kv:]
    q_refs, refs = refs[:2], refs[2:]
    if first_stage:
        acc, top, refs = refs[0], refs[1], refs[2:]
    else:
        acc_in, top_in, o_ref, acc, top, refs = *refs[:5], refs[5:]
    key_ref, val_ref, q_ref, first_ref, todo_ref, sem = refs
    z, y, core = idx_ref[0], idx_ref[1], idx_ref[2]
    rows = q_ref.shape[0]
    size = first_ref.shape[0] // 2
    group = 4 * CHUNK
    chunks = [(t, g) for t in ((0, 1) if first_stage else (half,)) for g in range(2) for _ in range(4)]
    own = [(z * 4 + y) * 2 + lax.rem(core + g, 2) for g in range(2)]
    copies = []

    def fetch(source, target):
        copy = pltpu.make_async_copy(source, target, sem.at[len(copies)])
        copy.start()
        copies.append(copy)

    for n, t in enumerate((0, 1) if first_stage else (half,)):
        for g in range(2):
            fetch(
                q_refs[g].at[pl.ds(t * group, group), :],
                q_ref.at[pl.ds((2 * n + g) * group, group), :],
            )
    if not first_stage:
        fetch(acc_in.at[pl.ds(half * rows, rows), :], acc)
        fetch(top_in.at[pl.ds(half * rows, rows), :], top)
    for array, row, dz, dy, dc, kind in pieces:
        block = (lax.rem(z + dz, 4) * 4 + lax.rem(y + dy, 4)) * 2 + lax.rem(core + dc, 2)
        begin = pl.multiple_of(block * size, size)
        fetch(kv_refs[array].at[pl.ds(row, size), :], (key_ref, val_ref)[kind].at[pl.ds(begin, size), :])
    if first_stage:
        top[...] = jnp.full_like(top, NEGATIVE)
        acc[...] = jnp.zeros_like(acc)

    low_first = [jnp.int32(0), jnp.int32(0)]
    high_first = [jnp.int32(0), jnp.int32(0)]
    begin = jnp.int32(0)
    first = [jnp.zeros((size, 1), jnp.int32) for _ in range(2)]
    token = lax.broadcasted_iota(jnp.int32, (size, 1), 0)
    for i in range(8):
        for g in range(2):
            low_first[g] = jnp.where(begin <= own[g] * size, begin, low_first[g])
            high_first[g] = jnp.where(begin <= own[g] * size + size - 1, begin, high_first[g])
            first[g] = jnp.where(token + own[g] * size >= begin, begin, first[g])
        begin = begin + len_ref[i]
    for g in range(2):
        first_ref[pl.ds(g * size, size), :] = first[g]
    lo = jnp.minimum(low_first[0], low_first[1]) // size
    lower = jnp.minimum(own[0], own[1])
    all_from = jnp.maximum(high_first[0], high_first[1])
    ones = jnp.ones((size, HD), BF)

    def local(j):
        return jnp.where(lax.rem(j, 2) == core, j // 8 == z, lax.rem(j // 2, 4) == y)

    def load(blocks):
        spans = [pl.ds(pl.multiple_of(j * size, size), size) for j in blocks]
        keys = [key_ref[span, :] for span in spans]
        vals = [jnp.concatenate([val_ref[span, :], ones], axis=1) for span in spans]
        if len(blocks) == 1:
            return keys[0], vals[0]
        return jnp.concatenate(keys, axis=0), jnp.concatenate(vals, axis=0)

    def positions(blocks):
        lane = lax.broadcasted_iota(jnp.int32, (1, size), 1)
        parts = [j * size + lane for j in blocks]
        return parts[0] if len(parts) == 1 else jnp.concatenate(parts, axis=1)

    def scores(row, key):
        return lax.dot_general(
            q_ref[pl.ds(row, CHUNK), :], key, (((1,), (1,)), ((), ())), preferred_element_type=F32
        )

    def absorb(row, s, val):
        span = pl.ds(row, CHUNK)
        old = top[span, :]
        new = jnp.maximum(old, jnp.max(s, axis=1, keepdims=True))
        top[span, :] = new
        alpha = jnp.exp2((old - new) * SCALE2)
        p = jnp.exp2((s - new[:, :1]) * SCALE2).astype(BF)
        pv = jnp.dot(p, val, preferred_element_type=F32)
        acc[span, :HD] = acc[span, :HD] * alpha + pv[:, :HD]
        acc[span, HD:] = acc[span, HD:] * alpha + pv[:, HD:]

    def whole(blocks, masked):
        key, val = load(blocks)
        kpos = positions(blocks)
        following = scores(0, key)
        for n, (t, g) in enumerate(chunks):
            s = following
            if n + 1 < len(chunks):
                following = scores((n + 1) * CHUNK, key)
            if masked:
                start = first_ref[g * size + t * CHUNK : g * size + (t + 1) * CHUNK, :]
                s = jnp.where(kpos >= start, s, NEGATIVE)
            absorb(n * CHUNK, s, val)

    def within(g, j, diagonal):
        key, val = load([j])
        own_g = (own[1] - own[0]) * g + own[0]
        kpos = positions([j])

        def width(t):
            return (t + 1) * CHUNK if diagonal else size

        def row(t, h):
            return pl.multiple_of(t * 2 * group + g * group + h * CHUNK, CHUNK)

        order = [(t, h) for t in range(2) for h in range(4)]
        following = scores(row(0, 0), key[: width(0)])
        for n, (t, h) in enumerate(order):
            s = following
            if n + 1 < len(order):
                following = scores(row(*order[n + 1]), key[: width(order[n + 1][0])])
            start = first_ref[pl.ds(pl.multiple_of(g * size + t * CHUNK, CHUNK), CHUNK), :]
            here = kpos[:, : width(t)]
            allowed = here >= start
            if diagonal:
                pos = own_g * size + t * CHUNK + lax.broadcasted_iota(jnp.int32, (CHUNK, 1), 0)
                allowed = allowed & (here <= pos)
            absorb(row(t, h), jnp.where(allowed, s, NEGATIVE), val[: width(t)])

    def collect(j, counts):
        full, part = counts
        here = local(j) if first_stage else ~local(j)
        all_full = j * size >= all_from

        @pl.when(here & all_full)
        def _():
            todo_ref[full] = j

        @pl.when(here & ~all_full)
        def _():
            todo_ref[31 - part] = j

        return (
            full + (here & all_full).astype(jnp.int32),
            part + (here & ~all_full).astype(jnp.int32),
        )

    full, part = lax.fori_loop(lo, lower, collect, (jnp.int32(0), jnp.int32(0)))
    odd = lax.rem(full, 2)

    @pl.when(odd == 1)
    def _():
        todo_ref[31 - part] = todo_ref[full - 1]

    part = part + odd
    for copy in copies:
        copy.wait()

    def full_pair(k, carry):
        whole([todo_ref[2 * k], todo_ref[2 * k + 1]], False)
        return carry

    def part_pair(k, carry):
        whole([todo_ref[31 - 2 * k], todo_ref[30 - 2 * k]], True)
        return carry

    lax.fori_loop(0, full // 2, full_pair, 0)
    lax.fori_loop(0, part // 2, part_pair, 0)

    @pl.when(lax.rem(part, 2) == 1)
    def _():
        whole([todo_ref[32 - part]], True)

    if first_stage:

        def one(g, carry):
            own_g = (own[1] - own[0]) * g + own[0]

            @pl.when(own_g > lower)
            def _():
                within(g, lower, False)

            within(g, own_g, True)
            return carry

        lax.fori_loop(0, 2, one, 0)
    else:
        o_ref[...] = (acc[:, :HD] / acc[:, HD:]).astype(BF)


def attention(idx, doc_lengths, kv, queries, state, half, total_tokens):
    rows = queries[0].shape[0] * (2 if half is None else 1)
    size = total_tokens // 32
    smem = pl.BlockSpec(memory_space=pltpu.SMEM)
    hbm = pl.BlockSpec(memory_space=pl.ANY)
    vm = pl.BlockSpec(memory_space=pltpu.VMEM)
    arrays, pieces = kv
    wide, narrow = (rows, 2 * HD), (rows, HD)
    states = (jax.ShapeDtypeStruct(wide, F32), jax.ShapeDtypeStruct(narrow, F32))
    return pl.pallas_call(
        functools.partial(attention_kernel, pieces, len(arrays), half),
        out_shape=states if half is None else jax.ShapeDtypeStruct((rows, HD), BF),
        in_specs=[smem, smem] + [hbm] * (len(arrays) + 2 + len(state)),
        out_specs=(vm, vm) if half is None else vm,
        scratch_shapes=[
            *([] if half is None else [pltpu.VMEM(wide, F32), pltpu.VMEM(narrow, F32)]),
            pltpu.VMEM((total_tokens, HD), BF),
            pltpu.VMEM((total_tokens, HD), BF),
            pltpu.VMEM((rows, HD), BF),
            pltpu.VMEM((2 * size, 1), jnp.int32),
            pltpu.SMEM((32,), jnp.int32),
            pltpu.SemaphoreType.DMA((len(pieces) + 6,)),
        ],
        compiler_params=pltpu.CompilerParams(vmem_limit_bytes=48 * MIB),
        cost_estimate=cost(8e6 * 512, 10 * MIB, 8e6),
        name="attention",
    )(idx, doc_lengths, *arrays, *queries, *state)


def out_kernel(dests, idx_ref, w_ref, mine_ref, other_ref, out_ref, scr):
    core = idx_ref[2]
    rows = scr.shape[0]

    @pl.when(pl.program_id(0) == 0)
    def _():
        for g, ref in enumerate((mine_ref, other_ref)):
            group = lax.rem(core + g, 2) * (4 * HD)
            for h in range(4):
                column = pl.ds(pl.multiple_of(group + h * HD, HD), HD)
                scr[:, column] = ref[h * rows : (h + 1) * rows, :]

    out_ref[...] = jnp.dot(scr[...], w_ref[...], preferred_element_type=F32).astype(out_ref.dtype)


def out_project(idx, w, mine, other, dests, dtype):
    rows = mine.shape[0] // 4
    feat, model = w.shape
    width = model // 4
    block = 512
    per = width // block

    def w_map(j, idx_ref):
        shift = jnp.int32(dests[0])
        for n, s in enumerate(dests):
            shift = jnp.where(j >= n * per, s, shift)
        return (0, lax.rem(idx_ref[3] + shift, 4) * per + lax.rem(j, per))

    return pl.pallas_call(
        functools.partial(out_kernel, dests),
        out_shape=jax.ShapeDtypeStruct((rows, width * len(dests)), dtype),
        grid_spec=pltpu.PrefetchScalarGridSpec(
            num_scalar_prefetch=1,
            grid=(per * len(dests),),
            in_specs=[pl.BlockSpec((feat, block), w_map)]
            + [pl.BlockSpec((4 * rows, HD), lambda j, idx_ref: (0, 0))] * 2,
            out_specs=pl.BlockSpec((rows, block), lambda j, idx_ref: (0, j)),
            scratch_shapes=[pltpu.VMEM((rows, feat), BF)],
        ),
        compiler_params=pltpu.CompilerParams(
            vmem_limit_bytes=32 * MIB, dimension_semantics=("arbitrary",)
        ),
        cost_estimate=cost(
            2 * rows * feat * width * len(dests), (2 * feat + 4 * rows) * width * len(dests)
        ),
        name="output_projection",
    )(idx, w, mine, other)


def exchange_near(mine, other):
    rows = mine.shape[0] // 2
    a_up, a_down = move_y(mine, 1), move_y(mine, -1)
    b_up, b_down_values = move_z(other, 1), move_z(other[rows:], -1)
    b_far = [move_z(b_up[:rows], 1), move_z(b_down_values, -1)]
    a_far = [move_y(a_up[:rows], 1), move_y(a_down[rows:], -1)]
    a_line = jnp.concatenate([mine, a_up, a_down, *a_far], axis=0)
    b_line = jnp.concatenate([other, b_up, *b_far], axis=0)
    return a_line, b_line


def move_y(value, shift):
    return dp_send(value, dy=shift)


def move_z(value, shift):
    return dp_send(value, dz=shift)


def exchange(a_line, b_line, rows, first_call):
    block = 2 * rows
    stages = [([], []) for _ in range(3)]

    def keep(n, array, places, dc):
        arrays, pieces = stages[n]
        for i, (dz, dy) in enumerate(places):
            for kind in range(2):
                pieces.append((len(arrays), i * block + kind * rows, dz % 4, dy % 4, dc, kind))
        arrays.append(array)

    from_left, from_right = move_y(b_line, 1), move_y(b_line, -1)
    from_below, from_above = move_z(a_line, 1), move_z(a_line[block:], -1)
    keep(0, a_line, [(0, 0), (0, -1), (0, 1), (0, 2)], 0)
    keep(0, b_line, [(0, 0), (-1, 0), (-2, 0)], 1)
    state = first_call(stages[0])
    state, from_left, from_right, from_below, from_above = lax.optimization_barrier(
        (state, from_left, from_right, from_below, from_above)
    )
    left_far = move_y(from_left[: block + rows], 1)
    right_far = move_y(from_right[block + rows :], -1)
    far_below, far_above = move_z(from_below[:block], 1), move_z(from_above, -1)

    keep(1, from_below, [(-1, 0), (-1, -1), (-1, 1), (-1, 2)], 0)
    keep(1, from_left, [(0, -1), (-1, -1), (-2, -1)], 1)
    keep(1, from_right, [(0, 1), (-1, 1), (-2, 1)], 1)
    keep(2, far_below, [(2, 0)], 0)
    keep(2, far_above, [(2, -1), (2, 1), (2, 2)], 0)
    arrays, pieces = stages[2]
    for place, (array, row, kind) in (
        (0, (left_far, 0, 0)),
        (0, (left_far, rows, 1)),
        (-1, (left_far, block, 0)),
        (-1, (right_far, 0, 1)),
        (-2, (right_far, rows, 0)),
        (-2, (right_far, block, 1)),
    ):
        index = len(arrays) + (array is right_far)
        pieces.append((index, row, place % 4, 2, 1, kind))
    arrays.extend([left_far, right_far])
    return state, stages[1:]


def gather_x(tokens):
    half = tokens.shape[0] // 2
    a, b = x_send(tokens, 1), x_send(tokens, -1)
    return a, b, x_send(a[:half], 1), x_send(b[half:], -1)


def body(tokens, norm_gain, w_query, key_weight, value_weight, w_output, doc_lengths):
    rows = tokens.shape[0]
    dp = lax.axis_index("dp").astype(jnp.int32)
    x = lax.axis_index("tensor").astype(jnp.int32)
    idx = jnp.stack([dp // 8, (dp // 2) % 4, dp % 2, x])
    positions = dp * rows + jnp.arange(rows, dtype=jnp.int32)
    cosine, sine = rope_tables(positions, doc_lengths)

    xn, mine, send = kv_project(
        idx, tokens, *gather_x(tokens), norm_gain[None, :], key_weight, value_weight, cosine, sine
    )
    other = dp_send(send, dc=1)
    xn, other = lax.optimization_barrier((xn, other))
    a_line, b_line = exchange_near(mine, other)
    q_send, q_mine = q_project(idx, xn, w_query, cosine, sine)
    a_line, b_line, q_send, q_mine = lax.optimization_barrier((a_line, b_line, q_send, q_mine))
    q_other = dp_send(q_send, dc=1)
    queries = (q_mine, q_other)
    total = rows * 32

    def first_call(kv):
        return attention(idx, doc_lengths, kv, queries, (), None, total)

    state, stages = exchange(a_line, b_line, rows, first_call)
    arrays, pieces = list(stages[0][0]), list(stages[0][1])
    for array, *place in stages[1][1]:
        pieces.append((len(arrays) + array, *place))
    arrays += stages[1][0]

    mixed = attention(idx, doc_lengths, (arrays, pieces), queries, state, 0, total)
    up, down, kept = reduce_near(idx, w_output, mixed)
    state, up, down = lax.optimization_barrier((state, up, down))
    got0 = x_send(up, 1), x_send(down, -1)
    mixed = attention(idx, doc_lengths, (arrays, pieces), queries, state, 1, total)
    mixed, got0 = lax.optimization_barrier((mixed, got0))
    result0 = reduce_end(kept, *got0)
    up, down, kept = reduce_near(idx, w_output, mixed)
    result1 = reduce_end(kept, x_send(up, 1), x_send(down, -1))
    return jnp.concatenate([result0, result1], axis=0)


def reduce_near(idx, w_output, mixed):
    group = mixed.shape[0] // 2
    other = dp_send(mixed[group:], dc=1)
    far = out_project(idx, w_output, mixed[:group], other, (2,), BF)
    half, width = far.shape[0] // 2, far.shape[1]
    far_up, far_down = x_send(far[:half], 1), x_send(far[half:], -1)
    near = out_project(idx, w_output, mixed[:group], other, (1, 3, 0), F32)
    nothing = jnp.zeros_like(far_up)
    up = near[:, :width] + jnp.concatenate([far_up, nothing], axis=0)
    down = near[:, width : 2 * width] + jnp.concatenate([nothing, far_down], axis=0)
    return up.astype(BF), down.astype(BF), near[:, 2 * width :]


def reduce_end(kept, from_up, from_down):
    return (kept + from_up.astype(F32) + from_down.astype(F32)).astype(BF)


def solution(mesh):
    return jax.shard_map(
        body,
        mesh=mesh,
        in_specs=(
            P("dp", "tensor"),
            P(),
            P(None, "tensor"),
            P(None, "tensor"),
            P(None, "tensor"),
            P("tensor", None),
            P(),
        ),
        out_specs=P("dp", "tensor"),
        check_vma=False,
    )
```

```python
import functools

import jax
import jax.numpy as jnp
from jax import lax
from jax.experimental import pallas as pl
from jax.experimental.pallas import tpu as pltpu
from jax.sharding import PartitionSpec as P

HD = 128
EPSILON = 1e-05
THETA = 500000.0
NEGATIVE = -1e30
DIMS = (4, 4, 2)
BF = jnp.bfloat16
F32 = jnp.float32
MIB = 1 << 20
LOG2E = 1.4426950408889634


def dp_perm(dz, dy, dc):
    nz, ny, nc = DIMS
    pairs = []
    for z in range(nz):
        for y in range(ny):
            for c in range(nc):
                src = (z * ny + y) * nc + c
                dst = (((z + dz) % nz) * ny + (y + dy) % ny) * nc + (c + dc) % nc
                pairs.append((src, dst))
    return pairs


def dp_send(value, dz=0, dy=0, dc=0):
    return lax.ppermute(value, "dp", dp_perm(dz, dy, dc))


def x_send(value, shift):
    return lax.ppermute(value, "tensor", [(i, (i + shift) % 4) for i in range(4)])


def cost(flops, bytes_accessed, transcendentals=0):
    return pl.CostEstimate(
        flops=int(flops), bytes_accessed=int(bytes_accessed), transcendentals=int(transcendentals)
    )


def rope_tables(positions, doc_lengths):
    doc_starts = jnp.cumsum(doc_lengths) - doc_lengths
    doc_first = jnp.max(
        jnp.where(doc_starts[None, :] <= positions[:, None], doc_starts[None, :], 0), axis=1
    )
    half_size = HD // 2
    exponents = jnp.arange(half_size, dtype=F32) * (2.0 / HD)
    frequency = jnp.exp(-exponents * jnp.log(F32(THETA)))
    angles = (positions - doc_first).astype(F32)[:, None] * frequency[None, :]
    cosine, sine = jnp.cos(angles), jnp.sin(angles)
    return (
        jnp.concatenate([cosine, cosine], axis=1),
        jnp.concatenate([-sine, sine], axis=1),
    )


def rotate(value, cosine, sine):
    return value * cosine + pltpu.roll(value, HD // 2, 1) * sine


def norm_rows(idx_ref, pieces, gain_ref, inv_ref, xn_ref, fresh):
    t_ref, a_ref, b_ref, c_ref, d_ref = pieces
    rows, width = t_ref.shape
    half = rows // 2
    x = idx_ref[3]
    step = 64

    def cols(shift):
        return pl.ds(pl.multiple_of(lax.rem(x + shift, 4) * width, width), width)

    def some(far_ref, far_begin, begin):
        part = pl.ds(begin, step)
        parts = [
            (t_ref[part, :], 0),
            (a_ref[part, :], 3),
            (b_ref[part, :], 1),
            (far_ref[pl.ds(far_begin, step), :], 2),
        ]
        floats = [(p.astype(F32), s) for p, s in parts]
        if fresh:
            square = sum(jnp.sum(f * f, axis=1, keepdims=True) for f, _ in floats)
            inv = lax.rsqrt(square * (1.0 / (4 * width)) + EPSILON)
            inv_ref[part, :] = jnp.broadcast_to(inv, (step, HD))
        else:
            inv = inv_ref[part, :][:, :1]
        for f, s in floats:
            gain = gain_ref[:, cols(s)].astype(F32)
            xn_ref[part, cols(s)] = (f * inv * gain).astype(BF)

    def top(i, carry):
        some(c_ref, pl.multiple_of(i * step, step), pl.multiple_of(i * step, step))
        return carry

    def bottom(i, carry):
        some(d_ref, pl.multiple_of(i * step, step), pl.multiple_of(half + i * step, step))
        return carry

    lax.fori_loop(0, half // step, top, 0)
    lax.fori_loop(0, half // step, bottom, 0)


def kv_kernel(
    idx_ref, t_ref, a_ref, b_ref, c_ref, d_ref, gain_ref, wk_ref, wv_ref, cos_ref, sin_ref,
    inv_ref, mine_ref, send_ref, xn_ref,
):
    rows = t_ref.shape[0]
    core = idx_ref[2]
    norm_rows(idx_ref, (t_ref, a_ref, b_ref, c_ref, d_ref), gain_ref, inv_ref, xn_ref, True)
    keys = jnp.dot(xn_ref[...], wk_ref[...], preferred_element_type=F32)
    cosine, sine = cos_ref[...], sin_ref[...]
    key0 = rotate(keys[:, :HD], cosine, sine).astype(BF)
    key1 = rotate(keys[:, HD:], cosine, sine).astype(BF)

    def put(first, second, begin):
        @pl.when(core == 0)
        def _():
            mine_ref[pl.ds(begin, rows), :] = first
            send_ref[pl.ds(begin, rows), :] = second

        @pl.when(core != 0)
        def _():
            mine_ref[pl.ds(begin, rows), :] = second
            send_ref[pl.ds(begin, rows), :] = first

    put(key0, key1, 0)
    vals = jnp.dot(xn_ref[...], wv_ref[...], preferred_element_type=F32).astype(BF)
    put(vals[:, :HD], vals[:, HD:], rows)


def kv_project(idx, t, a, b, c, d, gain, wk, wv, cosine, sine):
    rows = t.shape[0]
    width = wk.shape[0]
    vm = pl.BlockSpec(memory_space=pltpu.VMEM)
    return pl.pallas_call(
        kv_kernel,
        out_shape=(
            jax.ShapeDtypeStruct((rows, HD), F32),
            jax.ShapeDtypeStruct((2 * rows, HD), BF),
            jax.ShapeDtypeStruct((2 * rows, HD), BF),
        ),
        in_specs=[pl.BlockSpec(memory_space=pltpu.SMEM)] + [vm] * 10,
        out_specs=(vm, vm, vm),
        scratch_shapes=[pltpu.VMEM((rows, width), BF)],
        compiler_params=pltpu.CompilerParams(vmem_limit_bytes=40 * MIB),
        cost_estimate=cost(2 * rows * width * 4 * HD, 12 * MIB),
        name="norm_keys_values",
    )(idx, t, a, b, c, d, gain, wk, wv, cosine, sine)


def q_kernel(
    idx_ref, t_ref, a_ref, b_ref, c_ref, d_ref, gain_ref, inv_ref, wq_ref, cos_ref, sin_ref,
    send_ref, mine_ref, xn_ref,
):
    j = pl.program_id(0)
    half = xn_ref.shape[0] // 2

    @pl.when(j == 0)
    def _():
        norm_rows(idx_ref, (t_ref, a_ref, b_ref, c_ref, d_ref), gain_ref, inv_ref, xn_ref, False)

    res = jnp.dot(xn_ref[...], wq_ref[...], preferred_element_type=F32)
    cosine, sine = cos_ref[...], sin_ref[...]
    heads = [rotate(res[:, e * HD : (e + 1) * HD], cosine, sine).astype(BF) for e in range(2)]

    def put(out_ref):
        for e in range(2):
            for t in range(2):
                begin = pl.multiple_of((t * 4 + lax.rem(j, 2) * 2 + e) * half, half)
                out_ref[pl.ds(begin, half), :] = heads[e][t * half : (t + 1) * half]

    @pl.when(j < 2)
    def _():
        put(send_ref)

    @pl.when(j >= 2)
    def _():
        put(mine_ref)


def q_project(idx, pieces, gain, inv, wq, cosine, sine):
    rows = pieces[0].shape[0]
    width = wq.shape[0]

    def w_map(j, idx_ref):
        core = idx_ref[2]
        group = jnp.where(j < 2, 1 - core, core)
        return (0, group * 2 + lax.rem(j, 2))

    full = lambda shape: pl.BlockSpec(shape, lambda j, idx_ref: (0,) * len(shape))
    return pl.pallas_call(
        q_kernel,
        out_shape=tuple(jax.ShapeDtypeStruct((4 * rows, HD), BF) for _ in range(2)),
        grid_spec=pltpu.PrefetchScalarGridSpec(
            num_scalar_prefetch=1,
            grid=(4,),
            in_specs=[
                *[full(p.shape) for p in pieces],
                full(gain.shape),
                full(inv.shape),
                pl.BlockSpec((width, 2 * HD), w_map),
                full((rows, HD)),
                full((rows, HD)),
            ],
            out_specs=tuple(full((4 * rows, HD)) for _ in range(2)),
            scratch_shapes=[pltpu.VMEM((rows, width), BF)],
        ),
        compiler_params=pltpu.CompilerParams(
            vmem_limit_bytes=58 * MIB, dimension_semantics=("arbitrary",)
        ),
        cost_estimate=cost(2 * rows * width * 8 * HD, 14 * MIB),
        name="queries",
    )(idx, *pieces, gain, inv, wq, cosine, sine)


SCALE2 = HD ** (-0.5) * LOG2E
CHUNK = 256


def attention_kernel(pieces, n_kv, half, idx_ref, len_ref, *refs):
    first_stage = half is None
    kv_refs, refs = refs[:n_kv], refs[n_kv:]
    q_refs, refs = refs[:2], refs[2:]
    if first_stage:
        acc, top, refs = refs[0], refs[1], refs[2:]
    else:
        acc_in, top_in, o_ref, acc, top, refs = *refs[:5], refs[5:]
    key_ref, val_ref, q_ref, key_doc, q_doc, todo_ref, sem = refs
    z, y, core = idx_ref[0], idx_ref[1], idx_ref[2]
    rows = q_ref.shape[0]
    size = key_ref.shape[0] // 32
    group = 4 * CHUNK
    halves = (0, 1) if first_stage else (half,)
    own = [(z * 4 + y) * 2 + lax.rem(core + g, 2) for g in range(2)]
    lower = jnp.minimum(own[0], own[1])
    copies = []

    def fetch(source, target):
        copy = pltpu.make_async_copy(source, target, sem.at[len(copies)])
        copy.start()
        copies.append(copy)

    for n, t in enumerate(halves):
        for g in range(2):
            fetch(
                q_refs[g].at[pl.ds(t * group, group), :],
                q_ref.at[pl.ds((2 * n + g) * group, group), :],
            )
    if not first_stage:
        fetch(acc_in.at[pl.ds(half * rows, rows), :], acc)
        fetch(top_in.at[pl.ds(half * rows, rows), :], top)
    for array, row, dz, dy, dc, kind in pieces:
        block = (lax.rem(z + dz, 4) * 4 + lax.rem(y + dy, 4)) * 2 + lax.rem(core + dc, 2)
        begin = pl.multiple_of(block * size, size)
        fetch(kv_refs[array].at[pl.ds(row, size), :], (key_ref, val_ref)[kind].at[pl.ds(begin, size), :])
    if first_stage:
        top[...] = jnp.full_like(top, NEGATIVE)
        acc[...] = jnp.zeros_like(acc)

    lane = lax.broadcasted_iota(jnp.int32, (1, HD), 1)
    starts = jnp.zeros((1, HD), jnp.int32)
    ends = jnp.zeros((1, HD), jnp.int32)
    first = jnp.int32(0)
    begin = jnp.int32(0)
    for i in range(8):
        first = jnp.where(begin <= lower * size, begin, first)
        starts = jnp.where(lane == i, begin, starts)
        begin = begin + len_ref[i]
        ends = jnp.where(lane == i, begin, ends)
    lo = first // size

    def inside(begin, count):
        pos = begin + lax.broadcasted_iota(jnp.int32, (count, HD), 0)
        return (pos >= starts) & (pos < ends)

    def mark_keys(j, carry):
        span = pl.ds(pl.multiple_of(j * size, size), size)
        key_doc[span, :] = jnp.where(inside(j * size, size), 1.0, 0.0).astype(BF)
        return carry

    for n, t in enumerate(halves):
        for g in range(2):
            there = inside(own[g] * size + t * CHUNK, CHUNK) | (lane >= 8)
            mark = jnp.where(there, 0.0, NEGATIVE).astype(BF)
            for h in range(4):
                row = (2 * n + g) * group + h * CHUNK
                q_doc[row : row + CHUNK, :] = mark
    ones = jnp.ones((size, HD), BF)

    def local(j):
        return jnp.where(lax.rem(j, 2) == core, j // 8 == z, lax.rem(j // 2, 4) == y)

    def load(blocks):
        spans = [pl.ds(pl.multiple_of(j * size, size), size) for j in blocks]
        keys = [jnp.concatenate([key_ref[span, :], key_doc[span, :]], axis=1) for span in spans]
        vals = [jnp.concatenate([val_ref[span, :], ones], axis=1) for span in spans]
        if len(blocks) == 1:
            return keys[0], vals[0]
        return jnp.concatenate(keys, axis=0), jnp.concatenate(vals, axis=0)

    def scores(row, key):
        span = pl.ds(row, CHUNK)
        query = jnp.concatenate([q_ref[span, :], q_doc[span, :]], axis=1)
        return lax.dot_general(
            query, key, (((1,), (1,)), ((), ())), preferred_element_type=F32
        )

    def absorb(row, s, val):
        span = pl.ds(row, CHUNK)
        old = top[span, :]
        new = jnp.maximum(old, jnp.max(s, axis=1, keepdims=True))
        top[span, :] = new
        alpha = jnp.exp2((old - new) * SCALE2)
        p = jnp.exp2((s - new[:, :1]) * SCALE2).astype(BF)
        pv = jnp.dot(p, val, preferred_element_type=F32)
        acc[span, :HD] = acc[span, :HD] * alpha + pv[:, :HD]
        acc[span, HD:] = acc[span, HD:] * alpha + pv[:, HD:]

    def whole(blocks):
        key, val = load(blocks)
        following = scores(0, key)
        for row in range(0, rows, CHUNK):
            s = following
            if row + CHUNK < rows:
                following = scores(row + CHUNK, key)
            absorb(row, s, val)

    def within(g, blocks):
        key, val = load(blocks)
        before = size * (len(blocks) - 1)
        order = [(t, h) for t in range(2) for h in range(4)]

        def row(t, h):
            return pl.multiple_of((2 * t + g) * group + h * CHUNK, CHUNK)

        def part(n):
            return scores(row(*order[n]), key[: before + (order[n][0] + 1) * CHUNK])

        square = (CHUNK, CHUNK)
        causal = lax.broadcasted_iota(jnp.int32, square, 0) >= lax.broadcasted_iota(jnp.int32, square, 1)
        following = part(0)
        for n, (t, h) in enumerate(order):
            s = following
            if n + 1 < len(order):
                following = part(n + 1)
            edge = before + t * CHUNK
            corner = jnp.where(causal, s[:, edge:], NEGATIVE)
            s = corner if edge == 0 else jnp.concatenate([s[:, :edge], corner], axis=1)
            absorb(row(t, h), s, val[: edge + CHUNK])

    def collect(j, count):
        take = local(j) if first_stage else ~local(j)

        @pl.when(take)
        def _():
            todo_ref[count] = j
            mark_keys(j, 0)

        return count + take.astype(jnp.int32)

    count = lax.fori_loop(lo, lower, collect, jnp.int32(0))
    if first_stage:
        lax.fori_loop(lower, lower + 2, mark_keys, 0)
    for copy in copies:
        copy.wait()

    def pair(k, carry):
        whole([todo_ref[2 * k], todo_ref[2 * k + 1]])
        return carry

    lax.fori_loop(0, count // 2, pair, 0)

    @pl.when(lax.rem(count, 2) == 1)
    def _():
        whole([todo_ref[count - 1]])

    if first_stage:
        low_group = (own[0] != lower).astype(jnp.int32)
        within(low_group, [lower])
        within(1 - low_group, [lower, lower + 1])
    else:
        o_ref[...] = (acc[:, :HD] / acc[:, HD:]).astype(BF)


def attention(idx, doc_lengths, kv, queries, state, half, total_tokens):
    rows = queries[0].shape[0] * (2 if half is None else 1)
    smem = pl.BlockSpec(memory_space=pltpu.SMEM)
    hbm = pl.BlockSpec(memory_space=pl.ANY)
    vm = pl.BlockSpec(memory_space=pltpu.VMEM)
    arrays, pieces = kv
    wide, narrow = (rows, 2 * HD), (rows, HD)
    states = (jax.ShapeDtypeStruct(wide, F32), jax.ShapeDtypeStruct(narrow, F32))
    return pl.pallas_call(
        functools.partial(attention_kernel, pieces, len(arrays), half),
        out_shape=states if half is None else jax.ShapeDtypeStruct((rows, HD), BF),
        in_specs=[smem, smem] + [hbm] * (len(arrays) + 2 + len(state)),
        out_specs=(vm, vm) if half is None else vm,
        scratch_shapes=[
            *([] if half is None else [pltpu.VMEM(wide, F32), pltpu.VMEM(narrow, F32)]),
            pltpu.VMEM((total_tokens, HD), BF),
            pltpu.VMEM((total_tokens, HD), BF),
            pltpu.VMEM((rows, HD), BF),
            pltpu.VMEM((total_tokens, HD), BF),
            pltpu.VMEM((rows, HD), BF),
            pltpu.SMEM((32,), jnp.int32),
            pltpu.SemaphoreType.DMA((len(pieces) + 6,)),
        ],
        compiler_params=pltpu.CompilerParams(vmem_limit_bytes=58 * MIB),
        cost_estimate=cost(8e6 * 512, 10 * MIB, 8e6),
        name="attention",
    )(idx, doc_lengths, *arrays, *queries, *state)


def out_kernel(dests, idx_ref, w_ref, mine_ref, other_ref, out_ref, scr):
    core = idx_ref[2]
    rows = scr.shape[0]

    @pl.when(pl.program_id(0) == 0)
    def _():
        for g, ref in enumerate((mine_ref, other_ref)):
            group = lax.rem(core + g, 2) * (4 * HD)
            for h in range(4):
                column = pl.ds(pl.multiple_of(group + h * HD, HD), HD)
                scr[:, column] = ref[h * rows : (h + 1) * rows, :]

    out_ref[...] = jnp.dot(scr[...], w_ref[...], preferred_element_type=F32).astype(out_ref.dtype)


def out_project(idx, w, mine, other, dests, dtype):
    rows = mine.shape[0] // 4
    feat, model = w.shape
    width = model // 4
    block = 512
    per = width // block

    def w_map(j, idx_ref):
        shift = jnp.int32(dests[0])
        for n, s in enumerate(dests):
            shift = jnp.where(j >= n * per, s, shift)
        return (0, lax.rem(idx_ref[3] + shift, 4) * per + lax.rem(j, per))

    return pl.pallas_call(
        functools.partial(out_kernel, dests),
        out_shape=jax.ShapeDtypeStruct((rows, width * len(dests)), dtype),
        grid_spec=pltpu.PrefetchScalarGridSpec(
            num_scalar_prefetch=1,
            grid=(per * len(dests),),
            in_specs=[pl.BlockSpec((feat, block), w_map)]
            + [pl.BlockSpec((4 * rows, HD), lambda j, idx_ref: (0, 0))] * 2,
            out_specs=pl.BlockSpec((rows, block), lambda j, idx_ref: (0, j)),
            scratch_shapes=[pltpu.VMEM((rows, feat), BF)],
        ),
        compiler_params=pltpu.CompilerParams(
            vmem_limit_bytes=32 * MIB, dimension_semantics=("arbitrary",)
        ),
        cost_estimate=cost(
            2 * rows * feat * width * len(dests), (2 * feat + 4 * rows) * width * len(dests)
        ),
        name="output_projection",
    )(idx, w, mine, other)


def exchange_near(mine, other, meanwhile):
    rows = mine.shape[0] // 2
    a_up, a_down = move_y(mine, 1), move_y(mine, -1)
    b_up, b_down_values = move_z(other, 1), move_z(other[rows:], -1)
    (a_up, a_down, b_up, b_down_values), meanwhile = lax.optimization_barrier(
        ((a_up, a_down, b_up, b_down_values), meanwhile)
    )
    b_far = [move_z(b_up[:rows], 1), move_z(b_down_values, -1)]
    a_far = [move_y(a_up[:rows], 1), move_y(a_down[rows:], -1)]
    a_line = jnp.concatenate([mine, a_up, a_down, *a_far], axis=0)
    b_line = jnp.concatenate([other, b_up, *b_far], axis=0)
    return a_line, b_line, meanwhile


def move_y(value, shift):
    return dp_send(value, dy=shift)


def move_z(value, shift):
    return dp_send(value, dz=shift)


def exchange(a_line, b_line, rows, first_call):
    block = 2 * rows
    stages = [([], []) for _ in range(3)]

    def keep(n, array, places, dc):
        arrays, pieces = stages[n]
        for i, (dz, dy) in enumerate(places):
            for kind in range(2):
                pieces.append((len(arrays), i * block + kind * rows, dz % 4, dy % 4, dc, kind))
        arrays.append(array)

    from_left, from_right = move_y(b_line, 1), move_y(b_line, -1)
    from_below, from_above = move_z(a_line, 1), move_z(a_line[2 * block :], -1)
    keep(0, a_line, [(0, 0), (0, -1), (0, 1), (0, 2)], 0)
    keep(0, b_line, [(0, 0), (-1, 0), (-2, 0)], 1)
    state = first_call(stages[0])
    state, from_left, from_right, from_below, from_above = lax.optimization_barrier(
        (state, from_left, from_right, from_below, from_above)
    )
    left_far = move_y(from_left[: block + rows], 1)
    right_far = move_y(from_right[block + rows :], -1)
    far_below, far_above = move_z(from_below[: 2 * block], 1), move_z(from_above, -1)

    keep(1, from_below, [(-1, 0), (-1, -1), (-1, 1), (-1, 2)], 0)
    keep(1, from_left, [(0, -1), (-1, -1), (-2, -1)], 1)
    keep(1, from_right, [(0, 1), (-1, 1), (-2, 1)], 1)
    keep(2, far_below, [(2, 0), (2, -1)], 0)
    keep(2, far_above, [(2, 1), (2, 2)], 0)
    arrays, pieces = stages[2]
    for place, (array, row, kind) in (
        (0, (left_far, 0, 0)),
        (0, (left_far, rows, 1)),
        (-1, (left_far, block, 0)),
        (-1, (right_far, 0, 1)),
        (-2, (right_far, rows, 0)),
        (-2, (right_far, block, 1)),
    ):
        index = len(arrays) + (array is right_far)
        pieces.append((index, row, place % 4, 2, 1, kind))
    arrays.extend([left_far, right_far])
    return state, stages[1:]


def gather_x(tokens):
    half = tokens.shape[0] // 2
    a, b = x_send(tokens, 1), x_send(tokens, -1)
    return a, b, x_send(a[:half], 1), x_send(b[half:], -1)


def body(tokens, norm_gain, w_query, key_weight, value_weight, w_output, doc_lengths):
    rows = tokens.shape[0]
    dp = lax.axis_index("dp").astype(jnp.int32)
    x = lax.axis_index("tensor").astype(jnp.int32)
    idx = jnp.stack([dp // 8, (dp // 2) % 4, dp % 2, x])
    positions = dp * rows + jnp.arange(rows, dtype=jnp.int32)
    cosine, sine = rope_tables(positions, doc_lengths)

    gain = norm_gain[None, :]
    pieces = (tokens, *gather_x(tokens))
    inv, mine, send = kv_project(
        idx, *pieces, gain, key_weight, value_weight, cosine, sine
    )
    other = dp_send(send, dc=1)
    inv, other = lax.optimization_barrier((inv, other))
    queries = q_project(idx, pieces, gain, inv, w_query, cosine, sine)
    a_line, b_line, (q_send, q_mine) = exchange_near(mine, other, queries)
    a_line, b_line = lax.optimization_barrier((a_line, b_line))
    q_other = dp_send(q_send, dc=1)
    queries = (q_mine, q_other)
    total = rows * 32

    def first_call(kv):
        return attention(idx, doc_lengths, kv, queries, (), None, total)

    state, stages = exchange(a_line, b_line, rows, first_call)
    arrays, pieces = list(stages[0][0]), list(stages[0][1])
    for array, *place in stages[1][1]:
        pieces.append((len(arrays) + array, *place))
    arrays += stages[1][0]

    mixed = attention(idx, doc_lengths, (arrays, pieces), queries, state, 0, total)
    up, down, kept = reduce_near(idx, w_output, mixed)
    state, up, down = lax.optimization_barrier((state, up, down))
    got0 = x_send(up, 1), x_send(down, -1)
    mixed = attention(idx, doc_lengths, (arrays, pieces), queries, state, 1, total)
    mixed, got0 = lax.optimization_barrier((mixed, got0))
    result0 = reduce_end(kept, *got0)
    up, down, kept = reduce_near(idx, w_output, mixed)
    result1 = reduce_end(kept, x_send(up, 1), x_send(down, -1))
    return jnp.concatenate([result0, result1], axis=0)


def reduce_near(idx, w_output, mixed):
    group = mixed.shape[0] // 2
    other = dp_send(mixed[group:], dc=1)
    far = out_project(idx, w_output, mixed[:group], other, (2,), BF)
    half, width = far.shape[0] // 2, far.shape[1]
    far_up, far_down = x_send(far[:half], 1), x_send(far[half:], -1)
    near = out_project(idx, w_output, mixed[:group], other, (1, 3, 0), F32)
    nothing = jnp.zeros_like(far_up)
    up = near[:, :width] + jnp.concatenate([far_up, nothing], axis=0)
    down = near[:, width : 2 * width] + jnp.concatenate([nothing, far_down], axis=0)
    return up.astype(BF), down.astype(BF), near[:, 2 * width :]


def reduce_end(kept, from_up, from_down):
    return (kept + from_up.astype(F32) + from_down.astype(F32)).astype(BF)


def solution(mesh):
    return jax.shard_map(
        body,
        mesh=mesh,
        in_specs=(
            P("dp", "tensor"),
            P(),
            P(None, "tensor"),
            P(None, "tensor"),
            P(None, "tensor"),
            P("tensor", None),
            P(),
        ),
        out_specs=P("dp", "tensor"),
        check_vma=False,
    )
```

```python
import functools

import jax
import jax.numpy as jnp
from jax import lax
from jax.experimental import pallas as pl
from jax.experimental.pallas import tpu as pltpu
from jax.sharding import PartitionSpec as P

HD = 128
EPSILON = 1e-05
THETA = 500000.0
NEGATIVE = -1e30
DIMS = (4, 4, 2)
BF = jnp.bfloat16
F32 = jnp.float32
MIB = 1 << 20
LOG2E = 1.4426950408889634


def dp_perm(dz, dy, dc):
    nz, ny, nc = DIMS
    pairs = []
    for z in range(nz):
        for y in range(ny):
            for c in range(nc):
                src = (z * ny + y) * nc + c
                dst = (((z + dz) % nz) * ny + (y + dy) % ny) * nc + (c + dc) % nc
                pairs.append((src, dst))
    return pairs


def dp_send(value, dz=0, dy=0, dc=0):
    return lax.ppermute(value, "dp", dp_perm(dz, dy, dc))


def x_send(value, shift):
    return lax.ppermute(value, "tensor", [(i, (i + shift) % 4) for i in range(4)])


def cost(flops, bytes_accessed, transcendentals=0):
    return pl.CostEstimate(
        flops=int(flops), bytes_accessed=int(bytes_accessed), transcendentals=int(transcendentals)
    )


def rope_tables(positions, doc_lengths):
    doc_starts = jnp.cumsum(doc_lengths) - doc_lengths
    doc_first = jnp.max(
        jnp.where(doc_starts[None, :] <= positions[:, None], doc_starts[None, :], 0), axis=1
    )
    half_size = HD // 2
    exponents = jnp.arange(half_size, dtype=F32) * (2.0 / HD)
    frequency = jnp.exp(-exponents * jnp.log(F32(THETA)))
    angles = (positions - doc_first).astype(F32)[:, None] * frequency[None, :]
    cosine, sine = jnp.cos(angles), jnp.sin(angles)
    return (
        jnp.concatenate([cosine, cosine], axis=1),
        jnp.concatenate([-sine, sine], axis=1),
    )


def rotate(value, cosine, sine):
    return value * cosine + pltpu.roll(value, HD // 2, 1) * sine


def norm_rows(idx_ref, pieces, gain_ref, inv_ref, xn_ref, fresh):
    t_ref, *halves = pieces
    rows, width = t_ref.shape
    half = rows // 2
    x = idx_ref[3]
    step = 64

    def cols(shift):
        return pl.ds(pl.multiple_of(lax.rem(x + shift, 4) * width, width), width)

    def some(n, inner):
        part = pl.ds(n * half + inner, step)
        near = pl.ds(inner, step)
        below, above, far = halves[n], halves[2 + n], halves[4 + n]
        parts = [
            (t_ref[part, :], 0),
            (below[near, :], 3),
            (above[near, :], 1),
            (far[near, :], 2),
        ]
        floats = [(p.astype(F32), s) for p, s in parts]
        if fresh:
            square = sum(jnp.sum(f * f, axis=1, keepdims=True) for f, _ in floats)
            inv = lax.rsqrt(square * (1.0 / (4 * width)) + EPSILON)
            inv_ref[part, :] = jnp.broadcast_to(inv, (step, HD))
        else:
            inv = inv_ref[part, :][:, :1]
        for f, s in floats:
            gain = gain_ref[:, cols(s)].astype(F32)
            xn_ref[part, cols(s)] = (f * inv * gain).astype(BF)

    for n in range(2):

        def advance(i, carry, n=n):
            some(n, pl.multiple_of(i * step, step))
            return carry

        lax.fori_loop(0, half // step, advance, 0)


def kv_kernel(idx_ref, *refs):
    pieces, refs = refs[:7], refs[7:]
    gain_ref, wk_ref, wv_ref, cos_ref, sin_ref, inv_ref, mine_ref, send_ref, xn_ref = refs
    rows = xn_ref.shape[0]
    core = idx_ref[2]
    norm_rows(idx_ref, pieces, gain_ref, inv_ref, xn_ref, True)
    keys = jnp.dot(xn_ref[...], wk_ref[...], preferred_element_type=F32)
    cosine, sine = cos_ref[...], sin_ref[...]
    key0 = rotate(keys[:, :HD], cosine, sine).astype(BF)
    key1 = rotate(keys[:, HD:], cosine, sine).astype(BF)

    def put(first, second, begin):
        @pl.when(core == 0)
        def _():
            mine_ref[pl.ds(begin, rows), :] = first
            send_ref[pl.ds(begin, rows), :] = second

        @pl.when(core != 0)
        def _():
            mine_ref[pl.ds(begin, rows), :] = second
            send_ref[pl.ds(begin, rows), :] = first

    put(key0, key1, 0)
    vals = jnp.dot(xn_ref[...], wv_ref[...], preferred_element_type=F32).astype(BF)
    put(vals[:, :HD], vals[:, HD:], rows)


def kv_project(idx, pieces, gain, wk, wv, cosine, sine):
    rows = pieces[0].shape[0]
    width = wk.shape[0]
    vm = pl.BlockSpec(memory_space=pltpu.VMEM)
    return pl.pallas_call(
        kv_kernel,
        out_shape=(
            jax.ShapeDtypeStruct((rows, HD), F32),
            jax.ShapeDtypeStruct((2 * rows, HD), BF),
            jax.ShapeDtypeStruct((2 * rows, HD), BF),
        ),
        in_specs=[pl.BlockSpec(memory_space=pltpu.SMEM)] + [vm] * 12,
        out_specs=(vm, vm, vm),
        scratch_shapes=[pltpu.VMEM((rows, width), BF)],
        compiler_params=pltpu.CompilerParams(vmem_limit_bytes=40 * MIB),
        cost_estimate=cost(2 * rows * width * 4 * HD, 12 * MIB),
        name="norm_keys_values",
    )(idx, *pieces, gain, wk, wv, cosine, sine)


def q_kernel(idx_ref, *refs):
    pieces, refs = refs[:7], refs[7:]
    gain_ref, inv_ref, wq_ref, cos_ref, sin_ref, send_ref, mine_ref, xn_ref = refs
    j = pl.program_id(0)
    half = xn_ref.shape[0] // 2

    @pl.when(j == 0)
    def _():
        norm_rows(idx_ref, pieces, gain_ref, inv_ref, xn_ref, False)

    res = jnp.dot(xn_ref[...], wq_ref[...], preferred_element_type=F32)
    cosine, sine = cos_ref[...], sin_ref[...]
    heads = [rotate(res[:, e * HD : (e + 1) * HD], cosine, sine).astype(BF) for e in range(2)]

    def put(out_ref):
        for e in range(2):
            for t in range(2):
                begin = pl.multiple_of((t * 4 + lax.rem(j, 2) * 2 + e) * half, half)
                out_ref[pl.ds(begin, half), :] = heads[e][t * half : (t + 1) * half]

    @pl.when(j < 2)
    def _():
        put(send_ref)

    @pl.when(j >= 2)
    def _():
        put(mine_ref)


def q_project(idx, pieces, gain, inv, wq, cosine, sine):
    rows = pieces[0].shape[0]
    width = wq.shape[0]

    def w_map(j, idx_ref):
        core = idx_ref[2]
        group = jnp.where(j < 2, 1 - core, core)
        return (0, group * 2 + lax.rem(j, 2))

    full = lambda shape: pl.BlockSpec(shape, lambda j, idx_ref: (0,) * len(shape))
    return pl.pallas_call(
        q_kernel,
        out_shape=tuple(jax.ShapeDtypeStruct((4 * rows, HD), BF) for _ in range(2)),
        grid_spec=pltpu.PrefetchScalarGridSpec(
            num_scalar_prefetch=1,
            grid=(4,),
            in_specs=[
                *[full(p.shape) for p in pieces],
                full(gain.shape),
                full(inv.shape),
                pl.BlockSpec((width, 2 * HD), w_map),
                full((rows, HD)),
                full((rows, HD)),
            ],
            out_specs=tuple(full((4 * rows, HD)) for _ in range(2)),
            scratch_shapes=[pltpu.VMEM((rows, width), BF)],
        ),
        compiler_params=pltpu.CompilerParams(
            vmem_limit_bytes=58 * MIB, dimension_semantics=("arbitrary",)
        ),
        cost_estimate=cost(2 * rows * width * 8 * HD, 14 * MIB),
        name="queries",
    )(idx, *pieces, gain, inv, wq, cosine, sine)


SCALE2 = HD ** (-0.5) * LOG2E
CHUNK = 256
ATTENTION_VMEM = 36 * MIB


def attention_kernel(pieces, n_kv, call, last_call, idx_ref, len_ref, *refs):
    kv_refs, refs = refs[:n_kv], refs[n_kv:]
    q_refs, refs = refs[:2], refs[2:]
    if call > 0:
        acc_in, top_in, refs = refs[0], refs[1], refs[2:]
    if call == last_call:
        o_ref, refs = refs[0], refs[1:]
    acc, top, key_ref, val_ref, q_ref, key_doc, q_doc, todo_ref, sem = refs
    z, y, core = idx_ref[0], idx_ref[1], idx_ref[2]
    rows = q_ref.shape[0]
    size = key_ref.shape[0] // 32
    group = rows // 2
    own = [(z * 4 + y) * 2 + lax.rem(core + g, 2) for g in range(2)]
    lower = jnp.minimum(own[0], own[1])
    copies = []

    def fetch(source, target):
        copy = pltpu.make_async_copy(source, target, sem.at[len(copies)])
        copy.start()
        copies.append(copy)

    for g in range(2):
        fetch(q_refs[g], q_ref.at[pl.ds(g * group, group), :])
    if call > 0:
        fetch(acc_in, acc)
        fetch(top_in, top)
    for array, row, dz, dy, dc, kind in pieces:
        block = (lax.rem(z + dz, 4) * 4 + lax.rem(y + dy, 4)) * 2 + lax.rem(core + dc, 2)
        begin = pl.multiple_of(block * size, size)
        fetch(kv_refs[array].at[pl.ds(row, size), :], (key_ref, val_ref)[kind].at[pl.ds(begin, size), :])
    if call == 0:
        top[...] = jnp.full_like(top, NEGATIVE)
        acc[...] = jnp.zeros_like(acc)

    lane = lax.broadcasted_iota(jnp.int32, (1, HD), 1)
    starts = jnp.zeros((1, HD), jnp.int32)
    ends = jnp.zeros((1, HD), jnp.int32)
    first = jnp.int32(0)
    begin = jnp.int32(0)
    for i in range(8):
        first = jnp.where(begin <= lower * size, begin, first)
        starts = jnp.where(lane == i, begin, starts)
        begin = begin + len_ref[i]
        ends = jnp.where(lane == i, begin, ends)
    lo = first // size

    def inside(begin, count):
        pos = begin + lax.broadcasted_iota(jnp.int32, (count, HD), 0)
        return (pos >= starts) & (pos < ends)

    def mark_keys(j, carry):
        span = pl.ds(pl.multiple_of(j * size, size), size)
        key_doc[span, :] = jnp.where(inside(j * size, size), 1.0, 0.0).astype(BF)
        return carry

    for g in range(2):
        for t in range(2):
            there = inside(own[g] * size + t * CHUNK, CHUNK) | (lane >= 8)
            mark = jnp.where(there, 0.0, NEGATIVE).astype(BF)
            for h in range(4):
                row = g * group + (t * 4 + h) * CHUNK
                q_doc[row : row + CHUNK, :] = mark
    ones = jnp.ones((size, HD), BF)

    def stage(j):
        away = jnp.where(
            lax.rem(j, 2) == core, lax.rem(j // 8 - z + 4, 4), lax.rem(lax.rem(j // 2, 4) - y + 4, 4)
        )
        return jnp.where(away == 0, 0, jnp.where(away == 2, 2, 1))

    def load(blocks):
        spans = [pl.ds(pl.multiple_of(j * size, size), size) for j in blocks]
        keys = [jnp.concatenate([key_ref[span, :], key_doc[span, :]], axis=1) for span in spans]
        vals = [jnp.concatenate([val_ref[span, :], ones], axis=1) for span in spans]
        if len(blocks) == 1:
            return keys[0], vals[0]
        return jnp.concatenate(keys, axis=0), jnp.concatenate(vals, axis=0)

    def scores(row, key):
        span = pl.ds(row, CHUNK)
        query = jnp.concatenate([q_ref[span, :], q_doc[span, :]], axis=1)
        return lax.dot_general(
            query, key, (((1,), (1,)), ((), ())), preferred_element_type=F32
        )

    def absorb(row, s, val):
        span = pl.ds(row, CHUNK)
        old = top[span, :]
        new = jnp.maximum(old, jnp.max(s, axis=1, keepdims=True))
        top[span, :] = new
        alpha = jnp.exp2((old - new) * SCALE2)
        p = jnp.exp2((s - new[:, :1]) * SCALE2).astype(BF)
        pv = jnp.dot(p, val, preferred_element_type=F32)
        acc[span, :HD] = acc[span, :HD] * alpha + pv[:, :HD]
        acc[span, HD:] = acc[span, HD:] * alpha + pv[:, HD:]

    def whole(blocks):
        key, val = load(blocks)
        following = scores(0, key)
        for row in range(0, rows, CHUNK):
            s = following
            if row + CHUNK < rows:
                following = scores(row + CHUNK, key)
            absorb(row, s, val)

    def within(g, blocks):
        key, val = load(blocks)
        before = size * (len(blocks) - 1)
        order = [(t, h) for t in range(2) for h in range(4)]

        def row(t, h):
            return pl.multiple_of(g * group + (t * 4 + h) * CHUNK, CHUNK)

        def part(n):
            return scores(row(*order[n]), key[: before + (order[n][0] + 1) * CHUNK])

        square = (CHUNK, CHUNK)
        causal = lax.broadcasted_iota(jnp.int32, square, 0) >= lax.broadcasted_iota(jnp.int32, square, 1)
        following = part(0)
        for n, (t, h) in enumerate(order):
            s = following
            if n + 1 < len(order):
                following = part(n + 1)
            edge = before + t * CHUNK
            corner = jnp.where(causal, s[:, edge:], NEGATIVE)
            s = corner if edge == 0 else jnp.concatenate([s[:, :edge], corner], axis=1)
            absorb(row(t, h), s, val[: edge + CHUNK])

    def collect(j, count):
        take = stage(j) == call

        @pl.when(take)
        def _():
            todo_ref[count] = j
            mark_keys(j, 0)

        return count + take.astype(jnp.int32)

    count = lax.fori_loop(lo, lower, collect, jnp.int32(0))
    if call == 0:
        lax.fori_loop(lower, lower + 2, mark_keys, 0)
    for copy in copies:
        copy.wait()

    def pair(k, carry):
        whole([todo_ref[2 * k], todo_ref[2 * k + 1]])
        return carry

    lax.fori_loop(0, count // 2, pair, 0)

    @pl.when(lax.rem(count, 2) == 1)
    def _():
        whole([todo_ref[count - 1]])

    if call == 0:
        low_group = (own[0] != lower).astype(jnp.int32)
        within(low_group, [lower])
        within(1 - low_group, [lower, lower + 1])
    if call == last_call:
        o_ref[...] = (acc[:, :HD] / acc[:, HD:]).astype(BF)


def attention(idx, doc_lengths, kv, queries, state, call, last_call, total_tokens):
    rows = 2 * queries[0].shape[0]
    smem = pl.BlockSpec(memory_space=pltpu.SMEM)
    hbm = pl.BlockSpec(memory_space=pl.ANY)
    vm = pl.BlockSpec(memory_space=pltpu.VMEM)
    arrays, pieces = kv
    last = call == last_call
    wide, narrow = (rows, 2 * HD), (rows, HD)
    states = (jax.ShapeDtypeStruct(wide, F32), jax.ShapeDtypeStruct(narrow, F32))
    return pl.pallas_call(
        functools.partial(attention_kernel, pieces, len(arrays), call, last_call),
        out_shape=jax.ShapeDtypeStruct((rows, HD), BF) if last else states,
        in_specs=[smem, smem] + [hbm] * (len(arrays) + 2 + len(state)),
        out_specs=vm if last else (vm, vm),
        scratch_shapes=[
            *([pltpu.VMEM(wide, F32), pltpu.VMEM(narrow, F32)] if last else []),
            pltpu.VMEM((total_tokens, HD), BF),
            pltpu.VMEM((total_tokens, HD), BF),
            pltpu.VMEM((rows, HD), BF),
            pltpu.VMEM((total_tokens, HD), BF),
            pltpu.VMEM((rows, HD), BF),
            pltpu.SMEM((32,), jnp.int32),
            pltpu.SemaphoreType.DMA((len(pieces) + 4,)),
        ],
        compiler_params=pltpu.CompilerParams(vmem_limit_bytes=ATTENTION_VMEM),
        cost_estimate=cost(8e6 * 512, 10 * MIB, 8e6),
        name="attention",
    )(idx, doc_lengths, *arrays, *queries, *state)


def out_kernel(dests, idx_ref, w_ref, mine_ref, other_ref, out_ref, scr):
    core = idx_ref[2]
    half = scr.shape[0] // 2

    @pl.when(pl.program_id(0) == 0)
    def _():
        for g, ref in enumerate((mine_ref, other_ref)):
            group = lax.rem(core + g, 2) * (4 * HD)
            for h in range(4):
                column = pl.ds(pl.multiple_of(group + h * HD, HD), HD)
                for t in range(2):
                    at = (t * 4 + h) * half
                    scr[t * half : (t + 1) * half, column] = ref[at : at + half, :]

    out_ref[...] = jnp.dot(scr[...], w_ref[...], preferred_element_type=F32).astype(out_ref.dtype)


def out_project(idx, w, mine, other, dests, dtype):
    rows = mine.shape[0] // 4
    feat, model = w.shape
    width = model // 4
    block = 512
    per = width // block

    def w_map(j, idx_ref):
        shift = jnp.int32(dests[0])
        for n, s in enumerate(dests):
            shift = jnp.where(j >= n * per, s, shift)
        return (0, lax.rem(idx_ref[3] + shift, 4) * per + lax.rem(j, per))

    return pl.pallas_call(
        functools.partial(out_kernel, dests),
        out_shape=jax.ShapeDtypeStruct((rows, width * len(dests)), dtype),
        grid_spec=pltpu.PrefetchScalarGridSpec(
            num_scalar_prefetch=1,
            grid=(per * len(dests),),
            in_specs=[pl.BlockSpec((feat, block), w_map)]
            + [pl.BlockSpec((4 * rows, HD), lambda j, idx_ref: (0, 0))] * 2,
            out_specs=pl.BlockSpec((rows, block), lambda j, idx_ref: (0, j)),
            scratch_shapes=[pltpu.VMEM((rows, feat), BF)],
        ),
        compiler_params=pltpu.CompilerParams(
            vmem_limit_bytes=32 * MIB, dimension_semantics=("arbitrary",)
        ),
        cost_estimate=cost(
            2 * rows * feat * width * len(dests), (2 * feat + 4 * rows) * width * len(dests)
        ),
        name="output_projection",
    )(idx, w, mine, other)


def exchange_near(mine, other, meanwhile):
    rows = mine.shape[0] // 2
    a_up, a_down = move_y(mine, 1), move_y(mine, -1)
    b_up, b_down_values = move_z(other, 1), move_z(other[rows:], -1)
    (a_up, a_down, b_up, b_down_values), meanwhile = lax.optimization_barrier(
        ((a_up, a_down, b_up, b_down_values), meanwhile)
    )
    b_far = [move_z(b_up[:rows], 1), move_z(b_down_values, -1)]
    a_far = [move_y(a_up[:rows], 1), move_y(a_down[rows:], -1)]
    a_line = jnp.concatenate([mine, a_up, a_down, *a_far], axis=0)
    b_line = jnp.concatenate([other, b_up, *b_far], axis=0)
    return a_line, b_line, meanwhile


def move_y(value, shift):
    return dp_send(value, dy=shift)


def move_z(value, shift):
    return dp_send(value, dz=shift)


def exchange(a_line, b_line, rows, attend):
    block = 2 * rows
    stages = [([], []) for _ in range(3)]

    def keep(n, array, places, dc):
        arrays, pieces = stages[n]
        for i, (dz, dy) in enumerate(places):
            for kind in range(2):
                pieces.append((len(arrays), i * block + kind * rows, dz % 4, dy % 4, dc, kind))
        arrays.append(array)

    from_left, from_right = move_y(b_line, 1), move_y(b_line, -1)
    from_below, from_above = move_z(a_line, 1), move_z(a_line[2 * block :], -1)
    keep(0, a_line, [(0, 0), (0, -1), (0, 1), (0, 2)], 0)
    keep(0, b_line, [(0, 0), (-1, 0), (-2, 0)], 1)
    state = attend(stages[0], (), 0)
    state, from_left, from_right, from_below, from_above = lax.optimization_barrier(
        (state, from_left, from_right, from_below, from_above)
    )
    left_far = move_y(from_left[: block + rows], 1)
    right_far = move_y(from_right[block + rows :], -1)
    far_below, far_above = move_z(from_below[: 2 * block], 1), move_z(from_above, -1)

    keep(1, from_below, [(-1, 0), (-1, -1), (-1, 1), (-1, 2)], 0)
    keep(1, from_left, [(0, -1), (-1, -1), (-2, -1)], 1)
    keep(1, from_right, [(0, 1), (-1, 1), (-2, 1)], 1)
    keep(2, far_below, [(2, 0), (2, -1)], 0)
    keep(2, far_above, [(2, 1), (2, 2)], 0)
    arrays, pieces = stages[2]
    for place, (array, row, kind) in (
        (0, (left_far, 0, 0)),
        (0, (left_far, rows, 1)),
        (-1, (left_far, block, 0)),
        (-1, (right_far, 0, 1)),
        (-2, (right_far, rows, 0)),
        (-2, (right_far, block, 1)),
    ):
        index = len(arrays) + (array is right_far)
        pieces.append((index, row, place % 4, 2, 1, kind))
    arrays.extend([left_far, right_far])
    state = attend(stages[1], state, 1)
    return attend(stages[2], state, 2)


def gather_x(tokens):
    half = tokens.shape[0] // 2
    top, bottom = tokens[:half], tokens[half:]
    below_top, above_bottom = x_send(top, 1), x_send(bottom, -1)
    below_top, above_bottom, top, bottom = lax.optimization_barrier(
        (below_top, above_bottom, top, bottom)
    )
    far_top, far_bottom = x_send(below_top, 1), x_send(above_bottom, -1)
    below_bottom, above_top = x_send(bottom, 1), x_send(top, -1)
    return below_top, below_bottom, above_top, above_bottom, far_top, far_bottom


def body(tokens, norm_gain, w_query, key_weight, value_weight, w_output, doc_lengths):
    rows = tokens.shape[0]
    dp = lax.axis_index("dp").astype(jnp.int32)
    x = lax.axis_index("tensor").astype(jnp.int32)
    idx = jnp.stack([dp // 8, (dp // 2) % 4, dp % 2, x])
    positions = dp * rows + jnp.arange(rows, dtype=jnp.int32)
    cosine, sine = rope_tables(positions, doc_lengths)

    gain = norm_gain[None, :]
    pieces = (tokens, *gather_x(tokens))
    inv, mine, send = kv_project(idx, pieces, gain, key_weight, value_weight, cosine, sine)
    other = dp_send(send, dc=1)
    inv, other = lax.optimization_barrier((inv, other))
    queries = q_project(idx, pieces, gain, inv, w_query, cosine, sine)
    a_line, b_line, (q_send, q_mine) = exchange_near(mine, other, queries)
    a_line, b_line = lax.optimization_barrier((a_line, b_line))
    q_other = dp_send(q_send, dc=1)
    queries = (q_mine, q_other)
    total = rows * 32

    def attend(kv, state, call):
        return attention(idx, doc_lengths, kv, queries, state, call, 2, total)

    mixed = exchange(a_line, b_line, rows, attend)
    group = mixed.shape[0] // 2
    return reduce_out(idx, w_output, mixed[:group], dp_send(mixed[group:], dc=1))


def reduce_out(idx, w_output, mixed, other):
    far = out_project(idx, w_output, mixed, other, (2,), BF)
    half, width = far.shape[0] // 2, far.shape[1]
    far_up, far_down = x_send(far[:half], 1), x_send(far[half:], -1)
    near = out_project(idx, w_output, mixed, other, (1, 3), F32)
    up_ready = x_send(near[half:, :width].astype(BF), 1)
    down_ready = x_send(near[:half, width:].astype(BF), -1)
    kept = out_project(idx, w_output, mixed, other, (0,), F32)
    up_sum = x_send((near[:half, :width] + far_up).astype(BF), 1)
    down_sum = x_send((near[half:, width:] + far_down).astype(BF), -1)
    top = kept[:half] + up_sum.astype(F32) + down_ready.astype(F32)
    bottom = kept[half:] + up_ready.astype(F32) + down_sum.astype(F32)
    return jnp.concatenate([top.astype(BF), bottom.astype(BF)], axis=0)


def solution(mesh):
    return jax.shard_map(
        body,
        mesh=mesh,
        in_specs=(
            P("dp", "tensor"),
            P(),
            P(None, "tensor"),
            P(None, "tensor"),
            P(None, "tensor"),
            P("tensor", None),
            P(),
        ),
        out_specs=P("dp", "tensor"),
        check_vma=False,
    )
```

```python
import functools

import jax
import jax.numpy as jnp
from jax import lax
from jax.experimental import pallas as pl
from jax.experimental.pallas import tpu as pltpu
from jax.sharding import PartitionSpec as P

HD = 128
EPSILON = 1e-05
THETA = 500000.0
NEGATIVE = -1e30
DIMS = (4, 4, 2)
BF = jnp.bfloat16
F32 = jnp.float32
MIB = 1 << 20
LOG2E = 1.4426950408889634


def dp_perm(dz, dy, dc):
    nz, ny, nc = DIMS
    pairs = []
    for z in range(nz):
        for y in range(ny):
            for c in range(nc):
                src = (z * ny + y) * nc + c
                dst = (((z + dz) % nz) * ny + (y + dy) % ny) * nc + (c + dc) % nc
                pairs.append((src, dst))
    return pairs


def dp_send(value, dz=0, dy=0, dc=0):
    return lax.ppermute(value, "dp", dp_perm(dz, dy, dc))


def x_send(value, shift):
    return lax.ppermute(value, "tensor", [(i, (i + shift) % 4) for i in range(4)])


def cost(flops, bytes_accessed, transcendentals=0):
    return pl.CostEstimate(
        flops=int(flops), bytes_accessed=int(bytes_accessed), transcendentals=int(transcendentals)
    )


def rope_tables(positions, doc_lengths):
    doc_starts = jnp.cumsum(doc_lengths) - doc_lengths
    doc_first = jnp.max(
        jnp.where(doc_starts[None, :] <= positions[:, None], doc_starts[None, :], 0), axis=1
    )
    half_size = HD // 2
    exponents = jnp.arange(half_size, dtype=F32) * (2.0 / HD)
    frequency = jnp.exp(-exponents * jnp.log(F32(THETA)))
    angles = (positions - doc_first).astype(F32)[:, None] * frequency[None, :]
    cosine, sine = jnp.cos(angles), jnp.sin(angles)
    return (
        jnp.concatenate([cosine, cosine], axis=1),
        jnp.concatenate([-sine, sine], axis=1),
    )


def rotate(value, cosine, sine):
    return value * cosine + pltpu.roll(value, HD // 2, 1) * sine


KV_ROWS = 128


def norm_rows(idx_ref, parts, gain_ref, xn_ref):
    rows, width = parts[0][0].shape
    x = idx_ref[3]
    step = 64

    def advance(i, carry):
        span = pl.ds(pl.multiple_of(i * step, step), step)
        square = jnp.zeros((step, HD), F32)
        for ref, _ in parts:
            for column in range(0, width, HD):
                f = ref[span, column : column + HD].astype(F32)
                square = square + f * f
        mean = jnp.sum(square, axis=1, keepdims=True) * (1.0 / (4 * width))
        inv = jnp.broadcast_to(lax.rsqrt(mean + EPSILON), (step, HD))
        for ref, shift in parts:
            begin = lax.rem(x + shift, 4) * width
            for column in range(0, width, HD):
                at = pl.ds(pl.multiple_of(begin + column, HD), HD)
                f = ref[span, column : column + HD].astype(F32)
                xn_ref[span, at] = (f * inv * gain_ref[:, at].astype(F32)).astype(BF)
        return carry

    lax.fori_loop(0, rows // step, advance, 0)


def kv_kernel(idx_ref, *refs):
    (t_ref, *halves), refs = refs[:7], refs[7:]
    gain_ref, wk_ref, wv_ref, cos_ref, sin_ref, xn_ref, mine_ref, send_ref = refs
    i = pl.program_id(0)
    steps = pl.num_programs(0)
    rows = xn_ref.shape[0]
    total = mine_ref.shape[0] // 2
    core = idx_ref[2]

    for n in range(2):

        @pl.when((i >= steps // 2) == (n == 1))
        def _(n=n):
            below, above, far = halves[n], halves[2 + n], halves[4 + n]
            parts = [(t_ref, 0), (below, 3), (above, 1), (far, 2)]
            norm_rows(idx_ref, parts, gain_ref, xn_ref)

    normed = xn_ref[...]
    keys = jnp.dot(normed, wk_ref[...], preferred_element_type=F32)
    cosine, sine = cos_ref[...], sin_ref[...]
    key0 = rotate(keys[:, :HD], cosine, sine).astype(BF)
    key1 = rotate(keys[:, HD:], cosine, sine).astype(BF)
    vals = jnp.dot(normed, wv_ref[...], preferred_element_type=F32).astype(BF)

    def put(first, second, offset):
        at = pl.ds(pl.multiple_of(offset + i * rows, rows), rows)

        @pl.when(core == 0)
        def _():
            mine_ref[at, :] = first
            send_ref[at, :] = second

        @pl.when(core != 0)
        def _():
            mine_ref[at, :] = second
            send_ref[at, :] = first

    put(key0, key1, 0)
    put(vals[:, :HD], vals[:, HD:], total)


def kv_project(idx, pieces, gain, wk, wv, cosine, sine):
    rows, part = pieces[0].shape
    width = wk.shape[0]
    steps = rows // KV_ROWS
    last = steps // 2 - 1
    vm = pl.BlockSpec(memory_space=pltpu.VMEM)
    top = pl.BlockSpec((KV_ROWS, part), lambda i, idx_ref: (jnp.minimum(i, last), 0))
    bottom = pl.BlockSpec((KV_ROWS, part), lambda i, idx_ref: (jnp.maximum(i - last - 1, 0), 0))
    block = lambda columns: pl.BlockSpec((KV_ROWS, columns), lambda i, idx_ref: (i, 0))
    full = pl.BlockSpec((2 * rows, HD), lambda i, idx_ref: (0, 0))
    return pl.pallas_call(
        kv_kernel,
        out_shape=(
            jax.ShapeDtypeStruct((rows, width), BF),
            jax.ShapeDtypeStruct((2 * rows, HD), BF),
            jax.ShapeDtypeStruct((2 * rows, HD), BF),
        ),
        grid_spec=pltpu.PrefetchScalarGridSpec(
            num_scalar_prefetch=1,
            grid=(steps,),
            in_specs=[block(part), top, bottom, top, bottom, top, bottom, vm, vm, vm, block(HD), block(HD)],
            out_specs=(block(width), full, full),
        ),
        compiler_params=pltpu.CompilerParams(
            vmem_limit_bytes=28 * MIB, dimension_semantics=("arbitrary",)
        ),
        cost_estimate=cost(2 * rows * width * 4 * HD, 12 * MIB),
        name="norm_keys_values",
    )(idx, *pieces, gain, wk, wv, cosine, sine)


def q_kernel(idx_ref, xn_ref, wq_ref, cos_ref, sin_ref, send_ref, mine_ref):
    j = pl.program_id(0)
    half = xn_ref.shape[0] // 2
    res = jnp.dot(xn_ref[...], wq_ref[...], preferred_element_type=F32)
    cosine, sine = cos_ref[...], sin_ref[...]
    heads = [rotate(res[:, e * HD : (e + 1) * HD], cosine, sine).astype(BF) for e in range(2)]

    def put(out_ref):
        for e in range(2):
            for t in range(2):
                begin = pl.multiple_of((t * 4 + lax.rem(j, 2) * 2 + e) * half, half)
                out_ref[pl.ds(begin, half), :] = heads[e][t * half : (t + 1) * half]

    @pl.when(j < 2)
    def _():
        put(send_ref)

    @pl.when(j >= 2)
    def _():
        put(mine_ref)


def q_project(idx, xn, wq, cosine, sine):
    rows, width = xn.shape

    def w_map(j, idx_ref):
        core = idx_ref[2]
        group = jnp.where(j < 2, 1 - core, core)
        return (0, group * 2 + lax.rem(j, 2))

    full = lambda shape: pl.BlockSpec(shape, lambda j, idx_ref: (0,) * len(shape))
    return pl.pallas_call(
        q_kernel,
        out_shape=tuple(jax.ShapeDtypeStruct((4 * rows, HD), BF) for _ in range(2)),
        grid_spec=pltpu.PrefetchScalarGridSpec(
            num_scalar_prefetch=1,
            grid=(4,),
            in_specs=[
                full((rows, width)),
                pl.BlockSpec((width, 2 * HD), w_map),
                full((rows, HD)),
                full((rows, HD)),
            ],
            out_specs=tuple(full((4 * rows, HD)) for _ in range(2)),
        ),
        compiler_params=pltpu.CompilerParams(
            vmem_limit_bytes=24 * MIB, dimension_semantics=("arbitrary",)
        ),
        cost_estimate=cost(2 * rows * width * 8 * HD, 14 * MIB),
        name="queries",
    )(idx, xn, wq, cosine, sine)


SCALE2 = HD ** (-0.5) * LOG2E
CHUNK = 256
ATTENTION_VMEM = 32 * MIB


def attention_kernel(pieces, n_kv, call, last_call, idx_ref, len_ref, *refs):
    kv_refs, refs = refs[:n_kv], refs[n_kv:]
    q_refs, refs = refs[:2], refs[2:]
    if call > 0:
        acc_in, top_in, refs = refs[0], refs[1], refs[2:]
    if call == last_call:
        o_ref, refs = refs[0], refs[1:]
    acc, top, key_ref, val_ref, q_ref, key_doc, q_doc, todo_ref, sem = refs
    z, y, core = idx_ref[0], idx_ref[1], idx_ref[2]
    rows = q_ref.shape[0]
    size = key_ref.shape[0] // 32
    group = rows // 2
    own = [(z * 4 + y) * 2 + lax.rem(core + g, 2) for g in range(2)]
    lower = jnp.minimum(own[0], own[1])
    copies = []

    def fetch(source, target):
        copy = pltpu.make_async_copy(source, target, sem.at[len(copies)])
        copy.start()
        copies.append(copy)

    for g in range(2):
        fetch(q_refs[g], q_ref.at[pl.ds(g * group, group), :])
    if call > 0:
        fetch(acc_in, acc)
        fetch(top_in, top)
    for array, row, dz, dy, dc, kind in pieces:
        block = (lax.rem(z + dz, 4) * 4 + lax.rem(y + dy, 4)) * 2 + lax.rem(core + dc, 2)
        begin = pl.multiple_of(block * size, size)
        fetch(kv_refs[array].at[pl.ds(row, size), :], (key_ref, val_ref)[kind].at[pl.ds(begin, size), :])
    if call == 0:
        top[...] = jnp.full_like(top, NEGATIVE)
        acc[...] = jnp.zeros_like(acc)

    lane = lax.broadcasted_iota(jnp.int32, (1, HD), 1)
    starts = jnp.zeros((1, HD), jnp.int32)
    ends = jnp.zeros((1, HD), jnp.int32)
    first = jnp.int32(0)
    begin = jnp.int32(0)
    for i in range(8):
        first = jnp.where(begin <= lower * size, begin, first)
        starts = jnp.where(lane == i, begin, starts)
        begin = begin + len_ref[i]
        ends = jnp.where(lane == i, begin, ends)
    lo = first // size

    def inside(begin, count):
        pos = begin + lax.broadcasted_iota(jnp.int32, (count, HD), 0)
        return (pos >= starts) & (pos < ends)

    def mark_keys(j, carry):
        span = pl.ds(pl.multiple_of(j * size, size), size)
        key_doc[span, :] = jnp.where(inside(j * size, size), 1.0, 0.0).astype(BF)
        return carry

    for g in range(2):
        for t in range(2):
            there = inside(own[g] * size + t * CHUNK, CHUNK) | (lane >= 8)
            mark = jnp.where(there, 0.0, NEGATIVE).astype(BF)
            for h in range(4):
                row = g * group + (t * 4 + h) * CHUNK
                q_doc[row : row + CHUNK, :] = mark
    ones = jnp.ones((size, HD), BF)

    def stage(j):
        away = jnp.where(
            lax.rem(j, 2) == core, lax.rem(j // 8 - z + 4, 4), lax.rem(lax.rem(j // 2, 4) - y + 4, 4)
        )
        return jnp.where(away == 0, 0, jnp.where(away == 2, 2, 1))

    def load(blocks):
        spans = [pl.ds(pl.multiple_of(j * size, size), size) for j in blocks]
        keys = [jnp.concatenate([key_ref[span, :], key_doc[span, :]], axis=1) for span in spans]
        vals = [jnp.concatenate([val_ref[span, :], ones], axis=1) for span in spans]
        if len(blocks) == 1:
            return keys[0], vals[0]
        return jnp.concatenate(keys, axis=0), jnp.concatenate(vals, axis=0)

    def scores(row, key):
        span = pl.ds(row, CHUNK)
        query = jnp.concatenate([q_ref[span, :], q_doc[span, :]], axis=1)
        return lax.dot_general(
            query, key, (((1,), (1,)), ((), ())), preferred_element_type=F32
        )

    def absorb(row, s, val):
        span = pl.ds(row, CHUNK)
        old = top[span, :]
        new = jnp.maximum(old, jnp.max(s, axis=1, keepdims=True))
        top[span, :] = new
        alpha = jnp.exp2((old - new) * SCALE2)
        p = jnp.exp2((s - new[:, :1]) * SCALE2).astype(BF)
        pv = jnp.dot(p, val, preferred_element_type=F32)
        acc[span, :HD] = acc[span, :HD] * alpha + pv[:, :HD]
        acc[span, HD:] = acc[span, HD:] * alpha + pv[:, HD:]

    def whole(blocks):
        key, val = load(blocks)
        following = scores(0, key)
        for row in range(0, rows, CHUNK):
            s = following
            if row + CHUNK < rows:
                following = scores(row + CHUNK, key)
            absorb(row, s, val)

    def within(g, blocks):
        key, val = load(blocks)
        before = size * (len(blocks) - 1)
        order = [(t, h) for t in range(2) for h in range(4)]

        def row(t, h):
            return pl.multiple_of(g * group + (t * 4 + h) * CHUNK, CHUNK)

        def part(n):
            return scores(row(*order[n]), key[: before + (order[n][0] + 1) * CHUNK])

        square = (CHUNK, CHUNK)
        causal = lax.broadcasted_iota(jnp.int32, square, 0) >= lax.broadcasted_iota(jnp.int32, square, 1)
        following = part(0)
        for n, (t, h) in enumerate(order):
            s = following
            if n + 1 < len(order):
                following = part(n + 1)
            edge = before + t * CHUNK
            corner = jnp.where(causal, s[:, edge:], NEGATIVE)
            s = corner if edge == 0 else jnp.concatenate([s[:, :edge], corner], axis=1)
            absorb(row(t, h), s, val[: edge + CHUNK])

    def collect(j, count):
        take = stage(j) == call

        @pl.when(take)
        def _():
            todo_ref[count] = j
            mark_keys(j, 0)

        return count + take.astype(jnp.int32)

    count = lax.fori_loop(lo, lower, collect, jnp.int32(0))
    if call == 0:
        lax.fori_loop(lower, lower + 2, mark_keys, 0)
    for copy in copies:
        copy.wait()

    def pair(k, carry):
        whole([todo_ref[2 * k], todo_ref[2 * k + 1]])
        return carry

    lax.fori_loop(0, count // 2, pair, 0)

    @pl.when(lax.rem(count, 2) == 1)
    def _():
        whole([todo_ref[count - 1]])

    if call == 0:
        low_group = (own[0] != lower).astype(jnp.int32)
        within(low_group, [lower])
        within(1 - low_group, [lower, lower + 1])
    if call == last_call:
        o_ref[...] = (acc[:, :HD] / acc[:, HD:]).astype(BF)


def attention(idx, doc_lengths, kv, queries, state, call, last_call, total_tokens):
    rows = 2 * queries[0].shape[0]
    smem = pl.BlockSpec(memory_space=pltpu.SMEM)
    hbm = pl.BlockSpec(memory_space=pl.ANY)
    vm = pl.BlockSpec(memory_space=pltpu.VMEM)
    arrays, pieces = kv
    last = call == last_call
    wide, narrow = (rows, 2 * HD), (rows, HD)
    states = (jax.ShapeDtypeStruct(wide, F32), jax.ShapeDtypeStruct(narrow, F32))
    return pl.pallas_call(
        functools.partial(attention_kernel, pieces, len(arrays), call, last_call),
        out_shape=jax.ShapeDtypeStruct((rows, HD), BF) if last else states,
        in_specs=[smem, smem] + [hbm] * (len(arrays) + 2 + len(state)),
        out_specs=vm if last else (vm, vm),
        scratch_shapes=[
            *([pltpu.VMEM(wide, F32), pltpu.VMEM(narrow, F32)] if last else []),
            pltpu.VMEM((total_tokens, HD), BF),
            pltpu.VMEM((total_tokens, HD), BF),
            pltpu.VMEM((rows, HD), BF),
            pltpu.VMEM((total_tokens, HD), BF),
            pltpu.VMEM((rows, HD), BF),
            pltpu.SMEM((32,), jnp.int32),
            pltpu.SemaphoreType.DMA((len(pieces) + 4,)),
        ],
        compiler_params=pltpu.CompilerParams(vmem_limit_bytes=ATTENTION_VMEM),
        cost_estimate=cost(8e6 * 512, 10 * MIB, 8e6),
        name="attention",
    )(idx, doc_lengths, *arrays, *queries, *state)


def out_kernel(dests, split, add, idx_ref, w_ref, mine_ref, other_ref, *refs):
    added = refs[0] if add else None
    out_ref, scr = refs[-2:]
    core = idx_ref[2]
    j = pl.program_id(0)
    rows = scr.shape[0]
    half = rows // 2

    @pl.when(j == 0)
    def _():
        for g, ref in enumerate((mine_ref, other_ref)):
            group = lax.rem(core + g, 2) * (4 * HD)
            for h in range(4):
                column = pl.ds(pl.multiple_of(group + h * HD, HD), HD)
                for t in range(2):
                    at = (t * 4 + h) * half
                    scr[t * half : (t + 1) * half, column] = ref[at : at + half, :]

    if split is None:
        left = scr[...]
    else:
        number = j // (pl.num_programs(0) // 2)
        begin = (number + split - 2 * number * split) * half
        left = scr[pl.ds(pl.multiple_of(begin, half), half), :]
    res = jnp.dot(left, w_ref[...], preferred_element_type=F32)
    if add:
        res = res + added[...].astype(F32)
    out_ref[...] = res.astype(out_ref.dtype)


def out_project(idx, w, mine, other, dests, dtype, split=None, added=None):
    rows = mine.shape[0] // 4
    out_rows = rows if split is None else rows // 2
    feat, model = w.shape
    width = model // 4
    block = 512
    per = width // block

    def w_map(j, idx_ref):
        shift = jnp.int32(dests[0])
        for n, s in enumerate(dests):
            shift = jnp.where(j >= n * per, s, shift)
        return (0, lax.rem(idx_ref[3] + shift, 4) * per + lax.rem(j, per))

    columns = pl.BlockSpec((out_rows, block), lambda j, idx_ref: (0, j))
    return pl.pallas_call(
        functools.partial(out_kernel, dests, split, added is not None),
        out_shape=jax.ShapeDtypeStruct((out_rows, width * len(dests)), dtype),
        grid_spec=pltpu.PrefetchScalarGridSpec(
            num_scalar_prefetch=1,
            grid=(per * len(dests),),
            in_specs=[pl.BlockSpec((feat, block), w_map)]
            + [pl.BlockSpec((4 * rows, HD), lambda j, idx_ref: (0, 0))] * 2
            + ([columns] if added is not None else []),
            out_specs=columns,
            scratch_shapes=[pltpu.VMEM((rows, feat), BF)],
        ),
        compiler_params=pltpu.CompilerParams(
            vmem_limit_bytes=20 * MIB, dimension_semantics=("arbitrary",)
        ),
        cost_estimate=cost(
            2 * out_rows * feat * width * len(dests), (2 * feat + 4 * out_rows) * width * len(dests)
        ),
        name="output_projection",
    )(idx, w, mine, other, *(() if added is None else (added,)))


def sum_kernel(kept_ref, up_top, up_bottom, down_top, down_bottom, out_ref):
    half = up_top.shape[0]
    for n, (up, down) in enumerate(((up_top, down_top), (up_bottom, down_bottom))):
        span = slice(n * half, (n + 1) * half)
        out_ref[span, :] = (
            kept_ref[span, :] + up[...].astype(F32) + down[...].astype(F32)
        ).astype(BF)


def exchange_near(mine, other, meanwhile):
    rows = mine.shape[0] // 2
    a_up, a_down = move_y(mine, 1), move_y(mine, -1)
    b_up, b_down_values = move_z(other, 1), move_z(other[rows:], -1)
    (a_up, a_down, b_up, b_down_values), meanwhile = lax.optimization_barrier(
        ((a_up, a_down, b_up, b_down_values), meanwhile)
    )
    b_far = [move_z(b_up[:rows], 1), move_z(b_down_values, -1)]
    a_far = [move_y(a_up[:rows], 1), move_y(a_down[rows:], -1)]
    a_line = jnp.concatenate([mine, a_up, a_down, *a_far], axis=0)
    b_line = jnp.concatenate([other, b_up, *b_far], axis=0)
    return a_line, b_line, meanwhile


def move_y(value, shift):
    return dp_send(value, dy=shift)


def move_z(value, shift):
    return dp_send(value, dz=shift)


def exchange(a_line, b_line, rows, attend):
    block = 2 * rows
    stages = [([], []) for _ in range(3)]

    def keep(n, array, places, dc):
        arrays, pieces = stages[n]
        for i, (dz, dy) in enumerate(places):
            for kind in range(2):
                pieces.append((len(arrays), i * block + kind * rows, dz % 4, dy % 4, dc, kind))
        arrays.append(array)

    from_left, from_right = move_y(b_line, 1), move_y(b_line, -1)
    from_below, from_above = move_z(a_line, 1), move_z(a_line[2 * block :], -1)
    keep(0, a_line, [(0, 0), (0, -1), (0, 1), (0, 2)], 0)
    keep(0, b_line, [(0, 0), (-1, 0), (-2, 0)], 1)
    state = attend(stages[0], (), 0)
    state, from_left, from_right, from_below, from_above = lax.optimization_barrier(
        (state, from_left, from_right, from_below, from_above)
    )
    left_far = move_y(from_left[: block + rows], 1)
    right_far = move_y(from_right[block + rows :], -1)
    far_below, far_above = move_z(from_below[: 2 * block], 1), move_z(from_above, -1)

    keep(1, from_below, [(-1, 0), (-1, -1), (-1, 1), (-1, 2)], 0)
    keep(1, from_left, [(0, -1), (-1, -1), (-2, -1)], 1)
    keep(1, from_right, [(0, 1), (-1, 1), (-2, 1)], 1)
    keep(2, far_below, [(2, 0), (2, -1)], 0)
    keep(2, far_above, [(2, 1), (2, 2)], 0)
    arrays, pieces = stages[2]
    for place, (array, row, kind) in (
        (0, (left_far, 0, 0)),
        (0, (left_far, rows, 1)),
        (-1, (left_far, block, 0)),
        (-1, (right_far, 0, 1)),
        (-2, (right_far, rows, 0)),
        (-2, (right_far, block, 1)),
    ):
        index = len(arrays) + (array is right_far)
        pieces.append((index, row, place % 4, 2, 1, kind))
    arrays.extend([left_far, right_far])
    state = attend(stages[1], state, 1)
    return attend(stages[2], state, 2)


def gather_x(tokens):
    half = tokens.shape[0] // 2
    top, bottom = tokens[:half], tokens[half:]
    below_top, above_bottom = x_send(top, 1), x_send(bottom, -1)
    below_top, above_bottom, top, bottom = lax.optimization_barrier(
        (below_top, above_bottom, top, bottom)
    )
    far_top, far_bottom = x_send(below_top, 1), x_send(above_bottom, -1)
    below_bottom, above_top = x_send(bottom, 1), x_send(top, -1)
    return below_top, below_bottom, above_top, above_bottom, far_top, far_bottom


def body(tokens, norm_gain, w_query, key_weight, value_weight, w_output, doc_lengths):
    rows = tokens.shape[0]
    dp = lax.axis_index("dp").astype(jnp.int32)
    x = lax.axis_index("tensor").astype(jnp.int32)
    idx = jnp.stack([dp // 8, (dp // 2) % 4, dp % 2, x])
    positions = dp * rows + jnp.arange(rows, dtype=jnp.int32)
    cosine, sine = rope_tables(positions, doc_lengths)

    gain = norm_gain[None, :]
    pieces = (tokens, *gather_x(tokens))
    xn, mine, send = kv_project(idx, pieces, gain, key_weight, value_weight, cosine, sine)
    other = dp_send(send, dc=1)
    xn, other = lax.optimization_barrier((xn, other))
    queries = q_project(idx, xn, w_query, cosine, sine)
    a_line, b_line, (q_send, q_mine) = exchange_near(mine, other, queries)
    a_line, b_line = lax.optimization_barrier((a_line, b_line))
    q_other = dp_send(q_send, dc=1)
    queries = (q_mine, q_other)
    total = rows * 32

    def attend(kv, state, call):
        return attention(idx, doc_lengths, kv, queries, state, call, 2, total)

    mixed = exchange(a_line, b_line, rows, attend)
    group = mixed.shape[0] // 2
    return reduce_out(idx, w_output, mixed[:group], dp_send(mixed[group:], dc=1))


def reduce_out(idx, w_output, mixed, other):
    far = out_project(idx, w_output, mixed, other, (2,), BF)
    half, width = far.shape[0] // 2, far.shape[1]
    far_up, far_down = x_send(far[:half], 1), x_send(far[half:], -1)
    ready = out_project(idx, w_output, mixed, other, (1, 3), BF, split=1)
    up_bottom, down_top = x_send(ready[:, :width], 1), x_send(ready[:, width:], -1)
    kept = out_project(idx, w_output, mixed, other, (0,), F32)
    kept, far_up, far_down = lax.optimization_barrier((kept, far_up, far_down))
    added = jnp.concatenate([far_up, far_down], axis=1)
    sums = out_project(idx, w_output, mixed, other, (1, 3), BF, split=0, added=added)
    up_top, down_bottom = x_send(sums[:, :width], 1), x_send(sums[:, width:], -1)
    vm = pl.BlockSpec(memory_space=pltpu.VMEM)
    return pl.pallas_call(
        sum_kernel,
        out_shape=jax.ShapeDtypeStruct((2 * half, width), BF),
        in_specs=[vm] * 5,
        out_specs=vm,
        compiler_params=pltpu.CompilerParams(vmem_limit_bytes=16 * MIB),
        name="sum",
    )(kept, up_top, up_bottom, down_top, down_bottom)


def solution(mesh):
    return jax.shard_map(
        body,
        mesh=mesh,
        in_specs=(
            P("dp", "tensor"),
            P(),
            P(None, "tensor"),
            P(None, "tensor"),
            P(None, "tensor"),
            P("tensor", None),
            P(),
        ),
        out_specs=P("dp", "tensor"),
        check_vma=False,
    )
```

```python
import functools

import jax
import jax.numpy as jnp
from jax import lax
from jax.experimental import pallas as pl
from jax.experimental.pallas import tpu as pltpu
from jax.sharding import PartitionSpec as P

HD = 128
EPSILON = 1e-05
THETA = 500000.0
NEGATIVE = -1e30
DIMS = (4, 4, 2)
BF = jnp.bfloat16
F32 = jnp.float32
MIB = 1 << 20
LOG2E = 1.4426950408889634


def dp_perm(dz, dy, dc):
    nz, ny, nc = DIMS
    pairs = []
    for z in range(nz):
        for y in range(ny):
            for c in range(nc):
                src = (z * ny + y) * nc + c
                dst = (((z + dz) % nz) * ny + (y + dy) % ny) * nc + (c + dc) % nc
                pairs.append((src, dst))
    return pairs


def dp_send(value, dz=0, dy=0, dc=0):
    return lax.ppermute(value, "dp", dp_perm(dz, dy, dc))


def x_send(value, shift):
    return lax.ppermute(value, "tensor", [(i, (i + shift) % 4) for i in range(4)])


def cost(flops, bytes_accessed, transcendentals=0):
    return pl.CostEstimate(
        flops=int(flops), bytes_accessed=int(bytes_accessed), transcendentals=int(transcendentals)
    )


def rope_tables(positions, doc_lengths):
    doc_starts = jnp.cumsum(doc_lengths) - doc_lengths
    doc_first = jnp.max(
        jnp.where(doc_starts[None, :] <= positions[:, None], doc_starts[None, :], 0), axis=1
    )
    half_size = HD // 2
    exponents = jnp.arange(half_size, dtype=F32) * (2.0 / HD)
    frequency = jnp.exp(-exponents * jnp.log(F32(THETA)))
    angles = (positions - doc_first).astype(F32)[:, None] * frequency[None, :]
    cosine, sine = jnp.cos(angles), jnp.sin(angles)
    return (
        jnp.concatenate([cosine, cosine], axis=1),
        jnp.concatenate([-sine, sine], axis=1),
    )


def rotate(value, cosine, sine):
    return value * cosine + pltpu.roll(value, HD // 2, 1) * sine


KV_ROWS = 128


def norm_rows(idx_ref, parts, gain_ref, xn_ref):
    rows, width = parts[0][0].shape
    x = idx_ref[3]
    step = 64

    def advance(i, carry):
        span = pl.ds(pl.multiple_of(i * step, step), step)
        square = jnp.zeros((step, HD), F32)
        for ref, _ in parts:
            for column in range(0, width, HD):
                f = ref[span, column : column + HD].astype(F32)
                square = square + f * f
        mean = jnp.sum(square, axis=1, keepdims=True) * (1.0 / (4 * width))
        inv = jnp.broadcast_to(lax.rsqrt(mean + EPSILON), (step, HD))
        for ref, shift in parts:
            begin = lax.rem(x + shift, 4) * width
            for column in range(0, width, HD):
                at = pl.ds(pl.multiple_of(begin + column, HD), HD)
                f = ref[span, column : column + HD].astype(F32)
                xn_ref[span, at] = (f * inv * gain_ref[:, at].astype(F32)).astype(BF)
        return carry

    lax.fori_loop(0, rows // step, advance, 0)


def kv_kernel(idx_ref, *refs):
    (t_ref, *halves), refs = refs[:7], refs[7:]
    gain_ref, wk_ref, wv_ref, cos_ref, sin_ref, xn_ref, mine_ref, send_ref = refs
    i = pl.program_id(0)
    steps = pl.num_programs(0)
    rows = xn_ref.shape[0]
    total = mine_ref.shape[0] // 2
    core = idx_ref[2]

    for n in range(2):

        @pl.when((i >= steps // 2) == (n == 1))
        def _(n=n):
            below, above, far = halves[n], halves[2 + n], halves[4 + n]
            parts = [(t_ref, 0), (below, 3), (above, 1), (far, 2)]
            norm_rows(idx_ref, parts, gain_ref, xn_ref)

    normed = xn_ref[...]
    keys = jnp.dot(normed, wk_ref[...], preferred_element_type=F32)
    cosine, sine = cos_ref[...], sin_ref[...]
    key0 = rotate(keys[:, :HD], cosine, sine).astype(BF)
    key1 = rotate(keys[:, HD:], cosine, sine).astype(BF)
    vals = jnp.dot(normed, wv_ref[...], preferred_element_type=F32).astype(BF)

    def put(first, second, offset):
        at = pl.ds(pl.multiple_of(offset + i * rows, rows), rows)

        @pl.when(core == 0)
        def _():
            mine_ref[at, :] = first
            send_ref[at, :] = second

        @pl.when(core != 0)
        def _():
            mine_ref[at, :] = second
            send_ref[at, :] = first

    put(key0, key1, 0)
    put(vals[:, :HD], vals[:, HD:], total)


def kv_project(idx, pieces, gain, wk, wv, cosine, sine):
    rows, part = pieces[0].shape
    width = wk.shape[0]
    steps = rows // KV_ROWS
    last = steps // 2 - 1
    vm = pl.BlockSpec(memory_space=pltpu.VMEM)
    top = pl.BlockSpec((KV_ROWS, part), lambda i, idx_ref: (jnp.minimum(i, last), 0))
    bottom = pl.BlockSpec((KV_ROWS, part), lambda i, idx_ref: (jnp.maximum(i - last - 1, 0), 0))
    block = lambda columns: pl.BlockSpec((KV_ROWS, columns), lambda i, idx_ref: (i, 0))
    full = pl.BlockSpec((2 * rows, HD), lambda i, idx_ref: (0, 0))
    return pl.pallas_call(
        kv_kernel,
        out_shape=(
            jax.ShapeDtypeStruct((rows, width), BF),
            jax.ShapeDtypeStruct((2 * rows, HD), BF),
            jax.ShapeDtypeStruct((2 * rows, HD), BF),
        ),
        grid_spec=pltpu.PrefetchScalarGridSpec(
            num_scalar_prefetch=1,
            grid=(steps,),
            in_specs=[block(part), top, bottom, top, bottom, top, bottom, vm, vm, vm, block(HD), block(HD)],
            out_specs=(block(width), full, full),
        ),
        compiler_params=pltpu.CompilerParams(
            vmem_limit_bytes=16 * MIB, dimension_semantics=("arbitrary",)
        ),
        cost_estimate=cost(2 * rows * width * 4 * HD, 12 * MIB),
        name="norm_keys_values",
    )(idx, *pieces, gain, wk, wv, cosine, sine)


def q_kernel(idx_ref, xn_ref, wq_ref, cos_ref, sin_ref, send_ref, mine_ref):
    j = pl.program_id(0)
    half = xn_ref.shape[0] // 2
    res = jnp.dot(xn_ref[...], wq_ref[...], preferred_element_type=F32)
    cosine, sine = cos_ref[...], sin_ref[...]
    heads = [rotate(res[:, e * HD : (e + 1) * HD], cosine, sine).astype(BF) for e in range(2)]

    def put(out_ref):
        for e in range(2):
            for t in range(2):
                begin = pl.multiple_of((t * 4 + lax.rem(j, 2) * 2 + e) * half, half)
                out_ref[pl.ds(begin, half), :] = heads[e][t * half : (t + 1) * half]

    @pl.when(j < 2)
    def _():
        put(send_ref)

    @pl.when(j >= 2)
    def _():
        put(mine_ref)


def q_project(idx, xn, wq, cosine, sine):
    rows, width = xn.shape

    def w_map(j, idx_ref):
        core = idx_ref[2]
        group = jnp.where(j < 2, 1 - core, core)
        return (0, group * 2 + lax.rem(j, 2))

    full = lambda shape: pl.BlockSpec(shape, lambda j, idx_ref: (0,) * len(shape))
    return pl.pallas_call(
        q_kernel,
        out_shape=tuple(jax.ShapeDtypeStruct((4 * rows, HD), BF) for _ in range(2)),
        grid_spec=pltpu.PrefetchScalarGridSpec(
            num_scalar_prefetch=1,
            grid=(4,),
            in_specs=[
                full((rows, width)),
                pl.BlockSpec((width, 2 * HD), w_map),
                full((rows, HD)),
                full((rows, HD)),
            ],
            out_specs=tuple(full((4 * rows, HD)) for _ in range(2)),
        ),
        compiler_params=pltpu.CompilerParams(
            vmem_limit_bytes=24 * MIB, dimension_semantics=("arbitrary",)
        ),
        cost_estimate=cost(2 * rows * width * 8 * HD, 14 * MIB),
        name="queries",
    )(idx, xn, wq, cosine, sine)


SCALE2 = HD ** (-0.5) * LOG2E
CHUNK = 256
ATTENTION_VMEM = 32 * MIB


def attention_kernel(pieces, n_kv, call, last_call, idx_ref, len_ref, *refs):
    kv_refs, refs = refs[:n_kv], refs[n_kv:]
    q_refs, refs = refs[:2], refs[2:]
    if call > 0:
        acc_in, top_in, refs = refs[0], refs[1], refs[2:]
    if call == last_call:
        o_ref, refs = refs[0], refs[1:]
    acc, top, key_ref, val_ref, q_ref, key_doc, q_doc, todo_ref, sem = refs
    z, y, core = idx_ref[0], idx_ref[1], idx_ref[2]
    rows = q_ref.shape[0]
    size = key_ref.shape[0] // 32
    group = rows // 2
    own = [(z * 4 + y) * 2 + lax.rem(core + g, 2) for g in range(2)]
    lower = jnp.minimum(own[0], own[1])
    copies = []

    def fetch(source, target):
        copy = pltpu.make_async_copy(source, target, sem.at[len(copies)])
        copy.start()
        copies.append(copy)

    for g in range(2):
        fetch(q_refs[g], q_ref.at[pl.ds(g * group, group), :])
    if call > 0:
        fetch(acc_in, acc)
        fetch(top_in, top)
    for array, row, dz, dy, dc, kind in pieces:
        block = (lax.rem(z + dz, 4) * 4 + lax.rem(y + dy, 4)) * 2 + lax.rem(core + dc, 2)
        begin = pl.multiple_of(block * size, size)
        fetch(kv_refs[array].at[pl.ds(row, size), :], (key_ref, val_ref)[kind].at[pl.ds(begin, size), :])
    if call == 0:
        top[...] = jnp.full_like(top, NEGATIVE)
        acc[...] = jnp.zeros_like(acc)

    lane = lax.broadcasted_iota(jnp.int32, (1, HD), 1)
    starts = jnp.zeros((1, HD), jnp.int32)
    ends = jnp.zeros((1, HD), jnp.int32)
    first = jnp.int32(0)
    begin = jnp.int32(0)
    for i in range(8):
        first = jnp.where(begin <= lower * size, begin, first)
        starts = jnp.where(lane == i, begin, starts)
        begin = begin + len_ref[i]
        ends = jnp.where(lane == i, begin, ends)
    lo = first // size

    def inside(begin, count):
        pos = begin + lax.broadcasted_iota(jnp.int32, (count, HD), 0)
        return (pos >= starts) & (pos < ends)

    def mark_keys(j, carry):
        span = pl.ds(pl.multiple_of(j * size, size), size)
        key_doc[span, :] = jnp.where(inside(j * size, size), 1.0, 0.0).astype(BF)
        return carry

    for g in range(2):
        for t in range(2):
            there = inside(own[g] * size + t * CHUNK, CHUNK) | (lane >= 8)
            mark = jnp.where(there, 0.0, NEGATIVE).astype(BF)
            for h in range(4):
                row = g * group + (t * 4 + h) * CHUNK
                q_doc[row : row + CHUNK, :] = mark
    ones = jnp.ones((size, HD), BF)

    def stage(j):
        away = jnp.where(
            lax.rem(j, 2) == core, lax.rem(j // 8 - z + 4, 4), lax.rem(lax.rem(j // 2, 4) - y + 4, 4)
        )
        return jnp.where(away == 0, 0, jnp.where(away == 2, 2, 1))

    def load(blocks):
        spans = [pl.ds(pl.multiple_of(j * size, size), size) for j in blocks]
        keys = [jnp.concatenate([key_ref[span, :], key_doc[span, :]], axis=1) for span in spans]
        vals = [jnp.concatenate([val_ref[span, :], ones], axis=1) for span in spans]
        if len(blocks) == 1:
            return keys[0], vals[0]
        return jnp.concatenate(keys, axis=0), jnp.concatenate(vals, axis=0)

    def scores(row, key):
        span = pl.ds(row, CHUNK)
        query = jnp.concatenate([q_ref[span, :], q_doc[span, :]], axis=1)
        return lax.dot_general(
            query, key, (((1,), (1,)), ((), ())), preferred_element_type=F32
        )

    def absorb(row, s, val):
        span = pl.ds(row, CHUNK)
        old = top[span, :]
        new = jnp.maximum(old, jnp.max(s, axis=1, keepdims=True))
        top[span, :] = new
        alpha = jnp.exp2((old - new) * SCALE2)
        p = jnp.exp2((s - new[:, :1]) * SCALE2).astype(BF)
        pv = jnp.dot(p, val, preferred_element_type=F32)
        acc[span, :HD] = acc[span, :HD] * alpha + pv[:, :HD]
        acc[span, HD:] = acc[span, HD:] * alpha + pv[:, HD:]

    def whole(blocks):
        key, val = load(blocks)
        following = scores(0, key)
        for row in range(0, rows, CHUNK):
            s = following
            if row + CHUNK < rows:
                following = scores(row + CHUNK, key)
            absorb(row, s, val)

    def within(g, blocks):
        key, val = load(blocks)
        before = size * (len(blocks) - 1)
        order = [(t, h) for t in range(2) for h in range(4)]

        def row(t, h):
            return pl.multiple_of(g * group + (t * 4 + h) * CHUNK, CHUNK)

        def part(n):
            return scores(row(*order[n]), key[: before + (order[n][0] + 1) * CHUNK])

        square = (CHUNK, CHUNK)
        causal = lax.broadcasted_iota(jnp.int32, square, 0) >= lax.broadcasted_iota(jnp.int32, square, 1)
        following = part(0)
        for n, (t, h) in enumerate(order):
            s = following
            if n + 1 < len(order):
                following = part(n + 1)
            edge = before + t * CHUNK
            corner = jnp.where(causal, s[:, edge:], NEGATIVE)
            s = corner if edge == 0 else jnp.concatenate([s[:, :edge], corner], axis=1)
            absorb(row(t, h), s, val[: edge + CHUNK])

    def collect(j, count):
        take = stage(j) == call

        @pl.when(take)
        def _():
            todo_ref[count] = j
            mark_keys(j, 0)

        return count + take.astype(jnp.int32)

    count = lax.fori_loop(lo, lower, collect, jnp.int32(0))
    if call == 0:
        lax.fori_loop(lower, lower + 2, mark_keys, 0)
    for copy in copies:
        copy.wait()

    def pair(k, carry):
        whole([todo_ref[2 * k], todo_ref[2 * k + 1]])
        return carry

    lax.fori_loop(0, count // 2, pair, 0)

    @pl.when(lax.rem(count, 2) == 1)
    def _():
        whole([todo_ref[count - 1]])

    if call == 0:
        low_group = (own[0] != lower).astype(jnp.int32)
        within(low_group, [lower])
        within(1 - low_group, [lower, lower + 1])
    if call == last_call:
        o_ref[...] = (acc[:, :HD] / acc[:, HD:]).astype(BF)


def attention(idx, doc_lengths, kv, queries, state, call, last_call, total_tokens):
    rows = 2 * queries[0].shape[0]
    smem = pl.BlockSpec(memory_space=pltpu.SMEM)
    hbm = pl.BlockSpec(memory_space=pl.ANY)
    vm = pl.BlockSpec(memory_space=pltpu.VMEM)
    arrays, pieces = kv
    last = call == last_call
    wide, narrow = (rows, 2 * HD), (rows, HD)
    states = (jax.ShapeDtypeStruct(wide, F32), jax.ShapeDtypeStruct(narrow, F32))
    return pl.pallas_call(
        functools.partial(attention_kernel, pieces, len(arrays), call, last_call),
        out_shape=jax.ShapeDtypeStruct((rows, HD), BF) if last else states,
        in_specs=[smem, smem] + [hbm] * (len(arrays) + 2 + len(state)),
        out_specs=vm if last else (vm, vm),
        scratch_shapes=[
            *([pltpu.VMEM(wide, F32), pltpu.VMEM(narrow, F32)] if last else []),
            pltpu.VMEM((total_tokens, HD), BF),
            pltpu.VMEM((total_tokens, HD), BF),
            pltpu.VMEM((rows, HD), BF),
            pltpu.VMEM((total_tokens, HD), BF),
            pltpu.VMEM((rows, HD), BF),
            pltpu.SMEM((32,), jnp.int32),
            pltpu.SemaphoreType.DMA((len(pieces) + 4,)),
        ],
        compiler_params=pltpu.CompilerParams(vmem_limit_bytes=ATTENTION_VMEM),
        cost_estimate=cost(8e6 * 512, 10 * MIB, 8e6),
        name="attention",
    )(idx, doc_lengths, *arrays, *queries, *state)


def out_kernel(dests, split, add, idx_ref, w_ref, mine_ref, other_ref, *refs):
    added = refs[0] if add else None
    out_ref, scr = refs[-2:]
    core = idx_ref[2]
    j = pl.program_id(0)
    rows = scr.shape[0]
    half = rows // 2

    @pl.when(j == 0)
    def _():
        for g, ref in enumerate((mine_ref, other_ref)):
            group = lax.rem(core + g, 2) * (4 * HD)
            for h in range(4):
                column = pl.ds(pl.multiple_of(group + h * HD, HD), HD)
                for t in range(2):
                    at = (t * 4 + h) * half
                    scr[t * half : (t + 1) * half, column] = ref[at : at + half, :]

    if split is None:
        left = scr[...]
    else:
        number = j // (pl.num_programs(0) // 2)
        begin = (number + split - 2 * number * split) * half
        left = scr[pl.ds(pl.multiple_of(begin, half), half), :]
    res = jnp.dot(left, w_ref[...], preferred_element_type=F32)
    if add:
        res = res + added[...].astype(F32)
    out_ref[...] = res.astype(out_ref.dtype)


def out_project(idx, w, mine, other, dests, dtype, split=None, added=None):
    rows = mine.shape[0] // 4
    out_rows = rows if split is None else rows // 2
    feat, model = w.shape
    width = model // 4
    block = 512
    per = width // block

    def w_map(j, idx_ref):
        shift = jnp.int32(dests[0])
        for n, s in enumerate(dests):
            shift = jnp.where(j >= n * per, s, shift)
        return (0, lax.rem(idx_ref[3] + shift, 4) * per + lax.rem(j, per))

    columns = pl.BlockSpec((out_rows, block), lambda j, idx_ref: (0, j))
    return pl.pallas_call(
        functools.partial(out_kernel, dests, split, added is not None),
        out_shape=jax.ShapeDtypeStruct((out_rows, width * len(dests)), dtype),
        grid_spec=pltpu.PrefetchScalarGridSpec(
            num_scalar_prefetch=1,
            grid=(per * len(dests),),
            in_specs=[pl.BlockSpec((feat, block), w_map)]
            + [pl.BlockSpec((4 * rows, HD), lambda j, idx_ref: (0, 0))] * 2
            + ([columns] if added is not None else []),
            out_specs=columns,
            scratch_shapes=[pltpu.VMEM((rows, feat), BF)],
        ),
        compiler_params=pltpu.CompilerParams(
            vmem_limit_bytes=20 * MIB, dimension_semantics=("arbitrary",)
        ),
        cost_estimate=cost(
            2 * out_rows * feat * width * len(dests), (2 * feat + 4 * out_rows) * width * len(dests)
        ),
        name="output_projection",
    )(idx, w, mine, other, *(() if added is None else (added,)))


def sum_kernel(kept_ref, up_top, up_bottom, down_top, down_bottom, out_ref):
    half = up_top.shape[0]
    for n, (up, down) in enumerate(((up_top, down_top), (up_bottom, down_bottom))):
        span = slice(n * half, (n + 1) * half)
        out_ref[span, :] = (
            kept_ref[span, :] + up[...].astype(F32) + down[...].astype(F32)
        ).astype(BF)


def exchange_near(mine, other, meanwhile):
    a_up, a_down, a_far = move_y(mine, 1), move_y(mine, -1), move_y(mine, 2)
    b_up, b_far = move_z(other, 1), move_z(other, 2)
    (a_up, a_down, a_far, b_up, b_far), meanwhile = lax.optimization_barrier(
        ((a_up, a_down, a_far, b_up, b_far), meanwhile)
    )
    a_line = jnp.concatenate([mine, a_up, a_down, a_far], axis=0)
    b_line = jnp.concatenate([other, b_up, b_far], axis=0)
    return a_line, b_line, meanwhile


def move_y(value, shift):
    return dp_send(value, dy=shift)


def move_z(value, shift):
    return dp_send(value, dz=shift)


def exchange(a_line, b_line, rows, attend):
    block = 2 * rows
    stages = [([], []) for _ in range(3)]

    def keep(n, array, places, dc):
        arrays, pieces = stages[n]
        for i, (dz, dy) in enumerate(places):
            for kind in range(2):
                pieces.append((len(arrays), i * block + kind * rows, dz % 4, dy % 4, dc, kind))
        arrays.append(array)

    from_left, from_right = move_y(b_line, 1), move_y(b_line, -1)
    from_below, from_above = move_z(a_line, 1), move_z(a_line[2 * block :], -1)
    keep(0, a_line, [(0, 0), (0, -1), (0, 1), (0, 2)], 0)
    keep(0, b_line, [(0, 0), (-1, 0), (-2, 0)], 1)
    state = attend(stages[0], (), 0)
    state, from_left, from_right, from_below, from_above = lax.optimization_barrier(
        (state, from_left, from_right, from_below, from_above)
    )
    left_far = move_y(from_left[: block + rows], 1)
    right_far = move_y(from_right[block + rows :], -1)
    far_below, far_above = move_z(from_below[: 2 * block], 1), move_z(from_above, -1)

    keep(1, from_below, [(-1, 0), (-1, -1), (-1, 1), (-1, 2)], 0)
    keep(1, from_left, [(0, -1), (-1, -1), (-2, -1)], 1)
    keep(1, from_right, [(0, 1), (-1, 1), (-2, 1)], 1)
    keep(2, far_below, [(2, 0), (2, -1)], 0)
    keep(2, far_above, [(2, 1), (2, 2)], 0)
    arrays, pieces = stages[2]
    for place, (array, row, kind) in (
        (0, (left_far, 0, 0)),
        (0, (left_far, rows, 1)),
        (-1, (left_far, block, 0)),
        (-1, (right_far, 0, 1)),
        (-2, (right_far, rows, 0)),
        (-2, (right_far, block, 1)),
    ):
        index = len(arrays) + (array is right_far)
        pieces.append((index, row, place % 4, 2, 1, kind))
    arrays.extend([left_far, right_far])
    state = attend(stages[1], state, 1)
    return attend(stages[2], state, 2)


def gather_x(tokens):
    half = tokens.shape[0] // 2
    top, bottom = tokens[:half], tokens[half:]
    below_top, above_bottom = x_send(top, 1), x_send(bottom, -1)
    below_top, above_bottom, top, bottom = lax.optimization_barrier(
        (below_top, above_bottom, top, bottom)
    )
    far_top, far_bottom = x_send(below_top, 1), x_send(above_bottom, -1)
    below_bottom, above_top = x_send(bottom, 1), x_send(top, -1)
    return below_top, below_bottom, above_top, above_bottom, far_top, far_bottom


def body(tokens, norm_gain, w_query, key_weight, value_weight, w_output, doc_lengths):
    rows = tokens.shape[0]
    dp = lax.axis_index("dp").astype(jnp.int32)
    x = lax.axis_index("tensor").astype(jnp.int32)
    idx = jnp.stack([dp // 8, (dp // 2) % 4, dp % 2, x])
    positions = dp * rows + jnp.arange(rows, dtype=jnp.int32)
    cosine, sine = rope_tables(positions, doc_lengths)

    gain = norm_gain[None, :]
    pieces = (tokens, *gather_x(tokens))
    xn, mine, send = kv_project(idx, pieces, gain, key_weight, value_weight, cosine, sine)
    other = dp_send(send, dc=1)
    xn, other = lax.optimization_barrier((xn, other))
    queries = q_project(idx, xn, w_query, cosine, sine)
    a_line, b_line, (q_send, q_mine) = exchange_near(mine, other, queries)
    a_line, b_line = lax.optimization_barrier((a_line, b_line))
    q_other = dp_send(q_send, dc=1)
    queries = (q_mine, q_other)
    total = rows * 32

    def attend(kv, state, call):
        return attention(idx, doc_lengths, kv, queries, state, call, 2, total)

    mixed = exchange(a_line, b_line, rows, attend)
    group = mixed.shape[0] // 2
    return reduce_out(idx, w_output, mixed[:group], dp_send(mixed[group:], dc=1))


def reduce_out(idx, w_output, mixed, other):
    far = out_project(idx, w_output, mixed, other, (2,), BF)
    half, width = far.shape[0] // 2, far.shape[1]
    far_up, far_down = x_send(far[:half], 1), x_send(far[half:], -1)
    ready = out_project(idx, w_output, mixed, other, (1, 3), BF, split=1)
    up_bottom, down_top = x_send(ready[:, :width], 1), x_send(ready[:, width:], -1)
    kept = out_project(idx, w_output, mixed, other, (0,), F32)
    kept, far_up, far_down = lax.optimization_barrier((kept, far_up, far_down))
    added = jnp.concatenate([far_up, far_down], axis=1)
    sums = out_project(idx, w_output, mixed, other, (1, 3), BF, split=0, added=added)
    up_top, down_bottom = x_send(sums[:, :width], 1), x_send(sums[:, width:], -1)
    vm = pl.BlockSpec(memory_space=pltpu.VMEM)
    return pl.pallas_call(
        sum_kernel,
        out_shape=jax.ShapeDtypeStruct((2 * half, width), BF),
        in_specs=[vm] * 5,
        out_specs=vm,
        compiler_params=pltpu.CompilerParams(vmem_limit_bytes=16 * MIB),
        name="sum",
    )(kept, up_top, up_bottom, down_top, down_bottom)


def solution(mesh):
    return jax.shard_map(
        body,
        mesh=mesh,
        in_specs=(
            P("dp", "tensor"),
            P(),
            P(None, "tensor"),
            P(None, "tensor"),
            P(None, "tensor"),
            P("tensor", None),
            P(),
        ),
        out_specs=P("dp", "tensor"),
        check_vma=False,
    )
```

```python
import functools

import jax
import jax.numpy as jnp
from jax import lax
from jax.experimental import pallas as pl
from jax.experimental.pallas import tpu as pltpu
from jax.sharding import PartitionSpec as P

HD = 128
EPSILON = 1e-05
THETA = 500000.0
NEGATIVE = -1e30
DIMS = (4, 4, 2)
BF = jnp.bfloat16
F32 = jnp.float32
MIB = 1 << 20
LOG2E = 1.4426950408889634


def dp_perm(dz, dy, dc):
    nz, ny, nc = DIMS
    pairs = []
    for z in range(nz):
        for y in range(ny):
            for c in range(nc):
                src = (z * ny + y) * nc + c
                dst = (((z + dz) % nz) * ny + (y + dy) % ny) * nc + (c + dc) % nc
                pairs.append((src, dst))
    return pairs


def dp_send(value, dz=0, dy=0, dc=0):
    return lax.ppermute(value, "dp", dp_perm(dz, dy, dc))


def x_send(value, shift):
    return lax.ppermute(value, "tensor", [(i, (i + shift) % 4) for i in range(4)])


def cost(flops, bytes_accessed, transcendentals=0):
    return pl.CostEstimate(
        flops=int(flops), bytes_accessed=int(bytes_accessed), transcendentals=int(transcendentals)
    )


def rope_tables(positions, doc_lengths):
    doc_starts = jnp.cumsum(doc_lengths) - doc_lengths
    doc_first = jnp.max(
        jnp.where(doc_starts[None, :] <= positions[:, None], doc_starts[None, :], 0), axis=1
    )
    half_size = HD // 2
    exponents = jnp.arange(half_size, dtype=F32) * (2.0 / HD)
    frequency = jnp.exp(-exponents * jnp.log(F32(THETA)))
    angles = (positions - doc_first).astype(F32)[:, None] * frequency[None, :]
    cosine, sine = jnp.cos(angles), jnp.sin(angles)
    return (
        jnp.concatenate([cosine, cosine], axis=1),
        jnp.concatenate([-sine, sine], axis=1),
    )


def rotate(value, cosine, sine):
    return value * cosine + pltpu.roll(value, HD // 2, 1) * sine


KV_ROWS = 128


def norm_rows(idx_ref, parts, gain_ref, xn_ref):
    rows, width = parts[0][0].shape
    x = idx_ref[3]
    step = 64

    def advance(i, carry):
        span = pl.ds(pl.multiple_of(i * step, step), step)
        square = jnp.zeros((step, HD), F32)
        for ref, _ in parts:
            for column in range(0, width, HD):
                f = ref[span, column : column + HD].astype(F32)
                square = square + f * f
        mean = jnp.sum(square, axis=1, keepdims=True) * (1.0 / (4 * width))
        inv = jnp.broadcast_to(lax.rsqrt(mean + EPSILON), (step, HD))
        for ref, shift in parts:
            begin = lax.rem(x + shift, 4) * width
            for column in range(0, width, HD):
                at = pl.ds(pl.multiple_of(begin + column, HD), HD)
                f = ref[span, column : column + HD].astype(F32)
                xn_ref[span, at] = (f * inv * gain_ref[:, at].astype(F32)).astype(BF)
        return carry

    lax.fori_loop(0, rows // step, advance, 0)


def kv_kernel(idx_ref, *refs):
    (t_ref, *halves), refs = refs[:7], refs[7:]
    gain_ref, wk_ref, wv_ref, cos_ref, sin_ref, xn_ref, mine_ref, send_ref = refs
    i = pl.program_id(0)
    steps = pl.num_programs(0)
    rows = xn_ref.shape[0]
    total = mine_ref.shape[0] // 2
    core = idx_ref[2]

    for n in range(2):

        @pl.when((i >= steps // 2) == (n == 1))
        def _(n=n):
            below, above, far = halves[n], halves[2 + n], halves[4 + n]
            parts = [(t_ref, 0), (below, 3), (above, 1), (far, 2)]
            norm_rows(idx_ref, parts, gain_ref, xn_ref)

    normed = xn_ref[...]
    keys = jnp.dot(normed, wk_ref[...], preferred_element_type=F32)
    cosine, sine = cos_ref[...], sin_ref[...]
    key0 = rotate(keys[:, :HD], cosine, sine).astype(BF)
    key1 = rotate(keys[:, HD:], cosine, sine).astype(BF)
    vals = jnp.dot(normed, wv_ref[...], preferred_element_type=F32).astype(BF)

    def put(first, second, offset):
        at = pl.ds(pl.multiple_of(offset + i * rows, rows), rows)

        @pl.when(core == 0)
        def _():
            mine_ref[at, :] = first
            send_ref[at, :] = second

        @pl.when(core != 0)
        def _():
            mine_ref[at, :] = second
            send_ref[at, :] = first

    put(key0, key1, 0)
    put(vals[:, :HD], vals[:, HD:], total)


def kv_project(idx, pieces, gain, wk, wv, cosine, sine):
    rows, part = pieces[0].shape
    width = wk.shape[0]
    steps = rows // KV_ROWS
    last = steps // 2 - 1
    vm = pl.BlockSpec(memory_space=pltpu.VMEM)
    top = pl.BlockSpec((KV_ROWS, part), lambda i, idx_ref: (jnp.minimum(i, last), 0))
    bottom = pl.BlockSpec((KV_ROWS, part), lambda i, idx_ref: (jnp.maximum(i - last - 1, 0), 0))
    block = lambda columns: pl.BlockSpec((KV_ROWS, columns), lambda i, idx_ref: (i, 0))
    full = pl.BlockSpec((2 * rows, HD), lambda i, idx_ref: (0, 0))
    return pl.pallas_call(
        kv_kernel,
        out_shape=(
            jax.ShapeDtypeStruct((rows, width), BF),
            jax.ShapeDtypeStruct((2 * rows, HD), BF),
            jax.ShapeDtypeStruct((2 * rows, HD), BF),
        ),
        grid_spec=pltpu.PrefetchScalarGridSpec(
            num_scalar_prefetch=1,
            grid=(steps,),
            in_specs=[block(part), top, bottom, top, bottom, top, bottom, vm, vm, vm, block(HD), block(HD)],
            out_specs=(block(width), full, full),
        ),
        compiler_params=pltpu.CompilerParams(
            vmem_limit_bytes=16 * MIB, dimension_semantics=("arbitrary",)
        ),
        cost_estimate=cost(2 * rows * width * 4 * HD, 12 * MIB),
        name="norm_keys_values",
    )(idx, *pieces, gain, wk, wv, cosine, sine)


def q_kernel(idx_ref, xn_ref, wq_ref, cos_ref, sin_ref, send_ref, mine_ref):
    j = pl.program_id(0)
    half = xn_ref.shape[0] // 2
    res = jnp.dot(xn_ref[...], wq_ref[...], preferred_element_type=F32)
    cosine, sine = cos_ref[...], sin_ref[...]
    heads = [rotate(res[:, e * HD : (e + 1) * HD], cosine, sine).astype(BF) for e in range(2)]

    def put(out_ref):
        for e in range(2):
            for t in range(2):
                begin = pl.multiple_of((t * 4 + lax.rem(j, 2) * 2 + e) * half, half)
                out_ref[pl.ds(begin, half), :] = heads[e][t * half : (t + 1) * half]

    @pl.when(j < 2)
    def _():
        put(send_ref)

    @pl.when(j >= 2)
    def _():
        put(mine_ref)


def q_project(idx, xn, wq, cosine, sine):
    rows, width = xn.shape

    def w_map(j, idx_ref):
        core = idx_ref[2]
        group = jnp.where(j < 2, 1 - core, core)
        return (0, group * 2 + lax.rem(j, 2))

    full = lambda shape: pl.BlockSpec(shape, lambda j, idx_ref: (0,) * len(shape))
    return pl.pallas_call(
        q_kernel,
        out_shape=tuple(jax.ShapeDtypeStruct((4 * rows, HD), BF) for _ in range(2)),
        grid_spec=pltpu.PrefetchScalarGridSpec(
            num_scalar_prefetch=1,
            grid=(4,),
            in_specs=[
                full((rows, width)),
                pl.BlockSpec((width, 2 * HD), w_map),
                full((rows, HD)),
                full((rows, HD)),
            ],
            out_specs=tuple(full((4 * rows, HD)) for _ in range(2)),
        ),
        compiler_params=pltpu.CompilerParams(
            vmem_limit_bytes=24 * MIB, dimension_semantics=("arbitrary",)
        ),
        cost_estimate=cost(2 * rows * width * 8 * HD, 14 * MIB),
        name="queries",
    )(idx, xn, wq, cosine, sine)


SCALE2 = HD ** (-0.5) * LOG2E
CHUNK = 256
ATTENTION_VMEM = 32 * MIB


def attention_kernel(pieces, n_kv, call, last_call, idx_ref, len_ref, *refs):
    kv_refs, refs = refs[:n_kv], refs[n_kv:]
    q_refs, refs = refs[:2], refs[2:]
    if call > 0:
        acc_in, top_in, refs = refs[0], refs[1], refs[2:]
    if call == last_call:
        o_ref, refs = refs[0], refs[1:]
    acc, top, key_ref, val_ref, q_ref, key_doc, q_doc, todo_ref, sem = refs
    z, y, core = idx_ref[0], idx_ref[1], idx_ref[2]
    rows = q_ref.shape[0]
    size = key_ref.shape[0] // 32
    group = rows // 2
    own = [(z * 4 + y) * 2 + lax.rem(core + g, 2) for g in range(2)]
    lower = jnp.minimum(own[0], own[1])
    copies = []

    def fetch(source, target):
        copy = pltpu.make_async_copy(source, target, sem.at[len(copies)])
        copy.start()
        copies.append(copy)

    for g in range(2):
        fetch(q_refs[g], q_ref.at[pl.ds(g * group, group), :])
    if call > 0:
        fetch(acc_in, acc)
        fetch(top_in, top)
    for array, row, dz, dy, dc, kind in pieces:
        block = (lax.rem(z + dz, 4) * 4 + lax.rem(y + dy, 4)) * 2 + lax.rem(core + dc, 2)
        begin = pl.multiple_of(block * size, size)
        fetch(kv_refs[array].at[pl.ds(row, size), :], (key_ref, val_ref)[kind].at[pl.ds(begin, size), :])
    if call == 0:
        top[...] = jnp.full_like(top, NEGATIVE)
        acc[...] = jnp.zeros_like(acc)

    lane = lax.broadcasted_iota(jnp.int32, (1, HD), 1)
    starts = jnp.zeros((1, HD), jnp.int32)
    ends = jnp.zeros((1, HD), jnp.int32)
    first = jnp.int32(0)
    begin = jnp.int32(0)
    for i in range(8):
        first = jnp.where(begin <= lower * size, begin, first)
        starts = jnp.where(lane == i, begin, starts)
        begin = begin + len_ref[i]
        ends = jnp.where(lane == i, begin, ends)
    lo = first // size

    def inside(begin, count):
        pos = begin + lax.broadcasted_iota(jnp.int32, (count, HD), 0)
        return (pos >= starts) & (pos < ends)

    def mark_keys(j, carry):
        span = pl.ds(pl.multiple_of(j * size, size), size)
        key_doc[span, :] = jnp.where(inside(j * size, size), 1.0, 0.0).astype(BF)
        return carry

    for g in range(2):
        for t in range(2):
            there = inside(own[g] * size + t * CHUNK, CHUNK) | (lane >= 8)
            mark = jnp.where(there, 0.0, NEGATIVE).astype(BF)
            for h in range(4):
                row = g * group + (t * 4 + h) * CHUNK
                q_doc[row : row + CHUNK, :] = mark
    ones = jnp.ones((size, HD), BF)

    def stage(j):
        away = jnp.where(
            lax.rem(j, 2) == core, lax.rem(j // 8 - z + 4, 4), lax.rem(lax.rem(j // 2, 4) - y + 4, 4)
        )
        return jnp.where(away == 0, 0, jnp.where(away == 2, 2, 1))

    def load(blocks):
        spans = [pl.ds(pl.multiple_of(j * size, size), size) for j in blocks]
        keys = [jnp.concatenate([key_ref[span, :], key_doc[span, :]], axis=1) for span in spans]
        vals = [jnp.concatenate([val_ref[span, :], ones], axis=1) for span in spans]
        if len(blocks) == 1:
            return keys[0], vals[0]
        return jnp.concatenate(keys, axis=0), jnp.concatenate(vals, axis=0)

    def scores(row, key):
        span = pl.ds(row, CHUNK)
        query = jnp.concatenate([q_ref[span, :], q_doc[span, :]], axis=1)
        return lax.dot_general(
            query, key, (((1,), (1,)), ((), ())), preferred_element_type=F32
        )

    def absorb(row, s, val):
        span = pl.ds(row, CHUNK)
        old = top[span, :]
        new = jnp.maximum(old, jnp.max(s, axis=1, keepdims=True))
        top[span, :] = new
        alpha = jnp.exp2((old - new) * SCALE2)
        p = jnp.exp2((s - new[:, :1]) * SCALE2).astype(BF)
        pv = jnp.dot(p, val, preferred_element_type=F32)
        acc[span, :HD] = acc[span, :HD] * alpha + pv[:, :HD]
        acc[span, HD:] = acc[span, HD:] * alpha + pv[:, HD:]

    def whole(blocks):
        key, val = load(blocks)
        following = scores(0, key)
        for row in range(0, rows, CHUNK):
            s = following
            if row + CHUNK < rows:
                following = scores(row + CHUNK, key)
            absorb(row, s, val)

    def within(g, blocks):
        key, val = load(blocks)
        before = size * (len(blocks) - 1)
        order = [(t, h) for t in range(2) for h in range(4)]

        def row(t, h):
            return pl.multiple_of(g * group + (t * 4 + h) * CHUNK, CHUNK)

        def part(n):
            return scores(row(*order[n]), key[: before + (order[n][0] + 1) * CHUNK])

        square = (CHUNK, CHUNK)
        causal = lax.broadcasted_iota(jnp.int32, square, 0) >= lax.broadcasted_iota(jnp.int32, square, 1)
        following = part(0)
        for n, (t, h) in enumerate(order):
            s = following
            if n + 1 < len(order):
                following = part(n + 1)
            edge = before + t * CHUNK
            corner = jnp.where(causal, s[:, edge:], NEGATIVE)
            s = corner if edge == 0 else jnp.concatenate([s[:, :edge], corner], axis=1)
            absorb(row(t, h), s, val[: edge + CHUNK])

    def collect(j, count):
        take = stage(j) == call

        @pl.when(take)
        def _():
            todo_ref[count] = j
            mark_keys(j, 0)

        return count + take.astype(jnp.int32)

    count = lax.fori_loop(lo, lower, collect, jnp.int32(0))
    if call == 0:
        lax.fori_loop(lower, lower + 2, mark_keys, 0)
    for copy in copies:
        copy.wait()

    def pair(k, carry):
        whole([todo_ref[2 * k], todo_ref[2 * k + 1]])
        return carry

    lax.fori_loop(0, count // 2, pair, 0)

    odd = lax.rem(count, 2) == 1
    if call == 0:
        low_group = (own[0] != lower).astype(jnp.int32)

        @pl.when(odd)
        def _():
            left = todo_ref[count - 1]
            within(low_group, [left, lower])
            within(1 - low_group, [left, lower, lower + 1])

        @pl.when(jnp.logical_not(odd))
        def _():
            within(low_group, [lower])
            within(1 - low_group, [lower, lower + 1])

    else:

        @pl.when(odd)
        def _():
            whole([todo_ref[count - 1]])

    if call == last_call:
        o_ref[...] = (acc[:, :HD] / acc[:, HD:]).astype(BF)


def attention(idx, doc_lengths, kv, queries, state, call, last_call, total_tokens):
    rows = 2 * queries[0].shape[0]
    smem = pl.BlockSpec(memory_space=pltpu.SMEM)
    hbm = pl.BlockSpec(memory_space=pl.ANY)
    vm = pl.BlockSpec(memory_space=pltpu.VMEM)
    arrays, pieces = kv
    last = call == last_call
    wide, narrow = (rows, 2 * HD), (rows, HD)
    states = (jax.ShapeDtypeStruct(wide, F32), jax.ShapeDtypeStruct(narrow, F32))
    return pl.pallas_call(
        functools.partial(attention_kernel, pieces, len(arrays), call, last_call),
        out_shape=jax.ShapeDtypeStruct((rows, HD), BF) if last else states,
        in_specs=[smem, smem] + [hbm] * (len(arrays) + 2 + len(state)),
        out_specs=vm if last else (vm, vm),
        scratch_shapes=[
            *([pltpu.VMEM(wide, F32), pltpu.VMEM(narrow, F32)] if last else []),
            pltpu.VMEM((total_tokens, HD), BF),
            pltpu.VMEM((total_tokens, HD), BF),
            pltpu.VMEM((rows, HD), BF),
            pltpu.VMEM((total_tokens, HD), BF),
            pltpu.VMEM((rows, HD), BF),
            pltpu.SMEM((32,), jnp.int32),
            pltpu.SemaphoreType.DMA((len(pieces) + 4,)),
        ],
        compiler_params=pltpu.CompilerParams(vmem_limit_bytes=ATTENTION_VMEM),
        cost_estimate=cost(8e6 * 512, 10 * MIB, 8e6),
        name="attention",
    )(idx, doc_lengths, *arrays, *queries, *state)


def out_kernel(dests, split, add, idx_ref, w_ref, mine_ref, other_ref, *refs):
    added = refs[0] if add else None
    out_ref, scr = refs[-2:]
    core = idx_ref[2]
    j = pl.program_id(0)
    rows = scr.shape[0]
    half = rows // 2

    @pl.when(j == 0)
    def _():
        for g, ref in enumerate((mine_ref, other_ref)):
            group = lax.rem(core + g, 2) * (4 * HD)
            for h in range(4):
                column = pl.ds(pl.multiple_of(group + h * HD, HD), HD)
                for t in range(2):
                    at = (t * 4 + h) * half
                    scr[t * half : (t + 1) * half, column] = ref[at : at + half, :]

    if split is None:
        left = scr[...]
    else:
        number = j // (pl.num_programs(0) // 2)
        begin = (number + split - 2 * number * split) * half
        left = scr[pl.ds(pl.multiple_of(begin, half), half), :]
    res = jnp.dot(left, w_ref[...], preferred_element_type=F32)
    if add:
        res = res + added[...].astype(F32)
    out_ref[...] = res.astype(out_ref.dtype)


def out_project(idx, w, mine, other, dests, dtype, split=None, added=None):
    rows = mine.shape[0] // 4
    out_rows = rows if split is None else rows // 2
    feat, model = w.shape
    width = model // 4
    block = 512
    per = width // block

    def w_map(j, idx_ref):
        shift = jnp.int32(dests[0])
        for n, s in enumerate(dests):
            shift = jnp.where(j >= n * per, s, shift)
        return (0, lax.rem(idx_ref[3] + shift, 4) * per + lax.rem(j, per))

    columns = pl.BlockSpec((out_rows, block), lambda j, idx_ref: (0, j))
    return pl.pallas_call(
        functools.partial(out_kernel, dests, split, added is not None),
        out_shape=jax.ShapeDtypeStruct((out_rows, width * len(dests)), dtype),
        grid_spec=pltpu.PrefetchScalarGridSpec(
            num_scalar_prefetch=1,
            grid=(per * len(dests),),
            in_specs=[pl.BlockSpec((feat, block), w_map)]
            + [pl.BlockSpec((4 * rows, HD), lambda j, idx_ref: (0, 0))] * 2
            + ([columns] if added is not None else []),
            out_specs=columns,
            scratch_shapes=[pltpu.VMEM((rows, feat), BF)],
        ),
        compiler_params=pltpu.CompilerParams(
            vmem_limit_bytes=20 * MIB, dimension_semantics=("arbitrary",)
        ),
        cost_estimate=cost(
            2 * out_rows * feat * width * len(dests), (2 * feat + 4 * out_rows) * width * len(dests)
        ),
        name="output_projection",
    )(idx, w, mine, other, *(() if added is None else (added,)))


def sum_kernel(kept_ref, up_top, up_bottom, down_top, down_bottom, out_ref):
    half = up_top.shape[0]
    for n, (up, down) in enumerate(((up_top, down_top), (up_bottom, down_bottom))):
        span = slice(n * half, (n + 1) * half)
        out_ref[span, :] = (
            kept_ref[span, :] + up[...].astype(F32) + down[...].astype(F32)
        ).astype(BF)


def exchange_near(mine, other, meanwhile):
    a_up, a_down, a_far = move_y(mine, 1), move_y(mine, -1), move_y(mine, 2)
    b_up, b_far = move_z(other, 1), move_z(other, 2)
    (a_up, a_down, a_far, b_up, b_far), meanwhile = lax.optimization_barrier(
        ((a_up, a_down, a_far, b_up, b_far), meanwhile)
    )
    a_line = jnp.concatenate([mine, a_up, a_down, a_far], axis=0)
    b_line = jnp.concatenate([other, b_up, b_far], axis=0)
    return a_line, b_line, meanwhile


def move_y(value, shift):
    return dp_send(value, dy=shift)


def move_z(value, shift):
    return dp_send(value, dz=shift)


def exchange(a_line, b_line, rows, attend):
    block = 2 * rows
    stages = [([], []) for _ in range(3)]

    def keep(n, array, places, dc):
        arrays, pieces = stages[n]
        for i, (dz, dy) in enumerate(places):
            for kind in range(2):
                pieces.append((len(arrays), i * block + kind * rows, dz % 4, dy % 4, dc, kind))
        arrays.append(array)

    from_left, from_right = move_y(b_line, 1), move_y(b_line, -1)
    from_below, from_above = move_z(a_line, 1), move_z(a_line[2 * block :], -1)
    keep(0, a_line, [(0, 0), (0, -1), (0, 1), (0, 2)], 0)
    keep(0, b_line, [(0, 0), (-1, 0), (-2, 0)], 1)
    state = attend(stages[0], (), 0)
    state, from_left, from_right, from_below, from_above = lax.optimization_barrier(
        (state, from_left, from_right, from_below, from_above)
    )
    left_far = move_y(from_left[: block + rows], 1)
    right_far = move_y(from_right[block + rows :], -1)
    far_below, far_above = move_z(from_below[: 2 * block], 1), move_z(from_above, -1)

    keep(1, from_below, [(-1, 0), (-1, -1), (-1, 1), (-1, 2)], 0)
    keep(1, from_left, [(0, -1), (-1, -1), (-2, -1)], 1)
    keep(1, from_right, [(0, 1), (-1, 1), (-2, 1)], 1)
    keep(2, far_below, [(2, 0), (2, -1)], 0)
    keep(2, far_above, [(2, 1), (2, 2)], 0)
    arrays, pieces = stages[2]
    for place, (array, row, kind) in (
        (0, (left_far, 0, 0)),
        (0, (left_far, rows, 1)),
        (-1, (left_far, block, 0)),
        (-1, (right_far, 0, 1)),
        (-2, (right_far, rows, 0)),
        (-2, (right_far, block, 1)),
    ):
        index = len(arrays) + (array is right_far)
        pieces.append((index, row, place % 4, 2, 1, kind))
    arrays.extend([left_far, right_far])
    state = attend(stages[1], state, 1)
    return attend(stages[2], state, 2)


def gather_x(tokens):
    half = tokens.shape[0] // 2
    top = tokens[:half]
    tokens, top = lax.optimization_barrier((tokens, top))
    bottom = tokens[half:]
    below_top, above_bottom = x_send(top, 1), x_send(bottom, -1)
    below_top, above_bottom, top, bottom = lax.optimization_barrier(
        (below_top, above_bottom, top, bottom)
    )
    far_top, far_bottom = x_send(below_top, 1), x_send(above_bottom, -1)
    below_bottom, above_top = x_send(bottom, 1), x_send(top, -1)
    return below_top, below_bottom, above_top, above_bottom, far_top, far_bottom


def body(tokens, norm_gain, w_query, key_weight, value_weight, w_output, doc_lengths):
    rows = tokens.shape[0]
    dp = lax.axis_index("dp").astype(jnp.int32)
    x = lax.axis_index("tensor").astype(jnp.int32)
    idx = jnp.stack([dp // 8, (dp // 2) % 4, dp % 2, x])
    positions = dp * rows + jnp.arange(rows, dtype=jnp.int32)
    cosine, sine = rope_tables(positions, doc_lengths)

    gain = norm_gain[None, :]
    pieces = (tokens, *gather_x(tokens))
    xn, mine, send = kv_project(idx, pieces, gain, key_weight, value_weight, cosine, sine)
    other = dp_send(send, dc=1)
    xn, other = lax.optimization_barrier((xn, other))
    queries = q_project(idx, xn, w_query, cosine, sine)
    a_line, b_line, (q_send, q_mine) = exchange_near(mine, other, queries)
    a_line, b_line = lax.optimization_barrier((a_line, b_line))
    q_other = dp_send(q_send, dc=1)
    queries = (q_mine, q_other)
    total = rows * 32

    def attend(kv, state, call):
        return attention(idx, doc_lengths, kv, queries, state, call, 2, total)

    mixed = exchange(a_line, b_line, rows, attend)
    group = mixed.shape[0] // 2
    return reduce_out(idx, w_output, mixed[:group], dp_send(mixed[group:], dc=1))


def reduce_out(idx, w_output, mixed, other):
    far = out_project(idx, w_output, mixed, other, (2,), BF)
    half, width = far.shape[0] // 2, far.shape[1]
    far_up, far_down = x_send(far[:half], 1), x_send(far[half:], -1)
    ready = out_project(idx, w_output, mixed, other, (1, 3), BF, split=1)
    up_bottom, down_top = x_send(ready[:, :width], 1), x_send(ready[:, width:], -1)
    kept = out_project(idx, w_output, mixed, other, (0,), F32)
    kept, far_up, far_down = lax.optimization_barrier((kept, far_up, far_down))
    added = jnp.concatenate([far_up, far_down], axis=1)
    sums = out_project(idx, w_output, mixed, other, (1, 3), BF, split=0, added=added)
    up_top, down_bottom = x_send(sums[:, :width], 1), x_send(sums[:, width:], -1)
    vm = pl.BlockSpec(memory_space=pltpu.VMEM)
    return pl.pallas_call(
        sum_kernel,
        out_shape=jax.ShapeDtypeStruct((2 * half, width), BF),
        in_specs=[vm] * 5,
        out_specs=vm,
        compiler_params=pltpu.CompilerParams(vmem_limit_bytes=16 * MIB),
        name="sum",
    )(kept, up_top, up_bottom, down_top, down_bottom)


def solution(mesh):
    return jax.shard_map(
        body,
        mesh=mesh,
        in_specs=(
            P("dp", "tensor"),
            P(),
            P(None, "tensor"),
            P(None, "tensor"),
            P(None, "tensor"),
            P("tensor", None),
            P(),
        ),
        out_specs=P("dp", "tensor"),
        check_vma=False,
    )
```
